32 devices in a mesh: dp: 32 (over z, y, x, core).
Axes of the slice: x: 2, y: 2, z: 4, core: 2. Of those that a mesh axis runs over, the one named last changes fastest.
Arguments:
- frames: bfloat16 [32, 1024, 768], P('dp'), may hold values from -6 to 6
- cotangent: bfloat16 [32, 1024, 768], P('dp'), may hold values from -6 to 6
- lengths: int32 [32], P('dp'), may hold values from 128 to 1024, as said below
- w_qkv: float32 [768, 2304], P('dp'), may hold values from -4 to 4
- w_attn: float32 [768, 768], P('dp'), may hold values from -4 to 4
- w_in: float32 [768, 3072], P('dp'), may hold values from -4 to 4
- w_out: float32 [3072, 768], P('dp'), may hold values from -4 to 4
- vectors: float32 [9216], P('dp'), may hold values from -4 to 4
- moment_qkv: float32 [768, 2304], P('dp'), may hold values from -43.44464 to 43.44464
- moment_attn: float32 [768, 768], P('dp'), may hold values from -43.44464 to 43.44464
- moment_in: float32 [768, 3072], P('dp'), may hold values from -43.44464 to 43.44464
- moment_out: float32 [3072, 768], P('dp'), may hold values from -43.44464 to 43.44464
- moment_vec: float32 [9216], P('dp'), may hold values from -43.44464 to 43.44464
- square_qkv: float32 [768, 2304], P('dp'), may hold values from 4.9152 to 19.6608
- square_attn: float32 [768, 768], P('dp'), may hold values from 4.9152 to 19.6608
- square_in: float32 [768, 3072], P('dp'), may hold values from 4.9152 to 19.6608
- square_out: float32 [3072, 768], P('dp'), may hold values from 4.9152 to 19.6608
- square_vec: float32 [9216], P('dp'), may hold values from 4.9152 to 19.6608
Outputs:
- mixed: bfloat16 [32, 1024, 768], P('dp')
- input_grad: float32 [32, 1024, 768], P('dp')
- new_qkv: float32 [768, 2304], P('dp')
- new_attn: float32 [768, 768], P('dp')
- new_in: float32 [768, 3072], P('dp')
- new_out: float32 [3072, 768], P('dp')
- new_vectors: float32 [9216], P('dp')
- next_moment_qkv: float32 [768, 2304], P('dp')
- next_moment_attn: float32 [768, 768], P('dp')
- next_moment_in: float32 [768, 3072], P('dp')
- next_moment_out: float32 [3072, 768], P('dp')
- next_moment_vec: float32 [9216], P('dp')
- next_square_qkv: float32 [768, 2304], P('dp')
- next_square_attn: float32 [768, 768], P('dp')
- next_square_in: float32 [768, 3072], P('dp')
- next_square_out: float32 [3072, 768], P('dp')
- next_square_vec: float32 [9216], P('dp')
- norms: float32 [8], replicated
The draws below stay inside these ranges and needn't reach their ends.
Inputs may be any that keep to these rules, and one draw needn't show every extreme that they name: `lengths`: some clip has all 1024 frames.
All inputs are finite; a program needn't handle non-finite values.
Results may differ from the reference program's by a relative error of at most 0.014.
The reference program's roundings to bfloat16 on the way count: a program that leaves them out, or rounds other values in their place, can miss the bound.
Values may be sent and summed in bfloat16 or wider, within the bound.
No kernel may reach another device: no remote copies, remote signals or barrier semaphores. Data moves between devices by JAX's collectives and lax.ppermute only.
A program may use at most 192 MiB of HBM per device.

```python
import math
import jax
import jax.numpy as jnp
from jax import lax

D = 768
FF = 3072
HEADS = 12
HEAD_DIM = 64
SEQ = 1024
STEP = 10
CLIPS = 32
NVEC = 9216


def ramp_rows(noise, fan, top):
    rows = noise.shape[0]
    place = jnp.arange(rows, dtype=jnp.float32) / max(rows - 1, 1)
    return noise * jnp.sqrt(1.0 + (top - 1.0) * place)[:, None] * fan ** (-0.5)


def draw_w_qkv(key, part):
    key = jax.random.fold_in(key, 11)
    return ramp_rows(jnp.clip(jax.random.normal(key, (D, 3 * D), jnp.float32), -4.0, 4.0), D, 3.0)


def draw_w_attn(key, part):
    key = jax.random.fold_in(key, 12)
    return ramp_rows(jnp.clip(jax.random.normal(key, (D, D), jnp.float32), -4.0, 4.0), D // 16, 3.0)


def draw_w_in(key, part):
    key = jax.random.fold_in(key, 13)
    return ramp_rows(jnp.clip(jax.random.normal(key, (D, FF), jnp.float32), -4.0, 4.0), D, 3.0)


def draw_w_out(key, part):
    key = jax.random.fold_in(key, 14)
    return ramp_rows(jnp.clip(jax.random.normal(key, (FF, D), jnp.float32), -4.0, 4.0), FF, 3.0)


def draw_frames(key, part):
    key = jax.random.fold_in(key, 15)
    place = jnp.arange(D, dtype=jnp.float32) / (D - 1)
    noise = jnp.clip(jax.random.normal(key, (CLIPS, SEQ, D), jnp.float32), -4.0, 4.0)
    return (noise * (0.7 * jnp.sqrt(1.0 + 2.0 * place))).astype(jnp.bfloat16)


def draw_vectors(key, part):
    key = jax.random.fold_in(key, 16)
    first_key, second_key = jax.random.split(key)
    total = 8 * D + FF
    place = jnp.arange(total)
    first_gain = (place >= 3 * D) & (place < 4 * D)
    second_gain = (place >= 6 * D + FF) & (place < 7 * D + FF)
    within = jnp.where(place < 4 * D, place - 3 * D, place - (6 * D + FF)).astype(jnp.float32) / (D - 1)
    noise = jnp.clip(jax.random.normal(first_key, (total,), jnp.float32), -4.0, 4.0)
    jitter = jnp.clip(jax.random.normal(second_key, (total,), jnp.float32), -4.0, 4.0)
    gains = (0.6 + within) * (1.0 + 0.1 * jitter)
    return jnp.where(first_gain | second_gain, gains, 0.3 * noise)


def draw_lengths(key, part):
    key = jax.random.fold_in(key, 17)
    first_key, second_key = jax.random.split(key)
    place = jnp.arange(CLIPS, dtype=jnp.int32)
    lowest = SEQ // 8 + SEQ // 2 * place // max(CLIPS - 1, 1)
    extra = jax.random.randint(first_key, (CLIPS,), 0, SEQ // 4 + 1, dtype=jnp.int32)
    counts = jnp.minimum(lowest + extra, SEQ)
    chosen = jax.random.randint(second_key, (), CLIPS // 2, CLIPS, dtype=jnp.int32)
    return jnp.where(place == chosen, SEQ, counts).astype(jnp.int32)


def shard_levels(stream_key, dims, cuts, low, top_value):
    def one(dim, parts):
        steps = jax.random.uniform(jax.random.fold_in(jax.random.fold_in(stream_key, 6), dim), (parts,), jnp.float32, low / len(cuts), top_value / len(cuts))
        return jnp.repeat(jnp.exp(steps), dims[dim] // parts).reshape((-1,) + (1,) * (len(dims) - dim - 1))

    gain = one(*cuts[0])
    for cut in cuts[1:]:
        gain = gain * one(*cut)
    return gain


def scatter_about(stream_key, shape, scale, reach, cuts=(), kind=jnp.bfloat16):
    level = shard_levels(stream_key, shape, cuts, -0.22, 0.18) if cuts else 1.0
    values = jax.random.normal(stream_key, shape, jnp.float32) * scale * level
    return jnp.minimum(jnp.maximum(values, -reach), reach).astype(kind)


def setup_inputs(seed: int = 0) -> dict:
    key_of = jax.random.split(jax.random.key(seed), 19)
    frames = draw_frames(jax.random.fold_in(key_of[18], 71), 0)
    cotangent = scatter_about(key_of[1], (CLIPS, SEQ, D), 1.0, 6.0, ((0, 32),))
    lengths = draw_lengths(jax.random.fold_in(key_of[18], 71), 0)
    w_qkv = draw_w_qkv(jax.random.fold_in(key_of[18], 71), 0)
    w_attn = draw_w_attn(jax.random.fold_in(key_of[18], 71), 0)
    w_in = draw_w_in(jax.random.fold_in(key_of[18], 71), 0)
    w_out = draw_w_out(jax.random.fold_in(key_of[18], 71), 0)
    vectors = draw_vectors(jax.random.fold_in(key_of[18], 71), 0)
    moment_qkv = scatter_about(key_of[8], (D, 3 * D), (0.04 * (SEQ * CLIPS) ** 0.5), 43.44464, ((0, 32),), jnp.float32)
    moment_attn = scatter_about(key_of[9], (D, D), (0.04 * (SEQ * CLIPS) ** 0.5), 43.44464, ((0, 32),), jnp.float32)
    moment_in = scatter_about(key_of[10], (D, FF), (0.04 * (SEQ * CLIPS) ** 0.5), 43.44464, ((0, 32),), jnp.float32)
    moment_out = scatter_about(key_of[11], (FF, D), (0.04 * (SEQ * CLIPS) ** 0.5), 43.44464, ((0, 32),), jnp.float32)
    moment_vec = scatter_about(key_of[12], (NVEC,), (0.04 * (SEQ * CLIPS) ** 0.5), 43.44464, ((0, 32),), jnp.float32)
    square_qkv = jnp.clip(jnp.exp(math.log(19.6608) - 1.3862944 * jax.random.uniform(key_of[13], (D, 3 * D), jnp.float32) ** shard_levels(key_of[13], (D, 3 * D), ((0, 32),), -0.2, 0.2)), 4.9152, 19.6608)
    square_attn = jnp.clip(jnp.exp(math.log(19.6608) - 1.3862944 * jax.random.uniform(key_of[14], (D, D), jnp.float32) ** shard_levels(key_of[14], (D, D), ((0, 32),), -0.2, 0.2)), 4.9152, 19.6608)
    square_in = jnp.clip(jnp.exp(math.log(19.6608) - 1.3862944 * jax.random.uniform(key_of[15], (D, FF), jnp.float32) ** shard_levels(key_of[15], (D, FF), ((0, 32),), -0.2, 0.2)), 4.9152, 19.6608)
    square_out = jnp.clip(jnp.exp(math.log(19.6608) - 1.3862944 * jax.random.uniform(key_of[16], (FF, D), jnp.float32) ** shard_levels(key_of[16], (FF, D), ((0, 32),), -0.2, 0.2)), 4.9152, 19.6608)
    square_vec = jnp.clip(jnp.exp(math.log(19.6608) - 1.3862944 * jax.random.uniform(key_of[17], (NVEC,), jnp.float32) ** shard_levels(key_of[17], (NVEC,), ((0, 32),), -0.2, 0.2)), 4.9152, 19.6608)
    return dict(frames=frames, cotangent=cotangent, lengths=lengths, w_qkv=w_qkv, w_attn=w_attn, w_in=w_in, w_out=w_out, vectors=vectors, moment_qkv=moment_qkv, moment_attn=moment_attn, moment_in=moment_in, moment_out=moment_out, moment_vec=moment_vec, square_qkv=square_qkv, square_attn=square_attn, square_in=square_in, square_out=square_out, square_vec=square_vec)


@jax.custom_vjp
def low(v):
    return lax.optimization_barrier(v.astype(jnp.bfloat16)).astype(jnp.float32)

@jax.custom_vjp
def low_back(v):
    return v

def low_keep(v):
    return (low(v), None)

def low_pass(kept, grad):
    return (grad,)

def back_keep(v):
    return (v, None)

def back_low(kept, grad):
    return (low(grad),)
low.defvjp(low_keep, low_pass)
low_back.defvjp(back_keep, back_low)
HIGH = lax.Precision.HIGHEST

def layer_norm(resid):
    center = resid - lax.optimization_barrier(jnp.mean(resid, axis=-1, keepdims=True))
    spread = lax.optimization_barrier(jnp.mean(center * center, axis=-1, keepdims=True))
    return center * lax.rsqrt(spread + 1e-05)

def split_vector(vec):
    widths = [D, D, D, D, D, FF, D, D, D]
    pieces = []
    offset = 0
    for width in widths:
        pieces.append(vec[offset:offset + width])
        offset = offset + width
    return pieces

def clip_forward(frame, length, w_qkv, w_attn, w_in, w_out, vec):
    bias_q, bias_v, bias_o, gain1, shift1, bias1, bias2, gain2, shift2 = split_vector(vec)
    keep = (jnp.arange(SEQ) < length).astype(jnp.float32)
    packed = jnp.dot(frame, w_qkv, precision=HIGH) + jnp.concatenate([bias_q, jnp.zeros((D,), jnp.float32), bias_v])
    packed = low(low_back(packed))
    queries = packed[:, :D].reshape(SEQ, HEADS, HEAD_DIM)
    keys_all = packed[:, D:2 * D].reshape(SEQ, HEADS, HEAD_DIM)
    values_all = packed[:, 2 * D:].reshape(SEQ, HEADS, HEAD_DIM)
    scores = jnp.einsum('qhd,khd->hqk', queries, keys_all, precision=HIGH) * 0.125
    scores = jnp.where(keep[None, None, :] > 0, scores, -1000000000.0)
    scores = low_back(scores)
    peak = lax.optimization_barrier(jnp.max(scores, axis=-1, keepdims=True))
    expo = jnp.exp(scores - peak)
    probs = low(expo / lax.optimization_barrier(jnp.sum(expo, axis=-1, keepdims=True)))
    context = jnp.einsum('hqk,khd->qhd', probs, values_all, precision=HIGH).reshape(SEQ, D)
    context = low(low_back(context))
    attended = low_back(jnp.dot(context, w_attn, precision=HIGH) + bias_o)
    first = layer_norm(frame + attended) * gain1 + shift1
    hidden = low_back(jnp.dot(low(first), w_in, precision=HIGH) + bias1)
    active = low(jax.nn.gelu(hidden, approximate=False))
    branch = low_back(jnp.dot(active, w_out, precision=HIGH) + bias2)
    return (layer_norm(first + branch) * gain2 + shift2) * keep[:, None]

def adapt(weight, grad, moment, square, decay):
    new_moment = 0.9 * moment + 0.1 * grad
    new_square = 0.999 * square + 0.001 * grad * grad
    update = new_moment / (1.0 - 0.9 ** STEP) / (jnp.sqrt(new_square / (1.0 - 0.999 ** STEP)) + 1e-06)
    update = update + decay * weight
    return (new_moment, new_square, update)

def reference(frames, cotangent, lengths, w_qkv, w_attn, w_in, w_out, vectors, moment_qkv, moment_attn, moment_in, moment_out, moment_vec, square_qkv, square_attn, square_in, square_out, square_vec):

    def forward(master_qkv, master_attn, master_in, master_out, master_vec, inputs):
        low_qkv = low(master_qkv)
        low_attn = low(master_attn)
        low_in = low(master_in)
        low_out = low(master_out)
        low_vec = low(master_vec)
        checked = jax.checkpoint(clip_forward)

        def one_clip(carry, item):
            return (carry, checked(item[0], item[1], low_qkv, low_attn, low_in, low_out, low_vec))
        unused, outputs = lax.scan(one_clip, jnp.zeros((), jnp.float32), (inputs, lengths))
        return outputs
    outputs, pull = jax.vjp(forward, w_qkv, w_attn, w_in, w_out, vectors, frames.astype(jnp.float32))
    grad_qkv, grad_attn, grad_in, grad_out, grad_vec, grad_frames = pull(cotangent.astype(jnp.float32))
    matrices = [w_qkv, w_attn, w_in, w_out]
    grads = [grad_qkv, grad_attn, grad_in, grad_out]
    moments = [moment_qkv, moment_attn, moment_in, moment_out]
    squares = [square_qkv, square_attn, square_in, square_out]
    new_moments = []
    new_squares = []
    updates = []
    for weight, grad, moment, square in zip(matrices, grads, moments, squares):
        new_moment, new_square, update = adapt(weight, grad, moment, square, 0.01)
        new_moments.append(new_moment)
        new_squares.append(new_square)
        updates.append(update)
    weight_norms = [jnp.sqrt(jnp.sum(weight * weight)) for weight in matrices]
    update_norms = [jnp.sqrt(jnp.sum(update * update)) for update in updates]
    new_weights = [weight - 0.25 * (wn / un) * update for weight, update, wn, un in zip(matrices, updates, weight_norms, update_norms)]
    vec_moment, vec_square, vec_update = adapt(vectors, grad_vec, moment_vec, square_vec, 0.0)
    new_vec = vectors - 0.4 * vec_update
    norms = jnp.stack(weight_norms + update_norms)
    return (outputs.astype(jnp.bfloat16), grad_frames, new_weights[0], new_weights[1], new_weights[2], new_weights[3], new_vec, new_moments[0], new_moments[1], new_moments[2], new_moments[3], vec_moment, new_squares[0], new_squares[1], new_squares[2], new_squares[3], vec_square, norms)
```

```python
from functools import partial

import jax
import jax.numpy as jnp
from jax import lax
from jax.sharding import PartitionSpec as P

D = 768
FF = 3072
HEADS = 12
HEAD_DIM = 64
STEP = 10


def layer_norm(resid):
    center = resid - jnp.mean(resid, axis=-1, keepdims=True)
    spread = jnp.mean(center * center, axis=-1, keepdims=True)
    return center * lax.rsqrt(spread + 1e-05)


def normalize(resid, gain, shift):
    return layer_norm(resid) * gain + shift


def split_vector(vec):
    widths = [D, D, D, D, D, FF, D, D, D]
    pieces = []
    offset = 0
    for width in widths:
        pieces.append(vec[offset : offset + width])
        offset = offset + width
    return pieces


def adapt(weight, grad, moment, square, decay):
    new_moment = 0.9 * moment + 0.1 * grad
    new_square = 0.999 * square + 0.001 * grad * grad
    update = new_moment / (1.0 - 0.9**STEP) / (jnp.sqrt(new_square / (1.0 - 0.999**STEP)) + 1e-06)
    return (new_moment, new_square, update + decay * weight)


def swap(value, bit, n):
    return lax.ppermute(value, "dp", [(i, i ^ (1 << bit)) for i in range(n)])


def sum_all(value, n):
    for bit in range(n.bit_length() - 1):
        value = value + swap(value, bit, n)
    return value


def body(
    n,
    frames,
    cotangent,
    lengths,
    w_qkv,
    w_attn,
    w_in,
    w_out,
    vectors,
    moment_qkv,
    moment_attn,
    moment_in,
    moment_out,
    moment_vec,
    square_qkv,
    square_attn,
    square_in,
    square_out,
    square_vec,
):
    def gather(shard):
        return lax.all_gather(shard.astype(jnp.bfloat16), "dp", axis=0, tiled=True)

    def blocks(matrix, rows):
        return matrix.reshape(rows, -1, D).transpose(1, 0, 2).reshape(-1, D)

    rows_d, rows_f = w_qkv.shape[0], w_out.shape[0]
    width = vectors.shape[0]
    vec_rows = jnp.zeros((8, D), jnp.float32).at[0, :width].set(vectors)
    pack = jnp.concatenate(
        [blocks(w_qkv, rows_d), w_attn, blocks(w_in, rows_d), w_out, vec_rows], axis=0
    )
    whole = gather(pack[None])
    full_vec = whole[:, 8 * rows_d + rows_f, :width].reshape(-1)

    def columns(first, count):
        parts = [
            whole[:, first + i * rows_d : first + (i + 1) * rows_d].reshape(D, D)
            for i in range(count)
        ]
        return parts[0] if count == 1 else jnp.concatenate(parts, axis=1)

    full_qkv = columns(0, 3)
    full_attn = columns(3 * rows_d, 1)
    full_in = columns(4 * rows_d, FF // D)
    full_out = whole[:, 8 * rows_d : 8 * rows_d + rows_f].reshape(FF, D)
    bias_q, bias_v, bias_o, gain1, shift1, bias1, bias2, gain2, shift2 = split_vector(
        full_vec.astype(jnp.float32)
    )
    bias_qkv = jnp.concatenate([bias_q, jnp.zeros((D,), jnp.float32), bias_v])
    seq = frames.shape[1]
    block = min(512, seq)
    count = seq // block
    grad_out = jnp.zeros((FF, D), jnp.float32)
    grad_vec = jnp.zeros((8 * D + FF,), jnp.float32)
    clip_in = frames[0]
    keep = jnp.arange(seq) < lengths[0]
    keepf = keep.astype(jnp.float32)
    packed = (jnp.dot(clip_in, full_qkv, preferred_element_type=jnp.float32) + bias_qkv).astype(
        jnp.bfloat16
    )
    queries = packed[:, :D].reshape(seq, HEADS, HEAD_DIM)
    keys_all = packed[:, D : 2 * D].reshape(seq, HEADS, HEAD_DIM)
    values_all = packed[:, 2 * D :].reshape(seq, HEADS, HEAD_DIM)
    query_blocks = queries.reshape(count, block, HEADS, HEAD_DIM)

    def masked_scores(query_block):
        scores = (
            jnp.einsum("qhd,khd->hqk", query_block, keys_all, preferred_element_type=jnp.float32)
            * 0.125
        )
        return jnp.where(keep[None, None, :], scores, -1000000000.0)

    def attend(query_block):
        scores = masked_scores(query_block)
        peak = jnp.max(scores, axis=-1, keepdims=True)
        expo = jnp.exp(scores - peak)
        total = jnp.sum(expo, axis=-1, keepdims=True)
        probb = (expo / total).astype(jnp.bfloat16)
        context = jnp.einsum("hqk,khd->qhd", probb, values_all, preferred_element_type=jnp.float32)
        return (context, (peak + jnp.log(total))[..., 0])

    context, logsum = lax.map(attend, query_blocks)
    context_b = context.reshape(seq, D).astype(jnp.bfloat16)
    attended = jnp.dot(context_b, full_attn, preferred_element_type=jnp.float32) + bias_o
    first, first_pull = jax.vjp(normalize, clip_in.astype(jnp.float32) + attended, gain1, shift1)
    first_b = first.astype(jnp.bfloat16)
    hidden = jnp.dot(first_b, full_in, preferred_element_type=jnp.float32) + bias1
    active, gelu_pull = jax.vjp(partial(jax.nn.gelu, approximate=False), hidden)
    active_b = active.astype(jnp.bfloat16)
    branch = jnp.dot(active_b, full_out, preferred_element_type=jnp.float32) + bias2
    result, second_pull = jax.vjp(normalize, first + branch, gain2, shift2)
    mixed_rows = [(result * keepf[:, None]).astype(jnp.bfloat16)]
    dresult = cotangent[0].astype(jnp.float32) * keepf[:, None]
    dres2, dgain2, dshift2 = second_pull(dresult)
    dbranch = dres2.astype(jnp.bfloat16)
    grad_out = grad_out + jnp.einsum(
        "tf,td->fd", active_b, dbranch, preferred_element_type=jnp.float32
    )
    dbias2 = jnp.sum(dbranch.astype(jnp.float32), axis=0)
    dactive = jnp.einsum("td,fd->tf", dbranch, full_out, preferred_element_type=jnp.float32)
    dhidden = gelu_pull(dactive)[0].astype(jnp.bfloat16)
    grad_in = jnp.einsum("td,tf->df", first_b, dhidden, preferred_element_type=jnp.float32)
    dbias1 = jnp.sum(dhidden.astype(jnp.float32), axis=0)
    dfirst = dres2 + jnp.einsum("tf,df->td", dhidden, full_in, preferred_element_type=jnp.float32)
    dres1, dgain1, dshift1 = first_pull(dfirst)
    dattend = dres1.astype(jnp.bfloat16)
    grad_attn = jnp.einsum("tj,td->jd", context_b, dattend, preferred_element_type=jnp.float32)
    dbias_o = jnp.sum(dattend.astype(jnp.float32), axis=0)
    dcontext = jnp.einsum(
        "td,jd->tj", dattend, full_attn, preferred_element_type=jnp.float32
    ).astype(jnp.bfloat16)
    dcontext_blocks = dcontext.reshape(count, block, HEADS, HEAD_DIM)

    def attend_back(carry, item):
        dkeys, dvalues = carry
        query_block, dcontext_block, logsum_block = item
        probs = jnp.exp(masked_scores(query_block) - logsum_block[..., None])
        probb = probs.astype(jnp.bfloat16)
        dvalues = dvalues + jnp.einsum(
            "hqk,qhd->khd", probb, dcontext_block, preferred_element_type=jnp.float32
        )
        dprob = jnp.einsum(
            "qhd,khd->hqk", dcontext_block, values_all, preferred_element_type=jnp.float32
        )
        inner = jnp.sum(dprob * probs, axis=-1, keepdims=True)
        dscore = (probs * (dprob - inner)).astype(jnp.bfloat16)
        dquery = (
            jnp.einsum("hqk,khd->qhd", dscore, keys_all, preferred_element_type=jnp.float32) * 0.125
        )
        dkeys = (
            dkeys
            + jnp.einsum("hqk,qhd->khd", dscore, query_block, preferred_element_type=jnp.float32)
            * 0.125
        )
        return ((dkeys, dvalues), dquery)

    empty = jnp.zeros((seq, HEADS, HEAD_DIM), jnp.float32)
    (dkeys, dvalues), dqueries = lax.scan(
        attend_back, (empty, empty), (query_blocks, dcontext_blocks, logsum)
    )
    dpacked = jnp.concatenate(
        [dqueries.reshape(seq, D), dkeys.reshape(seq, D), dvalues.reshape(seq, D)], axis=1
    ).astype(jnp.bfloat16)
    grad_qkv = jnp.einsum("td,tj->dj", clip_in, dpacked, preferred_element_type=jnp.float32)
    dbias_qkv = jnp.sum(dpacked.astype(jnp.float32), axis=0)
    input_rows = [
        dres1 + jnp.einsum("tj,dj->td", dpacked, full_qkv, preferred_element_type=jnp.float32)
    ]
    grad_vec = grad_vec + jnp.concatenate(
        [
            dbias_qkv[:D],
            dbias_qkv[2 * D :],
            dbias_o,
            dgain1,
            dshift1,
            dbias1,
            dbias2,
            dgain2,
            dshift2,
        ]
    )
    locals_all = (grad_qkv, grad_attn, grad_in, grad_out, grad_vec)
    owned = (w_qkv, w_attn, w_in, w_out, vectors)
    def spread(matrix):
        return matrix.reshape(n, rows_d, -1, D).transpose(0, 2, 1, 3).reshape(n, -1, D)

    packed_grads = jnp.concatenate(
        [spread(grad_qkv), spread(grad_attn), spread(grad_in), grad_out.reshape(n, rows_f, D)],
        axis=1,
    ).astype(jnp.bfloat16)
    share = lax.psum_scatter(packed_grads, "dp", scatter_dimension=0, tiled=True)[0].astype(
        jnp.float32
    )

    def unblock(first, count):
        parts = [share[first + i * rows_d : first + (i + 1) * rows_d] for i in range(count)]
        return parts[0] if count == 1 else jnp.concatenate(parts, axis=1)

    total_vec = sum_all(grad_vec.reshape(-1, 128), n).reshape(-1)
    index = lax.axis_index("dp")
    shares = (
        unblock(0, 3),
        unblock(3 * rows_d, 1),
        unblock(4 * rows_d, FF // D),
        share[8 * rows_d :],
        lax.dynamic_slice_in_dim(total_vec, index * width, width, 0),
    )
    matrices = [w_qkv, w_attn, w_in, w_out]
    moments = [moment_qkv, moment_attn, moment_in, moment_out]
    squares = [square_qkv, square_attn, square_in, square_out]
    new_moments = []
    new_squares = []
    updates = []
    for weight, grad, moment, square in zip(matrices, shares[:4], moments, squares):
        new_moment, new_square, update = adapt(weight, grad, moment, square, 0.01)
        new_moments.append(new_moment)
        new_squares.append(new_square)
        updates.append(update)
    partial_sums = jnp.stack(
        [jnp.sum(weight * weight) for weight in matrices]
        + [jnp.sum(update * update) for update in updates]
    )
    norms = jnp.sqrt(sum_all(partial_sums, n))
    new_weights = [
        weight - 0.25 * (norms[place] / norms[4 + place]) * update
        for place, (weight, update) in enumerate(zip(matrices, updates))
    ]
    vec_moment, vec_square, vec_update = adapt(vectors, shares[4], moment_vec, square_vec, 0.0)
    new_vec = vectors - 0.4 * vec_update
    return (
        jnp.stack(mixed_rows),
        jnp.stack(input_rows),
        new_weights[0],
        new_weights[1],
        new_weights[2],
        new_weights[3],
        new_vec,
        new_moments[0],
        new_moments[1],
        new_moments[2],
        new_moments[3],
        vec_moment,
        new_squares[0],
        new_squares[1],
        new_squares[2],
        new_squares[3],
        vec_square,
        norms,
    )


def solution(mesh):
    placed = (
        P("dp", None, None),
        P("dp", None, None),
        P("dp"),
        P("dp", None),
        P("dp", None),
        P("dp", None),
        P("dp", None),
        P("dp"),
        P("dp", None),
        P("dp", None),
        P("dp", None),
        P("dp", None),
        P("dp"),
        P("dp", None),
        P("dp", None),
        P("dp", None),
        P("dp", None),
        P("dp"),
    )
    return jax.shard_map(
        partial(body, mesh.shape["dp"]),
        mesh=mesh,
        in_specs=placed,
        out_specs=(
            P("dp", None, None),
            P("dp", None, None),
            P("dp", None),
            P("dp", None),
            P("dp", None),
            P("dp", None),
            P("dp"),
            P("dp", None),
            P("dp", None),
            P("dp", None),
            P("dp", None),
            P("dp"),
            P("dp", None),
            P("dp", None),
            P("dp", None),
            P("dp", None),
            P("dp"),
            P(),
        ),
        check_vma=False,
    )
```

```python
from functools import partial

import jax
import jax.numpy as jnp
from jax import lax
from jax.experimental import pallas as pl
from jax.experimental.pallas import tpu as pltpu
from jax.sharding import PartitionSpec as P

D = 768
FF = 3072
HEADS = 12
HEAD_DIM = 64
PAIRS = HEADS // 2
WIDE = 2 * HEAD_DIM
CHUNKS = FF // D
STEP = 10
MASKED = -1e9
VMEM = 60 * 2**20
BF16 = jnp.bfloat16
F32 = jnp.float32


def dot(a, b):
    return jnp.dot(a, b, preferred_element_type=F32)


def dot_nt(a, b):
    return lax.dot_general(a, b, (((1,), (1,)), ((), ())), preferred_element_type=F32)


def dot_tn(a, b):
    return lax.dot_general(a, b, (((0,), (0,)), ((), ())), preferred_element_type=F32)


def cost(us):
    return pl.CostEstimate(flops=int(us * 5.0e7), bytes_accessed=0, transcendentals=0)


def arrange(value, matrix):
    return dot(value, matrix).astype(BF16)


def project_kernel(xa_ref, xb_ref, la_ref, lb_ref, ra_ref, rb_ref, bias_ref, out_ref):
    width = la_ref.shape[1]
    left = jnp.concatenate([la_ref[...], lb_ref[...]], axis=0)
    out_ref[:, :width] = (dot(xa_ref[...], left) + bias_ref[:, :width]).astype(BF16)
    right = jnp.concatenate([ra_ref[:, :width], rb_ref[:, :width]], axis=0)
    out_ref[:, width:] = (dot(xb_ref[...], right) + bias_ref[:, width:]).astype(BF16)


def project(x_a, x_b, left, right, bias):
    seq = x_a.shape[0]
    rows = min(512, seq)

    def fixed(shape):
        return pl.BlockSpec(shape, lambda i: (0, 0), pipeline_mode=pl.Buffered(1))

    return pl.pallas_call(
        project_kernel,
        grid=(seq // rows,),
        in_specs=[pl.BlockSpec((rows, D), lambda i: (i, 0))] * 2
        + [fixed(part.shape) for part in (*left, *right, bias)],
        out_specs=pl.BlockSpec((rows, 3 * D), lambda i: (i, 0)),
        out_shape=jax.ShapeDtypeStruct((seq, 3 * D), BF16),
        compiler_params=pltpu.CompilerParams(vmem_limit_bytes=VMEM),
        cost_estimate=cost(5),
        name="project",
    )(x_a, x_b, *left, *right, bias)


def attend_kernel(len_ref, q_ref, k_ref, v_ref, ctx_ref, ctxt_ref, lse_ref):
    seq = q_ref.shape[0]
    qt = (q_ref[...].astype(F32) * 0.125).T.astype(BF16)
    vt = v_ref[...].astype(F32).T.astype(BF16)
    k = k_ref[...]
    keep = lax.broadcasted_iota(jnp.int32, (seq, seq), 0) < len_ref[0]
    zero = jnp.zeros((HEAD_DIM, seq), BF16)
    ones = jnp.ones((16, seq), BF16)
    for h in range(2):
        rows = slice(h * HEAD_DIM, (h + 1) * HEAD_DIM)
        q = jnp.concatenate([qt[rows], zero] if h == 0 else [zero, qt[rows]], axis=0)
        scores = jnp.where(keep, dot(k, q), MASKED)
        peak = jnp.max(scores, axis=0, keepdims=True)
        expo = jnp.exp(scores - peak).astype(BF16)
        both = dot(jnp.concatenate([vt[rows], ones], axis=0), expo)
        total = both[HEAD_DIM : HEAD_DIM + 1]
        ctxt_ref[rows, :] = both[:HEAD_DIM] / total
        lse_ref[0, h : h + 1, :] = peak + jnp.log(total)
    ctx_ref[...] = ctxt_ref[...].T.astype(BF16)


def after(kernel, first, count):
    def call(*refs):
        kernel(*refs[:first], *refs[first + count :])

    return call


def untouched(values):
    return [pl.BlockSpec(memory_space=pl.ANY)] * len(values)


def attend(lengths, packed, first, count, before=(), waits=()):
    seq = packed.shape[0]
    extra = (*before, *waits)
    return pl.pallas_call(
        after(attend_kernel, 4, len(extra)),
        grid_spec=pltpu.PrefetchScalarGridSpec(
            num_scalar_prefetch=1,
            grid=(count,),
            in_specs=[
                pl.BlockSpec((seq, WIDE), lambda p, _, i=i: (0, i * PAIRS + first + p))
                for i in range(3)
            ]
            + untouched(extra),
            out_specs=[
                pl.BlockSpec((seq, WIDE), lambda p, _: (0, first + p)),
                pl.BlockSpec((WIDE, seq), lambda p, _: (first + p, 0)),
                pl.BlockSpec((1, 2, seq), lambda p, _: (first + p, 0, 0)),
            ],
        ),
        out_shape=[
            jax.ShapeDtypeStruct((seq, D), BF16),
            jax.ShapeDtypeStruct((D, seq), F32),
            jax.ShapeDtypeStruct((PAIRS, 2, seq), F32),
        ],
        input_output_aliases={4 + i: i for i in range(len(before))},
        compiler_params=pltpu.CompilerParams(vmem_limit_bytes=VMEM),
        cost_estimate=cost(4 * count),
        name="attend",
    )(lengths, packed, packed, packed, *extra)


def attend_back_kernel(
    block, len_ref, q_ref, k_ref, v_ref, do_ref, ctxt_ref, lse_ref, out_ref, sum_ref, dqt_ref
):
    seq = q_ref.shape[0]
    q = q_ref[...].astype(F32) * 0.125
    qt = q.T.astype(BF16)
    q = q.astype(BF16)
    do = do_ref[...]
    dof = do.astype(F32).T
    dot_ = dof.astype(BF16)
    prod = dof * ctxt_ref[...]
    kt = k_ref[...].astype(F32).T.astype(BF16)
    row = lax.broadcasted_iota(jnp.int32, (HEAD_DIM, seq), 0)

    def pieces(vec):
        high = vec.astype(BF16).astype(F32)
        mid = (vec - high).astype(BF16).astype(F32)
        low = vec - high - mid
        picked = jnp.where(row == 1, mid, jnp.where(row == 2, low, 0.0))
        return jnp.where(row == 0, high, picked).astype(BF16)

    q_aug, do_aug, fill = [], [], []
    for h in range(2):
        rows = slice(h * HEAD_DIM, (h + 1) * HEAD_DIM)
        lse = lse_ref[0, h : h + 1]
        delta = jnp.sum(prod[rows], axis=0, keepdims=True)
        q_parts = [qt[rows], pieces(-lse)]
        do_parts = [dot_[rows], pieces(-delta)]
        q_aug.append(jnp.concatenate(q_parts if h == 0 else q_parts[::-1], axis=0))
        do_aug.append(jnp.concatenate(do_parts if h == 0 else do_parts[::-1], axis=0))
        fill.append(MASKED - lse)
    lane = lax.broadcasted_iota(jnp.int32, (block, WIDE), 1)
    mine = (lane < HEAD_DIM, lane >= HEAD_DIM)
    one = (
        jnp.where(lane < HEAD_DIM + 3, 1.0, 0.0).astype(BF16),
        jnp.where(lane < 3, 1.0, 0.0).astype(BF16),
    )
    for j in range(seq // block):
        rows = slice(j * block, (j + 1) * block)
        keep = lax.broadcasted_iota(jnp.int32, (block, seq), 0) + j * block < len_ref[0]
        k, v = k_ref[rows, :], v_ref[rows, :]
        dv, dk = [], []
        for h in range(2):
            heads = slice(h * HEAD_DIM, (h + 1) * HEAD_DIM)
            k_aug, v_aug = jnp.where(mine[h], k, one[h]), jnp.where(mine[h], v, one[h])
            prob = jnp.exp(jnp.where(keep, dot(k_aug, q_aug[h]), fill[h]))
            dscore = (prob * dot(v_aug, do_aug[h])).astype(BF16)
            dv.append(dot(prob.astype(BF16), do))
            dk.append(dot(dscore, q))
            dq = dot(kt[heads, rows], dscore)
            if j == 0:
                dqt_ref[heads, :] = dq
            else:
                dqt_ref[heads, :] += dq
        out_ref[1, rows, :] = jnp.where(mine[0], dk[0], dk[1]).astype(BF16)
        out_ref[2, rows, :] = jnp.where(mine[0], dv[0], dv[1]).astype(BF16)
    out_ref[0] = (dqt_ref[...] * 0.125).T.astype(BF16)
    sum_ref[0, 0:1] = jnp.sum(out_ref[0].astype(F32), axis=0, keepdims=True)
    sum_ref[0, 1:2] = jnp.sum(out_ref[2].astype(F32), axis=0, keepdims=True)


def attend_back(lengths, packed, dctx, ctxt, lse, first, count, before=None, waits=()):
    seq = packed.shape[0]
    extra = tuple(waits) if before is None else (before, *waits)
    return pl.pallas_call(
        after(partial(attend_back_kernel, min(512, seq)), 7, len(extra)),
        grid_spec=pltpu.PrefetchScalarGridSpec(
            num_scalar_prefetch=1,
            grid=(count,),
            in_specs=[
                pl.BlockSpec((seq, WIDE), lambda p, _, i=i: (0, i * PAIRS + first + p))
                for i in range(3)
            ]
            + [
                pl.BlockSpec((seq, WIDE), lambda p, _: (0, first + p)),
                pl.BlockSpec((WIDE, seq), lambda p, _: (first + p, 0)),
                pl.BlockSpec((1, 2, seq), lambda p, _: (first + p, 0, 0)),
            ]
            + untouched(extra),
            out_specs=[
                pl.BlockSpec((3, seq, WIDE), lambda p, _: (0, 0, first + p)),
                pl.BlockSpec((1, 2, WIDE), lambda p, _: (p, 0, 0)),
            ],
            scratch_shapes=[pltpu.VMEM((WIDE, seq), F32)],
        ),
        out_shape=[
            jax.ShapeDtypeStruct((3, seq, D), BF16),
            jax.ShapeDtypeStruct((count, 2, WIDE), F32),
        ],
        input_output_aliases={} if before is None else {7: 0},
        compiler_params=pltpu.CompilerParams(vmem_limit_bytes=VMEM),
        cost_estimate=cost(6 * count),
        name="attend_back",
    )(lengths, packed, packed, packed, dctx, ctxt, lse, *extra)


def normal_parts(u):
    return 0.5 + 0.5 * lax.erf(u * 0.7071067811865476), jnp.exp(-0.5 * u * u)


def norm_forward(resid):
    center = resid - jnp.mean(resid, axis=-1, keepdims=True)
    inverse = lax.rsqrt(jnp.mean(center * center, axis=-1, keepdims=True) + 1e-05)
    return center * inverse, inverse


def norm_back(grad, gain, unit, inverse):
    du = grad * gain
    mean = jnp.mean(du, axis=-1, keepdims=True)
    return inverse * (du - mean - unit * jnp.mean(du * unit, axis=-1, keepdims=True))


def column_sum(value):
    return jnp.sum(value.astype(F32), axis=0, keepdims=True)


def feed_kernel(
    pieces,
    len_ref,
    place_ref,
    x_ref,
    ctx_ref,
    cot_ref,
    wo_ref,
    w1a_ref,
    w1b_ref,
    w1c_ref,
    w1d_ref,
    vec_ref,
    to_a_ref,
    to_b_ref,
    *refs,
):
    parts = refs[: len(pieces)]
    refs = refs[len(pieces) :]
    feed_step(
        pieces,
        parts,
        len_ref,
        place_ref,
        x_ref,
        ctx_ref,
        cot_ref,
        wo_ref,
        (w1a_ref, w1b_ref, w1c_ref, w1d_ref),
        vec_ref,
        to_a_ref,
        to_b_ref,
        *refs,
    )


def feed_step(
    pieces,
    parts,
    len_ref,
    place_ref,
    x_ref,
    ctx_ref,
    cot_ref,
    wo_ref,
    w1_refs,
    vec_ref,
    to_a_ref,
    to_b_ref,
    mixed_ref,
    first_ref,
    ctx_out_ref,
    act_ref,
    dbranch_ref,
    dhidden_ref,
    dres_ref,
    unit_ref,
    inverse_ref,
    sum_ref,
    slope_ref,
    w2_ref,
    sems,
):
    step = pl.program_id(0)
    rows = x_ref.shape[0]

    def copies():
        made = []
        for part, (first, count, column) in zip(parts, pieces):
            size, width = part.shape[0] // count, part.shape[1]
            for i in range(count):
                where = pl.multiple_of(place_ref[first + i] * size, size)
                target = w2_ref.at[pl.ds(where, size), pl.ds(column, width)]
                source = part.at[pl.ds(i * size, size), :]
                made.append(pltpu.make_async_copy(source, target, sems.at[len(made)]))
        return made

    def vec(i):
        return vec_ref[i : i + 1, :]

    @pl.when(step == 0)
    def _():
        for copy in copies():
            copy.start()
        sum_ref[...] = jnp.zeros_like(sum_ref)

    resid = x_ref[...].astype(F32) + (dot(ctx_ref[...], wo_ref[...]) + vec(2))
    unit1, inverse1 = norm_forward(resid)
    unit_ref[...] = unit1
    inverse_ref[...] = jnp.broadcast_to(inverse1, inverse_ref.shape)
    first = unit1 * vec(3) + vec(4)
    first_b = first.astype(BF16)
    first_ref[...] = arrange(first_b, to_a_ref[...])
    ctx_out_ref[...] = arrange(ctx_ref[...], to_b_ref[...])

    @pl.when(step == 0)
    def _():
        for copy in copies():
            copy.wait()

    branch = None
    for c in range(CHUNKS):
        cols = slice(c * D, (c + 1) * D)
        hidden = dot(first_b, w1_refs[c][...]) + vec(5 + c)
        phi, bell = normal_parts(hidden)
        active = (hidden * phi).astype(BF16)
        act_ref[:, cols] = active
        slope_ref[:, cols] = phi + hidden * bell * 0.3989422804014327
        part = dot(active, w2_ref[cols, :])
        branch = part if branch is None else branch + part
    unit2, inverse2 = norm_forward(first + (branch + vec(9)))
    place = lax.broadcasted_iota(jnp.int32, (rows, 1), 0) + step * rows
    keep = (place < len_ref[0]).astype(F32)
    mixed_ref[...] = ((unit2 * vec(10) + vec(11)) * keep).astype(BF16)
    dz = cot_ref[...].astype(F32) * keep
    dres2 = norm_back(dz, vec(10), unit2, inverse2)
    dres_ref[...] = dres2
    dbranch = dres2.astype(BF16)
    dbranch_ref[...] = dbranch
    sum_ref[9:10, :] += column_sum(dbranch)
    sum_ref[10:11, :] += column_sum(dz * unit2)
    sum_ref[11:12, :] += column_sum(dz)
    for c in range(CHUNKS):
        cols = slice(c * D, (c + 1) * D)
        dhidden = (dot_nt(dbranch, w2_ref[cols, :]) * slope_ref[:, cols]).astype(BF16)
        dhidden_ref[:, cols] = dhidden
        sum_ref[5 + c : 6 + c, :] += column_sum(dhidden)


def feed(lengths, x, ctx, cot, attn_in, vec, to_a, to_b, places, parts, pieces):
    seq = x.shape[0]
    rows = min(256, seq)

    def row(width):
        return pl.BlockSpec((rows, width), lambda i, *_: (i, 0))

    def fixed(shape, column=0):
        return pl.BlockSpec(shape, lambda i, *_: (0, column), pipeline_mode=pl.Buffered(1))

    outs = ((D, BF16), (D, BF16), (D, BF16), (FF, BF16), (D, BF16), (FF, BF16), (D, F32), (D, F32), (128, F32))
    return pl.pallas_call(
        partial(feed_kernel, pieces),
        grid_spec=pltpu.PrefetchScalarGridSpec(
            num_scalar_prefetch=2,
            grid=(seq // rows,),
            in_specs=[row(D), row(D), row(D)]
            + [fixed((D, D), c) for c in range(1 + CHUNKS)]
            + [fixed((12, D)), fixed((D, D)), fixed((D, D))]
            + untouched(parts),
            out_specs=[row(width) for width, _ in outs]
            + [pl.BlockSpec((12, D), lambda i, *_: (0, 0))],
            scratch_shapes=[
                pltpu.VMEM((rows, FF), F32),
                pltpu.VMEM((FF, D), BF16),
                pltpu.SemaphoreType.DMA((sum(count for _, count, _ in pieces),)),
            ],
        ),
        out_shape=[jax.ShapeDtypeStruct((seq, width), kind) for width, kind in outs]
        + [jax.ShapeDtypeStruct((12, D), F32)],
        compiler_params=pltpu.CompilerParams(vmem_limit_bytes=VMEM),
        cost_estimate=cost(28),
        name="feed",
    )(lengths, places, x, ctx, cot, *(attn_in,) * (1 + CHUNKS), vec, to_a, to_b, *parts)


def out_grad_kernel(blocks, where_ref, act_ref, grad_ref, out_ref, held_ref, sems):
    step, slot = pl.program_id(0), lax.rem(pl.program_id(0), 2)
    size = held_ref.shape[1] // blocks

    def copies(step, slot):
        made = []
        for i in range(blocks):
            place = pl.multiple_of(where_ref[step * blocks + i] * size, size)
            source = held_ref.at[slot, pl.ds(i * size, size), :]
            target = out_ref.at[pl.ds(place, size), :]
            made.append(pltpu.make_async_copy(source, target, sems.at[slot, i]))
        return made

    @pl.when(step >= 2)
    def _():
        for copy in copies(step - 2, slot):
            copy.wait()

    held_ref[slot] = dot_tn(act_ref[...], grad_ref[...]).astype(BF16)
    for copy in copies(step, slot):
        copy.start()

    @pl.when(step == CHUNKS - 1)
    def _():
        for copy in copies(step - 1, 1 - slot) + copies(step, slot):
            copy.wait()


def out_grad(act, grad, where):
    seq, blocks = act.shape[0], where.shape[0] // CHUNKS
    return pl.pallas_call(
        partial(out_grad_kernel, blocks),
        grid_spec=pltpu.PrefetchScalarGridSpec(
            num_scalar_prefetch=1,
            grid=(CHUNKS,),
            in_specs=[
                pl.BlockSpec((seq, D), lambda i, _: (0, i)),
                pl.BlockSpec((seq, D), lambda i, _: (0, 0), pipeline_mode=pl.Buffered(1)),
            ],
            out_specs=pl.BlockSpec(memory_space=pl.ANY),
            scratch_shapes=[
                pltpu.VMEM((2, D, D), BF16),
                pltpu.SemaphoreType.DMA((2, blocks)),
            ],
        ),
        out_shape=jax.ShapeDtypeStruct((FF, D), BF16),
        compiler_params=pltpu.CompilerParams(vmem_limit_bytes=VMEM),
        cost_estimate=cost(8),
        name="out_grad",
    )(where, act, grad)


def feed_back_kernel(
    dhidden_ref,
    dres_ref,
    unit_ref,
    inverse_ref,
    wo_ref,
    w1a_ref,
    w1b_ref,
    w1c_ref,
    w1d_ref,
    vec_ref,
    dres1_ref,
    dattend_ref,
    dctx_ref,
    sum_ref,
):
    @pl.when(pl.program_id(0) == 0)
    def _():
        sum_ref[...] = jnp.zeros_like(sum_ref)

    dfirst = dres_ref[...]
    for c, w1_ref in enumerate((w1a_ref, w1b_ref, w1c_ref, w1d_ref)):
        dfirst = dfirst + dot_nt(dhidden_ref[:, c * D : (c + 1) * D], w1_ref[...])
    unit = unit_ref[...]
    dres1 = norm_back(dfirst, vec_ref[3:4, :], unit, inverse_ref[:, 0:1])
    dres1_ref[...] = dres1
    dattend = dres1.astype(BF16)
    dattend_ref[...] = dattend
    dctx_ref[...] = dot_nt(dattend, wo_ref[...]).astype(BF16)
    sum_ref[2:3, :] += column_sum(dattend)
    sum_ref[3:4, :] += column_sum(dfirst * unit)
    sum_ref[4:5, :] += column_sum(dfirst)


def feed_back(dhidden, dres2, unit, inverse, attn_in, vec, waits=()):
    seq = dhidden.shape[0]
    rows = min(256, seq)

    def row(width):
        return pl.BlockSpec((rows, width), lambda i: (i, 0))

    def fixed(shape, column=0):
        return pl.BlockSpec(shape, lambda i: (0, column), pipeline_mode=pl.Buffered(1))

    return pl.pallas_call(
        after(feed_back_kernel, 10, len(waits)),
        grid=(seq // rows,),
        in_specs=[row(FF), row(D), row(D), row(128)]
        + [fixed((D, D), c) for c in range(1 + CHUNKS)]
        + [fixed((12, D))]
        + untouched(waits),
        out_specs=[row(D), row(D), row(D), pl.BlockSpec((8, D), lambda i: (0, 0))],
        out_shape=[
            jax.ShapeDtypeStruct((seq, D), F32),
            jax.ShapeDtypeStruct((seq, D), BF16),
            jax.ShapeDtypeStruct((seq, D), BF16),
            jax.ShapeDtypeStruct((8, D), F32),
        ],
        compiler_params=pltpu.CompilerParams(vmem_limit_bytes=VMEM),
        cost_estimate=cost(14),
        name="feed_back",
    )(dhidden, dres2, unit, inverse, *(attn_in,) * (1 + CHUNKS), vec, *waits)


def swap(value, bit, n):
    return lax.ppermute(value, "dp", [(i, i ^ (1 << bit)) for i in range(n)])


def sum_all(value, n):
    for bit in range(n.bit_length() - 1):
        value = value + swap(value, bit, n)
    return value


def own_bit(bit):
    return (lax.axis_index("dp") >> bit) & 1


def phase(*values):
    return lax.optimization_barrier(values)


class Order:
    def __init__(self, bits):
        self.bits, self.n = bits, 2 ** len(bits)

    def mask(self, place):
        return sum(((place >> k) & 1) << bit for k, bit in enumerate(self.bits))

    def matrix(self):
        rows = D // self.n
        place = jnp.arange(D, dtype=jnp.int32)
        block = self.mask(place // rows) ^ lax.axis_index("dp")
        source = block * rows + place % rows
        return (place[:, None] == source[None, :]).astype(BF16)

    def where(self):
        other = jnp.arange(self.n, dtype=jnp.int32) ^ lax.axis_index("dp")
        return sum(((other >> bit) & 1) << k for k, bit in enumerate(self.bits))

    def places(self, count):
        return self.mask(jnp.arange(count, dtype=jnp.int32)) ^ lax.axis_index("dp")


class Gather:
    def __init__(self, shard, n):
        self.value, self.n = shard, n

    def step(self, bit):
        self.value = jnp.concatenate([self.value, swap(self.value, bit, self.n)], axis=0)

    def cut(self, start, stop):
        return Gather(self.value[:, start:stop], self.n)


class Scatter:
    def __init__(self, value, n):
        self.terms, self.n = [value], n

    def step(self, bit):
        half = self.terms[0].shape[0] // 2
        away = self.total([t[half:] for t in self.terms]).astype(BF16)
        self.terms = [t[:half] for t in self.terms] + [swap(away, bit, self.n)]

    def total(self, parts=None):
        parts = self.terms if parts is None else parts
        result = parts[0].astype(F32)
        for part in parts[1:]:
            result = result + part.astype(F32)
        return result

    def join(self, other):
        self.terms = [jnp.concatenate([self.total(), other.total()], axis=1)]
        return self


def adapt(weight, grad, moment, square, decay):
    new_moment = 0.9 * moment + 0.1 * grad
    new_square = 0.999 * square + 0.001 * grad * grad
    update = new_moment / (1.0 - 0.9**STEP) / (jnp.sqrt(new_square / (1.0 - 0.999**STEP)) + 1e-06)
    return (new_moment, new_square, update + decay * weight)


def lane_sums(value):
    columns = jnp.sum(value * value, axis=0, keepdims=True)
    result = columns[:, :128]
    for start in range(128, value.shape[1], 128):
        result = result + columns[:, start : start + 128]
    return result


def adapt_kernel(first, *refs):
    before_ref, sums_ref = refs[8], refs[15]
    sums = before_ref[...]
    row = lax.broadcasted_iota(jnp.int32, sums.shape, 0)
    for i in range(2):
        weight_ref, grad_ref, moment_ref, square_ref = refs[i * 4 : i * 4 + 4]
        outs = refs[9 + i * 3 : 12 + i * 3]
        weight = weight_ref[...]
        values = adapt(weight, grad_ref[...], moment_ref[...], square_ref[...], 0.01)
        for out, value in zip(outs, values):
            out[...] = value
        sums = jnp.where(row == first + i, lane_sums(weight), sums)
        sums = jnp.where(row == 4 + first + i, lane_sums(values[2]), sums)
    sums_ref[...] = sums


def adapt_two(first, before, *operands):
    shapes = [jax.ShapeDtypeStruct(operands[i * 4].shape, F32) for i in (0, 0, 0, 1, 1, 1)]
    return pl.pallas_call(
        partial(adapt_kernel, first),
        out_shape=shapes + [jax.ShapeDtypeStruct((8, 128), F32)],
        compiler_params=pltpu.CompilerParams(vmem_limit_bytes=VMEM),
        cost_estimate=cost(2),
        name="adapt",
    )(*operands, before)


def renew_kernel(sums_ref, *refs):
    norms = jnp.sqrt(jnp.sum(sums_ref[...], axis=1, keepdims=True))
    refs[12][...] = jnp.broadcast_to(norms, (8, 128))
    for i in range(4):
        rate = 0.25 * (norms[i : i + 1] / norms[4 + i : 5 + i])
        refs[8 + i][...] = refs[i][...] - rate * refs[4 + i][...]


def renew(sums, weights, updates):
    return pl.pallas_call(
        renew_kernel,
        out_shape=[jax.ShapeDtypeStruct(weight.shape, F32) for weight in weights]
        + [jax.ShapeDtypeStruct((8, 128), F32)],
        compiler_params=pltpu.CompilerParams(vmem_limit_bytes=VMEM),
        cost_estimate=cost(2),
        name="renew",
    )(sums, *weights, *updates)


def body(
    n,
    frames,
    cotangent,
    lengths,
    w_qkv,
    w_attn,
    w_in,
    w_out,
    vectors,
    moment_qkv,
    moment_attn,
    moment_in,
    moment_out,
    moment_vec,
    square_qkv,
    square_attn,
    square_in,
    square_out,
    square_vec,
):
    rows_d, rows_f, width = w_qkv.shape[0], w_out.shape[0], vectors.shape[0]
    core, one, two, *others = range(n.bit_length() - 1)
    far = others[::-1]
    order_a, order_b = Order(far + [two, one, core]), Order(far + [one, two, core])
    x = frames[0]

    half = w_qkv.shape[1] // 2
    tail = jnp.pad(vectors.reshape(rows_d, 12), ((0, 0), (0, 116)))
    low_qkv = jnp.concatenate([w_qkv, tail], axis=1).astype(BF16)
    low_qkv, w_first, w_second, w_third = phase(low_qkv, w_attn, w_in, w_out)
    attn_in = jnp.concatenate([w_first, w_second], axis=1).astype(BF16)
    attn_in = lax.all_gather(attn_in, "dp", axis=0, tiled=True)
    qkv, out = Gather(low_qkv, n), Gather(w_third.astype(BF16), n)
    to_a, to_b = order_a.matrix(), order_b.matrix()
    x_a, x_b = arrange(x, to_a), arrange(x, to_b)
    for bit in far:
        qkv.step(bit)
        qkv.value, x_a, x_b = phase(qkv.value, x_a, x_b)
    left, right = qkv.cut(0, half), qkv.cut(half, 2 * half + 128)
    left.step(two)
    right.step(one)
    left.value, right.value, out.value = phase(left.value, right.value, out.value)
    for bit in far[:1]:
        out.step(bit)
    left.step(one)
    right.step(two)
    left.value, right.value = phase(left.value, right.value)
    left = (left.value, swap(left.value, core, n))
    right = (right.value, swap(right.value, core, n))
    left, right, out.value = phase(left, right, out.value)
    for bit in far[1:]:
        out.step(bit)
    vec_rows = jnp.concatenate([part[:, half:] for part in right], axis=0)
    vec = dot(to_b, vec_rows)[:, :12].reshape(12, D)
    bias_qkv = jnp.concatenate([vec[:1], jnp.zeros((1, D), F32), vec[1:2]], axis=1)

    packed = project(x_a, x_b, left, right, bias_qkv)
    packed, out.value = phase(packed, out.value)
    out_left, out_right = out.cut(0, D // 2), out.cut(D // 2, D)
    out_left.step(two)
    out_right.step(one)
    some = PAIRS // 2
    heads = attend(lengths, packed, 0, some)
    heads, out_left.value, out_right.value, attn_in = phase(
        heads, out_left.value, out_right.value, attn_in
    )
    out_left.step(one)
    out_right.step(two)
    heads = attend(lengths, packed, some, some, heads)
    heads, out_left.value, out_right.value = phase(heads, out_left.value, out_right.value)
    parts = [out_left.value, swap(out_left.value, core, n)]
    parts += [out_right.value, swap(out_right.value, core, n)]
    if rows_f % 16 == 0:
        places = jnp.concatenate([order_a.places(n), order_b.places(n)])
        pieces = tuple((i * n // 2, n // 2, i // 2 * (D // 2)) for i in range(4))
    else:
        sides = []
        for i, order in ((0, order_a), (2, order_b)):
            side = jnp.concatenate(parts[i : i + 2], axis=0).reshape(n, rows_f, D // 2)
            sides.append(side[jnp.argsort(order.places(n))].reshape(FF, D // 2))
        parts = [jnp.concatenate(sides, axis=1)]
        places, pieces = jnp.zeros((1,), jnp.int32), ((0, 1, 0),)
    ctx, ctxt, lse = heads

    mixed, first, ctx_b, act, dbranch, dhidden, dres2, unit, inverse, sums2 = feed(
        lengths, x, ctx, cotangent[0], attn_in, vec, to_a, to_b, places, parts, pieces
    )
    if rows_f % 16 == 0:
        grad_out = out_grad(act, dbranch, order_b.where())
    else:
        grad_out = dot_tn(act, dbranch).astype(BF16).reshape(n, rows_f, D)
        grad_out = grad_out[order_b.places(n)].reshape(FF, D)
    dhidden, grad_out = phase(dhidden, grad_out)
    sum_out = Scatter(grad_out, n)
    sum_out.step(core)
    grad_in = dot_tn(first, dhidden).astype(BF16)
    dhidden, grad_in = phase(dhidden, grad_in)
    sum_in = Scatter(grad_in, n)
    sum_in.step(core)
    dres1, dattend, dctx, sums1 = feed_back(dhidden, dres2, unit, inverse, attn_in, vec)

    sum_in.terms[-1], sum_out.terms[-1], dattend, dctx = phase(
        sum_in.terms[-1], sum_out.terms[-1], dattend, dctx
    )
    sum_in.step(one)
    sum_out.step(two)
    grad_attn = dot_tn(ctx_b, dattend).astype(BF16)
    some = 2 * PAIRS // 3
    dqkv, bias_a = attend_back(lengths, packed, dctx, ctxt, lse, 0, some, None, (grad_attn,))
    sum_in.terms[-1], sum_out.terms[-1], dqkv = phase(
        sum_in.terms[-1], sum_out.terms[-1], dqkv
    )
    sum_in.step(two)
    sum_out.step(one)
    dqkv, bias_b = attend_back(lengths, packed, dctx, ctxt, lse, some, PAIRS - some, dqkv)
    sum_in.terms[-1], sum_out.terms[-1], dqkv, bias_b = phase(
        sum_in.terms[-1], sum_out.terms[-1], dqkv, bias_b
    )
    sum_in.step(others[0])
    sum_out.step(others[0])
    late_a = Scatter(
        jnp.concatenate([dot_tn(x_a, dqkv[i]).astype(BF16) for i in range(2)], axis=1), n
    )
    late_b = Scatter(
        jnp.concatenate([dot_tn(x_b, dqkv[2]).astype(BF16), grad_attn], axis=1), n
    )
    bias_sums = jnp.concatenate([bias_a, bias_b], axis=0)
    grad_vec = jnp.concatenate(
        [
            bias_sums[:, 0].reshape(1, D),
            bias_sums[:, 1].reshape(1, D),
            sums1[2:5],
            sums2[5:],
        ]
    ).reshape(-1, 128)
    late_a.terms, late_b.terms, sum_in.terms[-1], sum_out.terms[-1] = phase(
        late_a.terms, late_b.terms, sum_in.terms[-1], sum_out.terms[-1]
    )
    for bit in others[1:]:
        sum_in.step(bit)
        sum_out.step(bit)
    share_in, share_out = sum_in.total(), sum_out.total()
    for bits in ((core, core), (one, two), (two, one)):
        late_a.step(bits[0])
        late_b.step(bits[1])
        late_a.terms[-1], late_b.terms[-1] = phase(late_a.terms[-1], late_b.terms[-1])
    late = late_a.join(late_b)
    for bit in others:
        late.step(bit)
    share_late = late.total()
    full_qkv = jnp.concatenate(
        [
            arrange(to_a, jnp.concatenate(left, axis=0)),
            arrange(to_b, jnp.concatenate([part[:, :half] for part in right], axis=0)),
        ],
        axis=1,
    )
    input_grad = dres1
    for i in range(3):
        input_grad = input_grad + dot_nt(dqkv[i], full_qkv[:, i * D : (i + 1) * D])

    next_in = adapt_two(
        2,
        jnp.zeros((8, 128), F32),
        *(w_in, share_in, moment_in, square_in),
        *(w_out, share_out, moment_out, square_out),
    )
    next_attn = adapt_two(
        0,
        next_in[6],
        *(w_qkv, share_late[:, : 3 * D], moment_qkv, square_qkv),
        *(w_attn, share_late[:, 3 * D :], moment_attn, square_attn),
    )
    sums = sum_all(jnp.concatenate([next_attn[6], grad_vec], axis=0), n)
    place = lax.axis_index("dp") * width
    share_vec = lax.dynamic_slice_in_dim(sums[8:].reshape(-1), place, width, 0)
    updates = (next_attn[2], next_attn[5], next_in[2], next_in[5])
    *new_weights, norms = renew(sums[:8], (w_qkv, w_attn, w_in, w_out), updates)
    vec_moment, vec_square, vec_update = adapt(vectors, share_vec, moment_vec, square_vec, 0.0)
    return (
        mixed[None],
        input_grad[None],
        *new_weights,
        vectors - 0.4 * vec_update,
        *(next_attn[0], next_attn[3], next_in[0], next_in[3], vec_moment),
        *(next_attn[1], next_attn[4], next_in[1], next_in[4], vec_square),
        norms[:, 0],
    )


def solution(mesh):
    clips, matrix, vector = P("dp", None, None), P("dp", None), P("dp")
    parameters = (matrix,) * 4 + (vector,)
    return jax.shard_map(
        partial(body, mesh.shape["dp"]),
        mesh=mesh,
        in_specs=(clips, clips, vector) + parameters * 3,
        out_specs=(clips, clips) + parameters * 3 + (P(),),
        check_vma=False,
    )
```

```python
from functools import partial

import jax
import jax.numpy as jnp
from jax import lax
from jax.experimental import pallas as pl
from jax.experimental.pallas import tpu as pltpu
from jax.sharding import PartitionSpec as P

D = 768
FF = 3072
HEADS = 12
HEAD_DIM = 64
PAIRS = HEADS // 2
WIDE = 2 * HEAD_DIM
CHUNKS = FF // D
STEP = 10
MASKED = -1e9
VMEM = 60 * 2**20
BF16 = jnp.bfloat16
F32 = jnp.float32


def dot(a, b):
    return jnp.dot(a, b, preferred_element_type=F32)


def dot_nt(a, b):
    return lax.dot_general(a, b, (((1,), (1,)), ((), ())), preferred_element_type=F32)


def dot_tn(a, b):
    return lax.dot_general(a, b, (((0,), (0,)), ((), ())), preferred_element_type=F32)


def cost(us):
    return pl.CostEstimate(flops=int(us * 5.0e7), bytes_accessed=0, transcendentals=0)


def arrange(value, matrix):
    return dot(value, matrix).astype(BF16)


def project_kernel(xa_ref, xb_ref, la_ref, lb_ref, ra_ref, rb_ref, bias_ref, out_ref):
    width = la_ref.shape[1]
    left = jnp.concatenate([la_ref[...], lb_ref[...]], axis=0)
    out_ref[:, :width] = (dot(xa_ref[...], left) + bias_ref[:, :width]).astype(BF16)
    right = jnp.concatenate([ra_ref[:, :width], rb_ref[:, :width]], axis=0)
    out_ref[:, width:] = (dot(xb_ref[...], right) + bias_ref[:, width:]).astype(BF16)


def project(x_a, x_b, left, right, bias):
    seq = x_a.shape[0]
    rows = min(512, seq)

    def fixed(shape):
        return pl.BlockSpec(shape, lambda i: (0, 0), pipeline_mode=pl.Buffered(1))

    return pl.pallas_call(
        project_kernel,
        grid=(seq // rows,),
        in_specs=[pl.BlockSpec((rows, D), lambda i: (i, 0))] * 2
        + [fixed(part.shape) for part in (*left, *right, bias)],
        out_specs=pl.BlockSpec((rows, 3 * D), lambda i: (i, 0)),
        out_shape=jax.ShapeDtypeStruct((seq, 3 * D), BF16),
        compiler_params=pltpu.CompilerParams(vmem_limit_bytes=VMEM),
        cost_estimate=cost(5),
        name="project",
    )(x_a, x_b, *left, *right, bias)


def attend_kernel(len_ref, q_ref, k_ref, v_ref, ctx_ref, ctxt_ref, lse_ref):
    seq = q_ref.shape[0]
    qt = (q_ref[...].astype(F32) * 0.125).T.astype(BF16)
    vt = v_ref[...].astype(F32).T.astype(BF16)
    k = k_ref[...]
    keep = lax.broadcasted_iota(jnp.int32, (seq, seq), 0) < len_ref[0]
    zero = jnp.zeros((HEAD_DIM, seq), BF16)
    ones = jnp.ones((16, seq), BF16)
    for h in range(2):
        rows = slice(h * HEAD_DIM, (h + 1) * HEAD_DIM)
        q = jnp.concatenate([qt[rows], zero] if h == 0 else [zero, qt[rows]], axis=0)
        scores = jnp.where(keep, dot(k, q), MASKED)
        peak = jnp.max(scores, axis=0, keepdims=True)
        expo = jnp.exp(scores - peak).astype(BF16)
        both = dot(jnp.concatenate([vt[rows], ones], axis=0), expo)
        total = both[HEAD_DIM : HEAD_DIM + 1]
        ctxt_ref[rows, :] = both[:HEAD_DIM] / total
        lse_ref[0, h : h + 1, :] = peak + jnp.log(total)
    ctx_ref[...] = ctxt_ref[...].T.astype(BF16)


def after(kernel, first, count):
    def call(*refs):
        kernel(*refs[:first], *refs[first + count :])

    return call


def untouched(values):
    return [pl.BlockSpec(memory_space=pl.ANY)] * len(values)


def attend(lengths, packed, first, count, before=(), waits=()):
    seq = packed.shape[0]
    extra = (*before, *waits)
    return pl.pallas_call(
        after(attend_kernel, 4, len(extra)),
        grid_spec=pltpu.PrefetchScalarGridSpec(
            num_scalar_prefetch=1,
            grid=(count,),
            in_specs=[
                pl.BlockSpec((seq, WIDE), lambda p, _, i=i: (0, i * PAIRS + first + p))
                for i in range(3)
            ]
            + untouched(extra),
            out_specs=[
                pl.BlockSpec((seq, WIDE), lambda p, _: (0, first + p)),
                pl.BlockSpec((WIDE, seq), lambda p, _: (first + p, 0)),
                pl.BlockSpec((1, 2, seq), lambda p, _: (first + p, 0, 0)),
            ],
        ),
        out_shape=[
            jax.ShapeDtypeStruct((seq, D), BF16),
            jax.ShapeDtypeStruct((D, seq), F32),
            jax.ShapeDtypeStruct((PAIRS, 2, seq), F32),
        ],
        input_output_aliases={4 + i: i for i in range(len(before))},
        compiler_params=pltpu.CompilerParams(vmem_limit_bytes=VMEM),
        cost_estimate=cost(4 * count),
        name="attend",
    )(lengths, packed, packed, packed, *extra)


def attend_back_kernel(
    block, len_ref, q_ref, k_ref, v_ref, do_ref, ctxt_ref, lse_ref, out_ref, sum_ref, dqt_ref
):
    seq = q_ref.shape[0]
    q = q_ref[...].astype(F32) * 0.125
    qt = q.T.astype(BF16)
    q = q.astype(BF16)
    do = do_ref[...]
    dof = do.astype(F32).T
    dot_ = dof.astype(BF16)
    prod = dof * ctxt_ref[...]
    kt = k_ref[...].astype(F32).T.astype(BF16)
    row = lax.broadcasted_iota(jnp.int32, (HEAD_DIM, seq), 0)

    def pieces(vec):
        high = vec.astype(BF16).astype(F32)
        mid = (vec - high).astype(BF16).astype(F32)
        low = vec - high - mid
        picked = jnp.where(row == 1, mid, jnp.where(row == 2, low, 0.0))
        return jnp.where(row == 0, high, picked).astype(BF16)

    q_aug, do_aug, fill = [], [], []
    for h in range(2):
        rows = slice(h * HEAD_DIM, (h + 1) * HEAD_DIM)
        lse = lse_ref[0, h : h + 1]
        delta = jnp.sum(prod[rows], axis=0, keepdims=True)
        q_parts = [qt[rows], pieces(-lse)]
        do_parts = [dot_[rows], pieces(-delta)]
        q_aug.append(jnp.concatenate(q_parts if h == 0 else q_parts[::-1], axis=0))
        do_aug.append(jnp.concatenate(do_parts if h == 0 else do_parts[::-1], axis=0))
        fill.append(MASKED - lse)
    lane = lax.broadcasted_iota(jnp.int32, (block, WIDE), 1)
    mine = (lane < HEAD_DIM, lane >= HEAD_DIM)
    one = (
        jnp.where(lane < HEAD_DIM + 3, 1.0, 0.0).astype(BF16),
        jnp.where(lane < 3, 1.0, 0.0).astype(BF16),
    )
    for j in range(seq // block):
        rows = slice(j * block, (j + 1) * block)
        keep = lax.broadcasted_iota(jnp.int32, (block, seq), 0) + j * block < len_ref[0]
        k, v = k_ref[rows, :], v_ref[rows, :]
        dv, dk = [], []
        for h in range(2):
            heads = slice(h * HEAD_DIM, (h + 1) * HEAD_DIM)
            k_aug, v_aug = jnp.where(mine[h], k, one[h]), jnp.where(mine[h], v, one[h])
            prob = jnp.exp(jnp.where(keep, dot(k_aug, q_aug[h]), fill[h]))
            dscore = (prob * dot(v_aug, do_aug[h])).astype(BF16)
            dv.append(dot(prob.astype(BF16), do))
            dk.append(dot(dscore, q))
            dq = dot(kt[heads, rows], dscore)
            if j == 0:
                dqt_ref[heads, :] = dq
            else:
                dqt_ref[heads, :] += dq
        out_ref[1, rows, :] = jnp.where(mine[0], dk[0], dk[1]).astype(BF16)
        out_ref[2, rows, :] = jnp.where(mine[0], dv[0], dv[1]).astype(BF16)
    out_ref[0] = (dqt_ref[...] * 0.125).T.astype(BF16)
    sum_ref[0, 0:1] = jnp.sum(out_ref[0].astype(F32), axis=0, keepdims=True)
    sum_ref[0, 1:2] = jnp.sum(out_ref[2].astype(F32), axis=0, keepdims=True)


def attend_back(lengths, packed, dctx, ctxt, lse, first, count, before=None, waits=()):
    seq = packed.shape[0]
    extra = tuple(waits) if before is None else (before, *waits)
    return pl.pallas_call(
        after(partial(attend_back_kernel, min(512, seq)), 7, len(extra)),
        grid_spec=pltpu.PrefetchScalarGridSpec(
            num_scalar_prefetch=1,
            grid=(count,),
            in_specs=[
                pl.BlockSpec((seq, WIDE), lambda p, _, i=i: (0, i * PAIRS + first + p))
                for i in range(3)
            ]
            + [
                pl.BlockSpec((seq, WIDE), lambda p, _: (0, first + p)),
                pl.BlockSpec((WIDE, seq), lambda p, _: (first + p, 0)),
                pl.BlockSpec((1, 2, seq), lambda p, _: (first + p, 0, 0)),
            ]
            + untouched(extra),
            out_specs=[
                pl.BlockSpec((3, seq, WIDE), lambda p, _: (0, 0, first + p)),
                pl.BlockSpec((1, 2, WIDE), lambda p, _: (p, 0, 0)),
            ],
            scratch_shapes=[pltpu.VMEM((WIDE, seq), F32)],
        ),
        out_shape=[
            jax.ShapeDtypeStruct((3, seq, D), BF16),
            jax.ShapeDtypeStruct((count, 2, WIDE), F32),
        ],
        input_output_aliases={} if before is None else {7: 0},
        compiler_params=pltpu.CompilerParams(vmem_limit_bytes=VMEM),
        cost_estimate=cost(6 * count),
        name="attend_back",
    )(lengths, packed, packed, packed, dctx, ctxt, lse, *extra)


def normal_parts(u):
    return 0.5 + 0.5 * lax.erf(u * 0.7071067811865476), jnp.exp(-0.5 * u * u)


def norm_forward(resid):
    center = resid - jnp.mean(resid, axis=-1, keepdims=True)
    inverse = lax.rsqrt(jnp.mean(center * center, axis=-1, keepdims=True) + 1e-05)
    return center * inverse, inverse


def norm_back(grad, gain, unit, inverse):
    du = grad * gain
    mean = jnp.mean(du, axis=-1, keepdims=True)
    return inverse * (du - mean - unit * jnp.mean(du * unit, axis=-1, keepdims=True))


def column_sum(value):
    return jnp.sum(value.astype(F32), axis=0, keepdims=True)


def waited(copies):
    for copy in copies:
        copy.wait()


def feed_kernel(pieces, steps, *refs):
    len_ref, place_ref, where_ref, x_ref, ctx_ref, cot_ref, vec_ref, to_a_ref, to_b_ref = refs[:9]
    attn_in_ref, parts, refs = refs[9], refs[10 : 10 + len(pieces)], refs[10 + len(pieces) :]
    mixed_ref, dres1_ref, dctx_ref, sum_ref, *grads = refs[:10]
    out_grads, in_grads, attn_grads = grads[:2], grads[2:4], grads[4:6]
    w_ref, w2_ref, act_ref, dhid_ref, first_ref, ctxb_ref, dbr_ref, dres_ref = refs[10:18]
    unit_ref, inverse_ref, slope_ref, held_ref, in_sems, part_sems, out_sems = refs[18:]
    step = pl.program_id(0)
    size = x_ref.shape[0]
    blocks = where_ref.shape[0] // CHUNKS
    first_grad, second_grad = steps, steps + CHUNKS
    back, last = steps + 2 * CHUNKS, 2 * steps + 2 * CHUNKS

    def vec(i):
        return vec_ref[i : i + 1, :]

    def weight(c):
        cols = slice(c * D, (c + 1) * D)
        return w_ref.at[:, cols]

    def load(c):
        cols = slice(c * D, (c + 1) * D)
        return pltpu.make_async_copy(attn_in_ref.at[:, cols], weight(c), in_sems.at[c])

    def part_copies():
        made = []
        for part, (first, count, column) in zip(parts, pieces):
            rows, width = part.shape[0] // count, part.shape[1]
            for i in range(count):
                where = pl.multiple_of(place_ref[first + i] * rows, rows)
                target = w2_ref.at[pl.ds(where, rows), pl.ds(column, width)]
                source = part.at[pl.ds(i * rows, rows), :]
                made.append(pltpu.make_async_copy(source, target, part_sems.at[len(made)]))
        return made

    @pl.when(step == 0)
    def _():
        for c in range(1 + CHUNKS):
            load(c).start()
        for copy in part_copies():
            copy.start()
        sum_ref[...] = jnp.zeros_like(sum_ref)

    @pl.when(step < steps)
    def _():
        rows = pl.ds(pl.multiple_of(step * size, size), size)

        def arrived(c):
            @pl.when(step == 0)
            def _():
                load(c).wait()

        arrived(0)
        resid = x_ref[...].astype(F32) + (dot(ctx_ref[...], weight(0)[...]) + vec(2))
        unit1, inverse1 = norm_forward(resid)
        unit_ref[rows, :] = unit1
        inverse_ref[rows, :] = jnp.broadcast_to(inverse1, (size, 128))
        first = unit1 * vec(3) + vec(4)
        first_b = first.astype(BF16)
        first_ref[rows, :] = arrange(first_b, to_a_ref[...])
        ctxb_ref[rows, :] = arrange(ctx_ref[...], to_b_ref[...])
        for c in range(CHUNKS):
            arrived(1 + c)
        @pl.when(step == 0)
        def _():
            waited(part_copies())

        branch = None
        for c in range(CHUNKS):
            cols = slice(c * D, (c + 1) * D)
            hidden = dot(first_b, weight(1 + c)[...]) + vec(5 + c)
            phi, bell = normal_parts(hidden)
            active = (hidden * phi).astype(BF16)
            act_ref[rows, cols] = active
            slope_ref[:, cols] = phi + hidden * bell * 0.3989422804014327
            part = dot(active, w2_ref[cols, :])
            branch = part if branch is None else branch + part
        unit2, inverse2 = norm_forward(first + (branch + vec(9)))
        place = lax.broadcasted_iota(jnp.int32, (size, 1), 0) + step * size
        keep = (place < len_ref[0]).astype(F32)
        mixed_ref[...] = ((unit2 * vec(10) + vec(11)) * keep).astype(BF16)
        dz = cot_ref[...].astype(F32) * keep
        dres2 = norm_back(dz, vec(10), unit2, inverse2)
        dres_ref[rows, :] = dres2
        dbranch = dres2.astype(BF16)
        dbr_ref[rows, :] = dbranch
        sum_ref[9:10, :] += column_sum(dbranch)
        sum_ref[10:11, :] += column_sum(dz * unit2)
        sum_ref[11:12, :] += column_sum(dz)
        for c in range(CHUNKS):
            cols = slice(c * D, (c + 1) * D)
            dhidden = (dot_nt(dbranch, w2_ref[cols, :]) * slope_ref[:, cols]).astype(BF16)
            dhid_ref[rows, cols] = dhidden
            sum_ref[5 + c : 6 + c, :] += column_sum(dhidden)

    def out_copies(step, go):
        chunk = step - first_grad
        slot = lax.rem(chunk, 2)
        rows = D // blocks
        for i in range(blocks):
            place = where_ref[chunk * blocks + i]
            source = held_ref.at[slot, pl.ds(i * rows, rows), :]
            for half in range(2):
                where = pl.multiple_of((place - half * 2 * blocks) * rows, rows)

                @pl.when((place >= 2 * blocks) == (half == 1))
                def _(half=half, where=where, source=source, i=i):
                    target = out_grads[half].at[pl.ds(where, rows), :]
                    go(pltpu.make_async_copy(source, target, out_sems.at[slot, i]))

    def in_copies(step, grads, column):
        slot = lax.rem(step - first_grad, 2)
        made = []
        for half in range(2):
            source = held_ref.at[slot, pl.ds(half * D // 2, D // 2), :]
            target = grads[half].at[:, pl.ds(column, D)]
            made.append(pltpu.make_async_copy(source, target, out_sems.at[slot, half]))
        return made

    def in_column(step):
        return pl.multiple_of((step - second_grad) * D, D)

    def start(copy):
        copy.start()

    def wait(copy):
        copy.wait()

    @pl.when((step >= first_grad) & (step < second_grad))
    def _():
        @pl.when(step >= first_grad + 2)
        def _():
            out_copies(step - 2, wait)

        cols = pl.ds(pl.multiple_of((step - first_grad) * D, D), D)
        grad = dot_tn(act_ref[:, cols], dbr_ref[...]).astype(BF16)
        held_ref[lax.rem(step - first_grad, 2)] = grad
        out_copies(step, start)

    @pl.when((step >= second_grad) & (step < back))
    def _():
        @pl.when(step < second_grad + 2)
        def _():
            out_copies(step - 2, wait)

        @pl.when(step >= second_grad + 2)
        def _():
            waited(in_copies(step - 2, in_grads, in_column(step - 2)))

        cols = pl.ds(in_column(step), D)
        grad = dot_tn(first_ref[...], dhid_ref[:, cols]).astype(BF16)
        held_ref[lax.rem(step - first_grad, 2)] = grad
        for copy in in_copies(step, in_grads, in_column(step)):
            copy.start()

    @pl.when((step >= back) & (step < last))
    def _():
        rows = pl.ds(pl.multiple_of((step - back) * size, size), size)
        dfirst = dres_ref[rows, :]
        for c in range(CHUNKS):
            dfirst = dfirst + dot_nt(dhid_ref[rows, c * D : (c + 1) * D], weight(1 + c)[...])
        unit = unit_ref[rows, :]
        dres1 = norm_back(dfirst, vec(3), unit, inverse_ref[rows, 0:1])
        dres1_ref[...] = dres1
        dattend = dres1.astype(BF16)
        dbr_ref[rows, :] = dattend
        dctx_ref[...] = dot_nt(dattend, weight(0)[...]).astype(BF16)
        sum_ref[2:3, :] += column_sum(dattend)
        sum_ref[3:4, :] += column_sum(dfirst * unit)
        sum_ref[4:5, :] += column_sum(dfirst)

    @pl.when(step == last)
    def _():
        waited(in_copies(back - 2, in_grads, in_column(back - 2)))
        waited(in_copies(back - 1, in_grads, in_column(back - 1)))
        held_ref[0] = dot_tn(ctxb_ref[...], dbr_ref[...]).astype(BF16)
        copies = in_copies(first_grad, attn_grads, 0)
        for copy in copies:
            copy.start()
        waited(copies)


def feed(lengths, x, ctx, cot, attn_in, vec, to_a, to_b, places, parts, pieces, where):
    seq = x.shape[0]
    size = min(256, seq)
    steps = seq // size
    back = steps + 2 * CHUNKS
    anywhere = pl.BlockSpec(memory_space=pl.ANY)

    def early(width):
        return pl.BlockSpec((size, width), lambda i, *_: (jnp.minimum(i, steps - 1), 0))

    def late(width):
        return pl.BlockSpec((size, width), lambda i, *_: (jnp.clip(i - back, 0, steps - 1), 0))

    def fixed(shape):
        return pl.BlockSpec(shape, lambda i, *_: (0, 0), pipeline_mode=pl.Buffered(1))

    shape = jax.ShapeDtypeStruct
    return pl.pallas_call(
        partial(feed_kernel, pieces, steps),
        grid_spec=pltpu.PrefetchScalarGridSpec(
            num_scalar_prefetch=3,
            grid=(2 * steps + 2 * CHUNKS + 1,),
            in_specs=[early(D)] * 3
            + [fixed((12, D)), fixed((D, D)), fixed((D, D))]
            + [anywhere] * (1 + len(parts)),
            out_specs=[early(D), late(D), late(D), pl.BlockSpec((12, D), lambda i, *_: (0, 0))]
            + [anywhere] * 6,
            scratch_shapes=[
                pltpu.VMEM((D, D + FF), BF16),
                pltpu.VMEM((FF, D), BF16),
                pltpu.VMEM((seq, FF), BF16),
                pltpu.VMEM((seq, FF), BF16),
                pltpu.VMEM((seq, D), BF16),
                pltpu.VMEM((seq, D), BF16),
                pltpu.VMEM((seq, D), BF16),
                pltpu.VMEM((seq, D), F32),
                pltpu.VMEM((seq, D), F32),
                pltpu.VMEM((seq, 128), F32),
                pltpu.VMEM((size, FF), F32),
                pltpu.VMEM((2, D, D), BF16),
                pltpu.SemaphoreType.DMA((1 + CHUNKS,)),
                pltpu.SemaphoreType.DMA((sum(count for _, count, _ in pieces),)),
                pltpu.SemaphoreType.DMA((2, max(2, where.shape[0] // CHUNKS))),
            ],
        ),
        out_shape=[
            shape((seq, D), BF16),
            shape((seq, D), F32),
            shape((seq, D), BF16),
            shape((12, D), F32),
        ]
        + [shape((FF // 2, D), BF16)] * 2
        + [shape((D // 2, FF), BF16)] * 2
        + [shape((D // 2, D), BF16)] * 2,
        compiler_params=pltpu.CompilerParams(vmem_limit_bytes=VMEM),
        cost_estimate=cost(50),
        name="feed",
    )(lengths, places, where, x, ctx, cot, vec, to_a, to_b, attn_in, *parts)


def swap(value, bit, n):
    return lax.ppermute(value, "dp", [(i, i ^ (1 << bit)) for i in range(n)])


def sum_all(value, n):
    for bit in range(n.bit_length() - 1):
        value = value + swap(value, bit, n)
    return value


def own_bit(bit):
    return (lax.axis_index("dp") >> bit) & 1


def phase(*values):
    return lax.optimization_barrier(values)


class Order:
    def __init__(self, bits):
        self.bits, self.n = bits, 2 ** len(bits)

    def mask(self, place):
        return sum(((place >> k) & 1) << bit for k, bit in enumerate(self.bits))

    def matrix(self):
        rows = D // self.n
        place = jnp.arange(D, dtype=jnp.int32)
        block = self.mask(place // rows) ^ lax.axis_index("dp")
        source = block * rows + place % rows
        return (place[:, None] == source[None, :]).astype(BF16)

    def where(self):
        other = jnp.arange(self.n, dtype=jnp.int32) ^ lax.axis_index("dp")
        return sum(((other >> bit) & 1) << k for k, bit in enumerate(self.bits))

    def places(self, count):
        return self.mask(jnp.arange(count, dtype=jnp.int32)) ^ lax.axis_index("dp")


class Gather:
    def __init__(self, shard, n):
        self.value, self.n = shard, n

    def step(self, bit):
        self.value = jnp.concatenate([self.value, swap(self.value, bit, self.n)], axis=0)

    def cut(self, start, stop):
        return Gather(self.value[:, start:stop], self.n)


class Scatter:
    def __init__(self, kept, away, bit, n):
        self.terms, self.n = [kept, swap(away, bit, n)], n

    def step(self, bit):
        half = self.terms[0].shape[0] // 2
        away = self.total([t[half:] for t in self.terms]).astype(BF16)
        self.terms = [t[:half] for t in self.terms] + [swap(away, bit, self.n)]

    def total(self, parts=None):
        parts = self.terms if parts is None else parts
        result = parts[0].astype(F32)
        for part in parts[1:]:
            result = result + part.astype(F32)
        return result

    def join(self, other):
        self.terms = [jnp.concatenate([self.total(), other.total()], axis=1)]
        return self


def adapt(weight, grad, moment, square, decay):
    new_moment = 0.9 * moment + 0.1 * grad
    new_square = 0.999 * square + 0.001 * grad * grad
    update = new_moment / (1.0 - 0.9**STEP) / (jnp.sqrt(new_square / (1.0 - 0.999**STEP)) + 1e-06)
    return (new_moment, new_square, update + decay * weight)


def lane_sums(value):
    columns = jnp.sum(value * value, axis=0, keepdims=True)
    result = columns[:, :128]
    for start in range(128, value.shape[1], 128):
        result = result + columns[:, start : start + 128]
    return result


def adapt_kernel(first, *refs):
    before_ref, sums_ref = refs[8], refs[15]
    sums = before_ref[...]
    row = lax.broadcasted_iota(jnp.int32, sums.shape, 0)
    for i in range(2):
        weight_ref, grad_ref, moment_ref, square_ref = refs[i * 4 : i * 4 + 4]
        outs = refs[9 + i * 3 : 12 + i * 3]
        weight = weight_ref[...]
        values = adapt(weight, grad_ref[...], moment_ref[...], square_ref[...], 0.01)
        for out, value in zip(outs, values):
            out[...] = value
        sums = jnp.where(row == first + i, lane_sums(weight), sums)
        sums = jnp.where(row == 4 + first + i, lane_sums(values[2]), sums)
    sums_ref[...] = sums


def adapt_two(first, before, *operands):
    shapes = [jax.ShapeDtypeStruct(operands[i * 4].shape, F32) for i in (0, 0, 0, 1, 1, 1)]
    return pl.pallas_call(
        partial(adapt_kernel, first),
        out_shape=shapes + [jax.ShapeDtypeStruct((8, 128), F32)],
        compiler_params=pltpu.CompilerParams(vmem_limit_bytes=VMEM),
        cost_estimate=cost(2),
        name="adapt",
    )(*operands, before)


def renew_kernel(sums_ref, *refs):
    norms = jnp.sqrt(jnp.sum(sums_ref[...], axis=1, keepdims=True))
    refs[12][...] = jnp.broadcast_to(norms, (8, 128))
    for i in range(4):
        rate = 0.25 * (norms[i : i + 1] / norms[4 + i : 5 + i])
        refs[8 + i][...] = refs[i][...] - rate * refs[4 + i][...]


def renew(sums, weights, updates):
    return pl.pallas_call(
        renew_kernel,
        out_shape=[jax.ShapeDtypeStruct(weight.shape, F32) for weight in weights]
        + [jax.ShapeDtypeStruct((8, 128), F32)],
        compiler_params=pltpu.CompilerParams(vmem_limit_bytes=VMEM),
        cost_estimate=cost(2),
        name="renew",
    )(sums, *weights, *updates)


def body(
    n,
    frames,
    cotangent,
    lengths,
    w_qkv,
    w_attn,
    w_in,
    w_out,
    vectors,
    moment_qkv,
    moment_attn,
    moment_in,
    moment_out,
    moment_vec,
    square_qkv,
    square_attn,
    square_in,
    square_out,
    square_vec,
):
    rows_d, rows_f, width = w_qkv.shape[0], w_out.shape[0], vectors.shape[0]
    core, one, two, *others = range(n.bit_length() - 1)
    far = others[::-1]
    order_a, order_b = Order(far + [two, one, core]), Order(far + [one, two, core])
    x = frames[0]

    half = w_qkv.shape[1] // 2
    tail = jnp.pad(vectors.reshape(rows_d, 12), ((0, 0), (0, 116)))
    low_qkv = jnp.concatenate([w_qkv, tail], axis=1).astype(BF16)
    low_qkv, w_first, w_second, w_third = phase(low_qkv, w_attn, w_in, w_out)
    attn_in = jnp.concatenate([w_first, w_second], axis=1).astype(BF16)
    attn_in = lax.all_gather(attn_in, "dp", axis=0, tiled=True)
    qkv, out = Gather(low_qkv, n), Gather(w_third.astype(BF16), n)
    to_a, to_b = order_a.matrix(), order_b.matrix()
    x_a, x_b = arrange(x, to_a), arrange(x, to_b)
    for bit in far:
        qkv.step(bit)
        qkv.value, out.value, x_a, x_b = phase(qkv.value, out.value, x_a, x_b)
        out.step(bit)
    left, right = qkv.cut(0, half), qkv.cut(half, 2 * half + 128)
    for bits in ((two, one), (one, two)):
        left.step(bits[0])
        right.step(bits[1])
        left.value, right.value, out.value = phase(left.value, right.value, out.value)
    left = (left.value, swap(left.value, core, n))
    right = (right.value, swap(right.value, core, n))
    left, right, out.value = phase(left, right, out.value)
    vec_rows = jnp.concatenate([part[:, half:] for part in right], axis=0)
    vec = dot(to_b, vec_rows)[:, :12].reshape(12, D)
    bias_qkv = jnp.concatenate([vec[:1], jnp.zeros((1, D), F32), vec[1:2]], axis=1)

    out_left, out_right = out.cut(0, D // 2), out.cut(D // 2, D)
    out_left.step(two)
    out_right.step(one)
    packed = project(x_a, x_b, left, right, bias_qkv)
    some = PAIRS // 2
    heads = attend(lengths, packed, 0, some)
    heads, out_left.value, out_right.value, attn_in = phase(
        heads, out_left.value, out_right.value, attn_in
    )
    out_left.step(one)
    out_right.step(two)
    heads = attend(lengths, packed, some, some, heads)
    heads, out_left.value, out_right.value = phase(heads, out_left.value, out_right.value)
    parts = [out_left.value, swap(out_left.value, core, n)]
    parts += [out_right.value, swap(out_right.value, core, n)]
    if rows_f % 16 == 0:
        places = jnp.concatenate([order_a.places(n), order_b.places(n)])
        pieces = tuple((i * n // 2, n // 2, i // 2 * (D // 2)) for i in range(4))
    else:
        sides = []
        for i, order in ((0, order_a), (2, order_b)):
            side = jnp.concatenate(parts[i : i + 2], axis=0).reshape(n, rows_f, D // 2)
            sides.append(side[jnp.argsort(order.places(n))].reshape(FF, D // 2))
        parts = [jnp.concatenate(sides, axis=1)]
        places, pieces = jnp.zeros((1,), jnp.int32), ((0, 1, 0),)
    ctx, ctxt, lse = heads

    aligned = rows_f % 16 == 0
    where = order_b.where() if aligned else jnp.arange(CHUNKS, dtype=jnp.int32)
    mixed, dres1, dctx, sums, *grads = feed(
        lengths, x, ctx, cotangent[0], attn_in, vec, to_a, to_b, places, parts, pieces, where
    )
    if not aligned:
        grad = jnp.concatenate(grads[:2], axis=0).reshape(n, rows_f, D)
        grads[:2] = jnp.split(grad[order_b.places(n)].reshape(FF, D), 2)
    sum_out = Scatter(*grads[:2], core, n)
    sum_in = Scatter(*grads[2:4], core, n)

    dqkv, biases = None, []
    for first, count, bits in ((0, 1, (one, two)), (1, 4, (two, one)), (5, 1, None)):
        dqkv, bias = attend_back(lengths, packed, dctx, ctxt, lse, first, count, dqkv)
        biases.append(bias)
        if bits is not None:
            sum_in.terms[-1], sum_out.terms[-1], dqkv = phase(
                sum_in.terms[-1], sum_out.terms[-1], dqkv
            )
            sum_in.step(bits[0])
            sum_out.step(bits[1])
    dqkv, sum_in.terms[-1], sum_out.terms[-1] = phase(
        dqkv, sum_in.terms[-1], sum_out.terms[-1]
    )

    def late_grads(side):
        cols = slice(side * D // 2, (side + 1) * D // 2)
        queries, keys = [dot_tn(x_a[:, cols], dqkv[i]).astype(BF16) for i in range(2)]
        values = dot_tn(x_b[:, cols], dqkv[2]).astype(BF16)
        return (
            jnp.concatenate([queries, keys], axis=1),
            jnp.concatenate([values, grads[4 + side]], axis=1),
        )

    away_a, away_b = late_grads(1)
    away_a, away_b, dqkv = phase(away_a, away_b, dqkv)
    kept_a, kept_b = late_grads(0)
    late_a, late_b = Scatter(kept_a, away_a, core, n), Scatter(kept_b, away_b, core, n)
    sum_in.step(others[0])
    sum_out.step(others[0])
    late_a.terms, late_b.terms, sum_in.terms[-1], sum_out.terms[-1] = phase(
        late_a.terms, late_b.terms, sum_in.terms[-1], sum_out.terms[-1]
    )
    late_a.step(one)
    late_b.step(two)
    for bit in others[1:]:
        sum_in.step(bit)
        sum_out.step(bit)
    late_a.terms[-1], late_b.terms[-1], sum_in.terms[-1], sum_out.terms[-1] = phase(
        late_a.terms[-1], late_b.terms[-1], sum_in.terms[-1], sum_out.terms[-1]
    )
    late_a.step(two)
    late_b.step(one)
    late_a.terms[-1], late_b.terms[-1] = phase(late_a.terms[-1], late_b.terms[-1])
    share_in, share_out = sum_in.total(), sum_out.total()
    late = late_a.join(late_b)
    for bit in others:
        late.step(bit)
    share_late = late.total()
    bias_sums = jnp.concatenate(biases, axis=0)
    grad_vec = jnp.concatenate(
        [bias_sums[:, 0].reshape(1, D), bias_sums[:, 1].reshape(1, D), sums[2:]]
    ).reshape(-1, 128)
    full_qkv = jnp.concatenate(
        [
            arrange(to_a, jnp.concatenate(left, axis=0)),
            arrange(to_b, jnp.concatenate([part[:, :half] for part in right], axis=0)),
        ],
        axis=1,
    )
    input_grad = dres1
    for i in range(3):
        input_grad = input_grad + dot_nt(dqkv[i], full_qkv[:, i * D : (i + 1) * D])

    next_in = adapt_two(
        2,
        jnp.zeros((8, 128), F32),
        *(w_in, share_in, moment_in, square_in),
        *(w_out, share_out, moment_out, square_out),
    )
    next_attn = adapt_two(
        0,
        next_in[6],
        *(w_qkv, share_late[:, : 3 * D], moment_qkv, square_qkv),
        *(w_attn, share_late[:, 3 * D :], moment_attn, square_attn),
    )
    reduced = sum_all(jnp.concatenate([next_attn[6], grad_vec], axis=0), n)
    place = lax.axis_index("dp") * width
    share_vec = lax.dynamic_slice_in_dim(reduced[8:].reshape(-1), place, width, 0)
    updates = (next_attn[2], next_attn[5], next_in[2], next_in[5])
    *new_weights, norms = renew(reduced[:8], (w_qkv, w_attn, w_in, w_out), updates)
    vec_moment, vec_square, vec_update = adapt(vectors, share_vec, moment_vec, square_vec, 0.0)
    return (
        mixed[None],
        input_grad[None],
        *new_weights,
        vectors - 0.4 * vec_update,
        *(next_attn[0], next_attn[3], next_in[0], next_in[3], vec_moment),
        *(next_attn[1], next_attn[4], next_in[1], next_in[4], vec_square),
        norms[:, 0],
    )


def solution(mesh):
    clips, matrix, vector = P("dp", None, None), P("dp", None), P("dp")
    parameters = (matrix,) * 4 + (vector,)
    return jax.shard_map(
        partial(body, mesh.shape["dp"]),
        mesh=mesh,
        in_specs=(clips, clips, vector) + parameters * 3,
        out_specs=(clips, clips) + parameters * 3 + (P(),),
        check_vma=False,
    )
```

```python
from functools import partial

import jax
import jax.numpy as jnp
from jax import lax
from jax.experimental import pallas as pl
from jax.experimental.pallas import tpu as pltpu
from jax.sharding import PartitionSpec as P

D = 768
FF = 3072
HEADS = 12
HEAD_DIM = 64
PAIRS = HEADS // 2
WIDE = 2 * HEAD_DIM
CHUNKS = FF // D
STEP = 10
MASKED = -1e9
VMEM = 60 * 2**20
ROOM = 24 * 2**20
BF16 = jnp.bfloat16
F32 = jnp.float32


def dot(a, b):
    return jnp.dot(a, b, preferred_element_type=F32)


def dot_nt(a, b):
    return lax.dot_general(a, b, (((1,), (1,)), ((), ())), preferred_element_type=F32)


def dot_tn(a, b):
    return lax.dot_general(a, b, (((0,), (0,)), ((), ())), preferred_element_type=F32)


def cost(us):
    return pl.CostEstimate(flops=int(us * 5.0e7), bytes_accessed=0, transcendentals=0)


def arrange(value, matrix):
    return dot(value, matrix).astype(BF16)


def project_kernel(xa_ref, xb_ref, la_ref, lb_ref, ra_ref, rb_ref, bias_ref, out_ref):
    width = la_ref.shape[1]
    left = jnp.concatenate([la_ref[...], lb_ref[...]], axis=0)
    out_ref[:, :width] = (dot(xa_ref[...], left) + bias_ref[:, :width]).astype(BF16)
    right = jnp.concatenate([ra_ref[:, :width], rb_ref[:, :width]], axis=0)
    out_ref[:, width:] = (dot(xb_ref[...], right) + bias_ref[:, width:]).astype(BF16)


def project(x_a, x_b, left, right, bias):
    seq = x_a.shape[0]
    rows = min(512, seq)

    def fixed(shape):
        return pl.BlockSpec(shape, lambda i: (0, 0), pipeline_mode=pl.Buffered(1))

    return pl.pallas_call(
        project_kernel,
        grid=(seq // rows,),
        in_specs=[pl.BlockSpec((rows, D), lambda i: (i, 0))] * 2
        + [fixed(part.shape) for part in (*left, *right, bias)],
        out_specs=pl.BlockSpec((rows, 3 * D), lambda i: (i, 0)),
        out_shape=jax.ShapeDtypeStruct((seq, 3 * D), BF16),
        compiler_params=pltpu.CompilerParams(vmem_limit_bytes=ROOM),
        cost_estimate=cost(5),
        name="project",
    )(x_a, x_b, *left, *right, bias)


def attend_kernel(len_ref, q_ref, k_ref, v_ref, ctx_ref, ctxt_ref, lse_ref):
    seq = q_ref.shape[0]
    qt = (q_ref[...].astype(F32) * 0.125).T.astype(BF16)
    vt = v_ref[...].astype(F32).T.astype(BF16)
    k = k_ref[...]
    keep = lax.broadcasted_iota(jnp.int32, (seq, seq), 0) < len_ref[0]
    zero = jnp.zeros((HEAD_DIM, seq), BF16)
    ones = jnp.ones((16, seq), BF16)
    for h in range(2):
        rows = slice(h * HEAD_DIM, (h + 1) * HEAD_DIM)
        q = jnp.concatenate([qt[rows], zero] if h == 0 else [zero, qt[rows]], axis=0)
        scores = jnp.where(keep, dot(k, q), MASKED)
        peak = jnp.max(scores, axis=0, keepdims=True)
        expo = jnp.exp(scores - peak).astype(BF16)
        both = dot(jnp.concatenate([vt[rows], ones], axis=0), expo)
        total = both[HEAD_DIM : HEAD_DIM + 1]
        ctxt_ref[rows, :] = both[:HEAD_DIM] / total
        lse_ref[0, h : h + 1, :] = peak + jnp.log(total)
    ctx_ref[...] = ctxt_ref[...].T.astype(BF16)


def after(kernel, first, count):
    def call(*refs):
        kernel(*refs[:first], *refs[first + count :])

    return call


def untouched(values):
    return [pl.BlockSpec(memory_space=pl.ANY)] * len(values)


def attend(lengths, packed, first, count, before=(), waits=()):
    seq = packed.shape[0]
    extra = (*before, *waits)
    return pl.pallas_call(
        after(attend_kernel, 4, len(extra)),
        grid_spec=pltpu.PrefetchScalarGridSpec(
            num_scalar_prefetch=1,
            grid=(count,),
            in_specs=[
                pl.BlockSpec((seq, WIDE), lambda p, _, i=i: (0, i * PAIRS + first + p))
                for i in range(3)
            ]
            + untouched(extra),
            out_specs=[
                pl.BlockSpec((seq, WIDE), lambda p, _: (0, first + p)),
                pl.BlockSpec((WIDE, seq), lambda p, _: (first + p, 0)),
                pl.BlockSpec((1, 2, seq), lambda p, _: (first + p, 0, 0)),
            ],
        ),
        out_shape=[
            jax.ShapeDtypeStruct((seq, D), BF16),
            jax.ShapeDtypeStruct((D, seq), F32),
            jax.ShapeDtypeStruct((PAIRS, 2, seq), F32),
        ],
        input_output_aliases={4 + i: i for i in range(len(before))},
        compiler_params=pltpu.CompilerParams(vmem_limit_bytes=ROOM),
        cost_estimate=cost(4 * count),
        name="attend",
    )(lengths, packed, packed, packed, *extra)


def attend_back_kernel(
    block, len_ref, q_ref, k_ref, v_ref, do_ref, ctxt_ref, lse_ref, out_ref, sum_ref, dqt_ref
):
    seq = q_ref.shape[0]
    q = q_ref[...].astype(F32) * 0.125
    qt = q.T.astype(BF16)
    q = q.astype(BF16)
    do = do_ref[...]
    dof = do.astype(F32).T
    dot_ = dof.astype(BF16)
    prod = dof * ctxt_ref[...]
    kt = k_ref[...].astype(F32).T.astype(BF16)
    row = lax.broadcasted_iota(jnp.int32, (HEAD_DIM, seq), 0)

    def pieces(vec):
        high = vec.astype(BF16).astype(F32)
        mid = (vec - high).astype(BF16).astype(F32)
        low = vec - high - mid
        picked = jnp.where(row == 1, mid, jnp.where(row == 2, low, 0.0))
        return jnp.where(row == 0, high, picked).astype(BF16)

    q_aug, do_aug, fill = [], [], []
    for h in range(2):
        rows = slice(h * HEAD_DIM, (h + 1) * HEAD_DIM)
        lse = lse_ref[0, h : h + 1]
        delta = jnp.sum(prod[rows], axis=0, keepdims=True)
        q_parts = [qt[rows], pieces(-lse)]
        do_parts = [dot_[rows], pieces(-delta)]
        q_aug.append(jnp.concatenate(q_parts if h == 0 else q_parts[::-1], axis=0))
        do_aug.append(jnp.concatenate(do_parts if h == 0 else do_parts[::-1], axis=0))
        fill.append(MASKED - lse)
    lane = lax.broadcasted_iota(jnp.int32, (block, WIDE), 1)
    mine = (lane < HEAD_DIM, lane >= HEAD_DIM)
    one = (
        jnp.where(lane < HEAD_DIM + 3, 1.0, 0.0).astype(BF16),
        jnp.where(lane < 3, 1.0, 0.0).astype(BF16),
    )
    for j in range(seq // block):
        rows = slice(j * block, (j + 1) * block)
        keep = lax.broadcasted_iota(jnp.int32, (block, seq), 0) + j * block < len_ref[0]
        k, v = k_ref[rows, :], v_ref[rows, :]
        dv, dk = [], []
        for h in range(2):
            heads = slice(h * HEAD_DIM, (h + 1) * HEAD_DIM)
            k_aug, v_aug = jnp.where(mine[h], k, one[h]), jnp.where(mine[h], v, one[h])
            prob = jnp.exp(jnp.where(keep, dot(k_aug, q_aug[h]), fill[h]))
            dscore = (prob * dot(v_aug, do_aug[h])).astype(BF16)
            dv.append(dot(prob.astype(BF16), do))
            dk.append(dot(dscore, q))
            dq = dot(kt[heads, rows], dscore)
            if j == 0:
                dqt_ref[heads, :] = dq
            else:
                dqt_ref[heads, :] += dq
        out_ref[1, rows, :] = jnp.where(mine[0], dk[0], dk[1]).astype(BF16)
        out_ref[2, rows, :] = jnp.where(mine[0], dv[0], dv[1]).astype(BF16)
    out_ref[0] = (dqt_ref[...] * 0.125).T.astype(BF16)
    sum_ref[0, 0:1] = jnp.sum(out_ref[0].astype(F32), axis=0, keepdims=True)
    sum_ref[0, 1:2] = jnp.sum(out_ref[2].astype(F32), axis=0, keepdims=True)


def attend_back(lengths, packed, dctx, ctxt, lse, first, count, before=None, waits=()):
    seq = packed.shape[0]
    extra = tuple(waits) if before is None else (before, *waits)
    return pl.pallas_call(
        after(partial(attend_back_kernel, min(512, seq)), 7, len(extra)),
        grid_spec=pltpu.PrefetchScalarGridSpec(
            num_scalar_prefetch=1,
            grid=(count,),
            in_specs=[
                pl.BlockSpec((seq, WIDE), lambda p, _, i=i: (0, i * PAIRS + first + p))
                for i in range(3)
            ]
            + [
                pl.BlockSpec((seq, WIDE), lambda p, _: (0, first + p)),
                pl.BlockSpec((WIDE, seq), lambda p, _: (first + p, 0)),
                pl.BlockSpec((1, 2, seq), lambda p, _: (first + p, 0, 0)),
            ]
            + untouched(extra),
            out_specs=[
                pl.BlockSpec((3, seq, WIDE), lambda p, _: (0, 0, first + p)),
                pl.BlockSpec((1, 2, WIDE), lambda p, _: (p, 0, 0)),
            ],
            scratch_shapes=[pltpu.VMEM((WIDE, seq), F32)],
        ),
        out_shape=[
            jax.ShapeDtypeStruct((3, seq, D), BF16),
            jax.ShapeDtypeStruct((count, 2, WIDE), F32),
        ],
        input_output_aliases={} if before is None else {7: 0},
        compiler_params=pltpu.CompilerParams(vmem_limit_bytes=ROOM),
        cost_estimate=cost(6 * count),
        name="attend_back",
    )(lengths, packed, packed, packed, dctx, ctxt, lse, *extra)


def normal_parts(u):
    return 0.5 + 0.5 * lax.erf(u * 0.7071067811865476), jnp.exp(-0.5 * u * u)


def norm_forward(resid):
    center = resid - jnp.mean(resid, axis=-1, keepdims=True)
    inverse = lax.rsqrt(jnp.mean(center * center, axis=-1, keepdims=True) + 1e-05)
    return center * inverse, inverse


def norm_back(grad, gain, unit, inverse):
    du = grad * gain
    mean = jnp.mean(du, axis=-1, keepdims=True)
    return inverse * (du - mean - unit * jnp.mean(du * unit, axis=-1, keepdims=True))


def column_sum(value):
    return jnp.sum(value.astype(F32), axis=0, keepdims=True)


def waited(copies):
    for copy in copies:
        copy.wait()


def feed_kernel(in_pieces, out_pieces, steps, *refs):
    len_ref, place_ref, where_ref, x_ref, ctx_ref, cot_ref, vec_ref, to_a_ref, to_b_ref = refs[:9]
    in_parts, refs = refs[9 : 9 + len(in_pieces)], refs[9 + len(in_pieces) :]
    out_parts, refs = refs[: len(out_pieces)], refs[len(out_pieces) :]
    mixed_ref, dres1_ref, dctx_ref, sum_ref, *grads = refs[:10]
    out_grads, in_grads, attn_grads = grads[:2], grads[2:4], grads[4:6]
    w_ref, w2_ref, act_ref, dhid_ref, first_ref, ctxb_ref, dbr_ref, dres_ref = refs[10:18]
    unit_ref, inverse_ref, slope_ref, held_ref, in_sems, part_sems, out_sems = refs[18:]
    step = pl.program_id(0)
    size = x_ref.shape[0]
    blocks = where_ref.shape[0] // CHUNKS
    first_grad, second_grad = steps, steps + CHUNKS
    back, last = steps + 2 * CHUNKS, 2 * steps + 2 * CHUNKS

    def vec(i):
        return vec_ref[i : i + 1, :]

    def weight(c):
        return w_ref.at[:, c * D : (c + 1) * D]

    def part_copies(whole_ref, parts, pieces, sems):
        made, total = [], 0
        for part, (first, count, column) in zip(parts, pieces):
            rows, width = part.shape[0] // count, part.shape[1]
            columns = pl.ds(pl.multiple_of(place_ref[column] * 128, 128), width)
            for i in range(count):
                where = pl.multiple_of(place_ref[first + i] * rows, rows)
                target = whole_ref.at[pl.ds(where, rows), columns]
                source = part.at[pl.ds(i * rows, rows), :]
                made.append(pltpu.make_async_copy(source, target, sems.at[total]))
                total += 1
        return made

    def in_weights():
        return part_copies(w_ref, in_parts, in_pieces, in_sems)

    def out_weights():
        return part_copies(w2_ref, out_parts, out_pieces, part_sems)

    @pl.when(step == 0)
    def _():
        for copy in in_weights() + out_weights():
            copy.start()
        sum_ref[...] = jnp.zeros_like(sum_ref)

    @pl.when(step < steps)
    def _():
        rows = pl.ds(pl.multiple_of(step * size, size), size)

        @pl.when(step == 0)
        def _():
            waited(in_weights())

        resid = x_ref[...].astype(F32) + (dot(ctx_ref[...], weight(0)[...]) + vec(2))
        unit1, inverse1 = norm_forward(resid)
        unit_ref[rows, :] = unit1
        inverse_ref[rows, :] = jnp.broadcast_to(inverse1, (size, 128))
        first = unit1 * vec(3) + vec(4)
        first_b = first.astype(BF16)
        first_ref[rows, :] = arrange(first_b, to_a_ref[...])
        ctxb_ref[rows, :] = arrange(ctx_ref[...], to_b_ref[...])

        @pl.when(step == 0)
        def _():
            waited(out_weights())

        branch = None
        for c in range(CHUNKS):
            cols = slice(c * D, (c + 1) * D)
            hidden = dot(first_b, weight(1 + c)[...]) + vec(5 + c)
            phi, bell = normal_parts(hidden)
            active = (hidden * phi).astype(BF16)
            act_ref[rows, cols] = active
            slope_ref[:, cols] = phi + hidden * bell * 0.3989422804014327
            part = dot(active, w2_ref[cols, :])
            branch = part if branch is None else branch + part
        unit2, inverse2 = norm_forward(first + (branch + vec(9)))
        place = lax.broadcasted_iota(jnp.int32, (size, 1), 0) + step * size
        keep = (place < len_ref[0]).astype(F32)
        mixed_ref[...] = ((unit2 * vec(10) + vec(11)) * keep).astype(BF16)
        dz = cot_ref[...].astype(F32) * keep
        dres2 = norm_back(dz, vec(10), unit2, inverse2)
        dres_ref[rows, :] = dres2
        dbranch = dres2.astype(BF16)
        dbr_ref[rows, :] = dbranch
        sum_ref[9:10, :] += column_sum(dbranch)
        sum_ref[10:11, :] += column_sum(dz * unit2)
        sum_ref[11:12, :] += column_sum(dz)
        for c in range(CHUNKS):
            cols = slice(c * D, (c + 1) * D)
            dhidden = (dot_nt(dbranch, w2_ref[cols, :]) * slope_ref[:, cols]).astype(BF16)
            dhid_ref[rows, cols] = dhidden
            sum_ref[5 + c : 6 + c, :] += column_sum(dhidden)

    def out_copies(step, go):
        chunk = step - first_grad
        slot = lax.rem(chunk, 2)
        rows = D // blocks
        for i in range(blocks):
            place = where_ref[chunk * blocks + i]
            source = held_ref.at[slot, pl.ds(i * rows, rows), :]
            for half in range(2):
                where = pl.multiple_of((place - half * 2 * blocks) * rows, rows)

                @pl.when((place >= 2 * blocks) == (half == 1))
                def _(half=half, where=where, source=source, i=i):
                    target = out_grads[half].at[pl.ds(where, rows), :]
                    go(pltpu.make_async_copy(source, target, out_sems.at[slot, i]))

    def in_copies(step, grads, column):
        slot = lax.rem(step - first_grad, 2)
        made = []
        for half in range(2):
            source = held_ref.at[slot, pl.ds(half * D // 2, D // 2), :]
            target = grads[half].at[:, pl.ds(column, D)]
            made.append(pltpu.make_async_copy(source, target, out_sems.at[slot, half]))
        return made

    def in_column(step):
        return pl.multiple_of((step - second_grad) * D, D)

    def start(copy):
        copy.start()

    def wait(copy):
        copy.wait()

    @pl.when((step >= first_grad) & (step < second_grad))
    def _():
        @pl.when(step >= first_grad + 2)
        def _():
            out_copies(step - 2, wait)

        cols = pl.ds(pl.multiple_of((step - first_grad) * D, D), D)
        grad = dot_tn(act_ref[:, cols], dbr_ref[...]).astype(BF16)
        held_ref[lax.rem(step - first_grad, 2)] = grad
        out_copies(step, start)

    @pl.when((step >= second_grad) & (step < back))
    def _():
        @pl.when(step < second_grad + 2)
        def _():
            out_copies(step - 2, wait)

        @pl.when(step >= second_grad + 2)
        def _():
            waited(in_copies(step - 2, in_grads, in_column(step - 2)))

        cols = pl.ds(in_column(step), D)
        grad = dot_tn(first_ref[...], dhid_ref[:, cols]).astype(BF16)
        held_ref[lax.rem(step - first_grad, 2)] = grad
        for copy in in_copies(step, in_grads, in_column(step)):
            copy.start()

    @pl.when((step >= back) & (step < last))
    def _():
        rows = pl.ds(pl.multiple_of((step - back) * size, size), size)
        dfirst = dres_ref[rows, :]
        for c in range(CHUNKS):
            dfirst = dfirst + dot_nt(dhid_ref[rows, c * D : (c + 1) * D], weight(1 + c)[...])
        unit = unit_ref[rows, :]
        dres1 = norm_back(dfirst, vec(3), unit, inverse_ref[rows, 0:1])
        dres1_ref[...] = dres1
        dattend = dres1.astype(BF16)
        dbr_ref[rows, :] = dattend
        dctx_ref[...] = dot_nt(dattend, weight(0)[...]).astype(BF16)
        sum_ref[2:3, :] += column_sum(dattend)
        sum_ref[3:4, :] += column_sum(dfirst * unit)
        sum_ref[4:5, :] += column_sum(dfirst)

    @pl.when(step == last)
    def _():
        waited(in_copies(back - 2, in_grads, in_column(back - 2)))
        waited(in_copies(back - 1, in_grads, in_column(back - 1)))
        held_ref[0] = dot_tn(ctxb_ref[...], dbr_ref[...]).astype(BF16)
        copies = in_copies(first_grad, attn_grads, 0)
        for copy in copies:
            copy.start()
        waited(copies)


def feed(lengths, x, ctx, cot, vec, to_a, to_b, places, where, in_side, out_side):
    (in_parts, in_pieces), (out_parts, out_pieces) = in_side, out_side
    seq = x.shape[0]
    size = min(256, seq)
    steps = seq // size
    back = steps + 2 * CHUNKS
    anywhere = pl.BlockSpec(memory_space=pl.ANY)

    def early(width):
        return pl.BlockSpec((size, width), lambda i, *_: (jnp.minimum(i, steps - 1), 0))

    def late(width):
        return pl.BlockSpec((size, width), lambda i, *_: (jnp.clip(i - back, 0, steps - 1), 0))

    def fixed(shape):
        return pl.BlockSpec(shape, lambda i, *_: (0, 0), pipeline_mode=pl.Buffered(1))

    shape = jax.ShapeDtypeStruct
    return pl.pallas_call(
        partial(feed_kernel, in_pieces, out_pieces, steps),
        grid_spec=pltpu.PrefetchScalarGridSpec(
            num_scalar_prefetch=3,
            grid=(2 * steps + 2 * CHUNKS + 1,),
            in_specs=[early(D)] * 3
            + [fixed((12, D)), fixed((D, D)), fixed((D, D))]
            + untouched(in_parts)
            + untouched(out_parts),
            out_specs=[early(D), late(D), late(D), pl.BlockSpec((12, D), lambda i, *_: (0, 0))]
            + [anywhere] * 6,
            scratch_shapes=[
                pltpu.VMEM((D, D + FF), BF16),
                pltpu.VMEM((FF, D), BF16),
                pltpu.VMEM((seq, FF), BF16),
                pltpu.VMEM((seq, FF), BF16),
                pltpu.VMEM((seq, D), BF16),
                pltpu.VMEM((seq, D), BF16),
                pltpu.VMEM((seq, D), BF16),
                pltpu.VMEM((seq, D), F32),
                pltpu.VMEM((seq, D), F32),
                pltpu.VMEM((seq, 128), F32),
                pltpu.VMEM((size, FF), F32),
                pltpu.VMEM((2, D, D), BF16),
                pltpu.SemaphoreType.DMA((sum(count for _, count, _ in in_pieces),)),
                pltpu.SemaphoreType.DMA((sum(count for _, count, _ in out_pieces),)),
                pltpu.SemaphoreType.DMA((2, max(2, where.shape[0] // CHUNKS))),
            ],
        ),
        out_shape=[
            shape((seq, D), BF16),
            shape((seq, D), F32),
            shape((seq, D), BF16),
            shape((12, D), F32),
        ]
        + [shape((FF // 2, D), BF16)] * 2
        + [shape((D // 2, FF), BF16)] * 2
        + [shape((D // 2, D), BF16)] * 2,
        compiler_params=pltpu.CompilerParams(vmem_limit_bytes=VMEM),
        cost_estimate=cost(50),
        name="feed",
    )(lengths, places, where, x, ctx, cot, vec, to_a, to_b, *in_parts, *out_parts)


def swap(value, bit, n):
    return lax.ppermute(value, "dp", [(i, i ^ (1 << bit)) for i in range(n)])


def sum_all(value, n):
    for bit in range(n.bit_length() - 1):
        value = value + swap(value, bit, n)
    return value


def own_bit(bit):
    return (lax.axis_index("dp") >> bit) & 1


def phase(*values):
    return lax.optimization_barrier(values)


class Order:
    def __init__(self, bits):
        self.bits, self.n = bits, 2 ** len(bits)

    def mask(self, place):
        return sum(((place >> k) & 1) << bit for k, bit in enumerate(self.bits))

    def matrix(self):
        rows = D // self.n
        place = jnp.arange(D, dtype=jnp.int32)
        block = self.mask(place // rows) ^ lax.axis_index("dp")
        source = block * rows + place % rows
        return (place[:, None] == source[None, :]).astype(BF16)

    def where(self):
        other = jnp.arange(self.n, dtype=jnp.int32) ^ lax.axis_index("dp")
        return sum(((other >> bit) & 1) << k for k, bit in enumerate(self.bits))

    def places(self, count):
        return self.mask(jnp.arange(count, dtype=jnp.int32)) ^ lax.axis_index("dp")


class Gather:
    def __init__(self, shard, n):
        self.value, self.n = shard, n

    def step(self, bit):
        self.value = jnp.concatenate([self.value, swap(self.value, bit, self.n)], axis=0)

    def cut(self, start, stop):
        return Gather(self.value[:, start:stop], self.n)


class Scatter:
    def __init__(self, kept, got, n):
        self.terms, self.n = [kept, got], n

    def away(self):
        half = self.terms[0].shape[0] // 2
        return self.total([t[half:] for t in self.terms]).astype(BF16)

    def send(self, away, bit):
        self.terms = [t[: away.shape[0]] for t in self.terms] + [swap(away, bit, self.n)]

    def step(self, bit):
        self.send(self.away(), bit)

    def total(self, parts=None):
        parts = self.terms if parts is None else parts
        result = parts[0].astype(F32)
        for part in parts[1:]:
            result = result + part.astype(F32)
        return result

    def join(self, other):
        self.terms = [jnp.concatenate([self.total(), other.total()], axis=1)]
        return self


def adapt(weight, grad, moment, square, decay):
    new_moment = 0.9 * moment + 0.1 * grad
    new_square = 0.999 * square + 0.001 * grad * grad
    update = new_moment / (1.0 - 0.9**STEP) / (jnp.sqrt(new_square / (1.0 - 0.999**STEP)) + 1e-06)
    return (new_moment, new_square, update + decay * weight)


def lane_sums(value):
    columns = jnp.sum(value * value, axis=0, keepdims=True)
    result = columns[:, :128]
    for start in range(128, value.shape[1], 128):
        result = result + columns[:, start : start + 128]
    return result


def adapt_kernel(first, *refs):
    before_ref, sums_ref = refs[8], refs[15]
    sums = before_ref[...]
    row = lax.broadcasted_iota(jnp.int32, sums.shape, 0)
    for i in range(2):
        weight_ref, grad_ref, moment_ref, square_ref = refs[i * 4 : i * 4 + 4]
        outs = refs[9 + i * 3 : 12 + i * 3]
        weight = weight_ref[...]
        values = adapt(weight, grad_ref[...], moment_ref[...], square_ref[...], 0.01)
        for out, value in zip(outs, values):
            out[...] = value
        sums = jnp.where(row == first + i, lane_sums(weight), sums)
        sums = jnp.where(row == 4 + first + i, lane_sums(values[2]), sums)
    sums_ref[...] = sums


def adapt_two(first, before, *operands):
    shapes = [jax.ShapeDtypeStruct(operands[i * 4].shape, F32) for i in (0, 0, 0, 1, 1, 1)]
    return pl.pallas_call(
        partial(adapt_kernel, first),
        out_shape=shapes + [jax.ShapeDtypeStruct((8, 128), F32)],
        compiler_params=pltpu.CompilerParams(vmem_limit_bytes=VMEM),
        cost_estimate=cost(2),
        name="adapt",
    )(*operands, before)


def renew_kernel(sums_ref, *refs):
    norms = jnp.sqrt(jnp.sum(sums_ref[...], axis=1, keepdims=True))
    refs[12][...] = jnp.broadcast_to(norms, (8, 128))
    for i in range(4):
        rate = 0.25 * (norms[i : i + 1] / norms[4 + i : 5 + i])
        refs[8 + i][...] = refs[i][...] - rate * refs[4 + i][...]


def renew(sums, weights, updates):
    return pl.pallas_call(
        renew_kernel,
        out_shape=[jax.ShapeDtypeStruct(weight.shape, F32) for weight in weights]
        + [jax.ShapeDtypeStruct((8, 128), F32)],
        compiler_params=pltpu.CompilerParams(vmem_limit_bytes=VMEM),
        cost_estimate=cost(2),
        name="renew",
    )(sums, *weights, *updates)


def body(
    n,
    frames,
    cotangent,
    lengths,
    w_qkv,
    w_attn,
    w_in,
    w_out,
    vectors,
    moment_qkv,
    moment_attn,
    moment_in,
    moment_out,
    moment_vec,
    square_qkv,
    square_attn,
    square_in,
    square_out,
    square_vec,
):
    rows_d, rows_f, width = w_qkv.shape[0], w_out.shape[0], vectors.shape[0]
    core, one, two, *others = range(n.bit_length() - 1)
    far = others[::-1]
    order_a, order_b = Order(far + [two, one, core]), Order(far + [one, two, core])
    x = frames[0]

    aligned = rows_d % 8 == 0
    half = w_qkv.shape[1] // 2
    tail = jnp.pad(vectors.reshape(rows_d, 12), ((0, 0), (0, 116)))
    low_qkv = jnp.concatenate([w_qkv, tail], axis=1).astype(BF16)
    low_qkv, *masters = phase(low_qkv, w_attn, w_in, w_out)
    low_in = jnp.concatenate(masters[:2], axis=1).astype(BF16)
    qkv, out = Gather(low_qkv, n), Gather(masters[2].astype(BF16), n)
    to_a, to_b = phase(order_a.matrix(), order_b.matrix())
    x_a, x_b = arrange(x, to_a), arrange(x, to_b)
    inner = Gather(low_in, n)
    if aligned:
        side = low_in.shape[1] // 2
        mine = own_bit(core)
        kept = lax.dynamic_slice_in_dim(low_in, mine * side, side, 1)
        got = swap(lax.dynamic_slice_in_dim(low_in, (1 - mine) * side, side, 1), core, n)
        pair = [jnp.where(mine == 0, kept, got), jnp.where(mine == 0, got, kept)]
        inner.value = jnp.concatenate(pair, axis=0)
    else:
        attn_in = lax.all_gather(low_in, "dp", axis=0, tiled=True)
    qkv.step(far[0])
    qkv.value, inner.value, x_a, x_b = phase(qkv.value, inner.value, x_a, x_b)
    for bit in far[1:]:
        qkv.step(bit)
        (qkv.value,) = phase(qkv.value)
    left, right = qkv.cut(0, half), qkv.cut(half, 2 * half + 128)
    for bits, more in (((two, one), far[:1]), ((one, two), far[1:])):
        left.step(bits[0])
        right.step(bits[1])
        for bit in more if aligned else ():
            inner.step(bit)
        left.value, right.value, inner.value = phase(left.value, right.value, inner.value)
    left = (left.value, swap(left.value, core, n))
    right = (right.value, swap(right.value, core, n))
    cut = 1024 if aligned else low_in.shape[1]
    in_left, in_right = inner.cut(0, cut), inner.cut(cut, inner.value.shape[1])

    def in_step(bit_left, bit_right):
        if aligned:
            in_left.step(bit_left)
            in_right.step(bit_right)

    left, right, in_left.value, in_right.value, out.value = phase(
        left, right, in_left.value, in_right.value, out.value
    )
    in_step(two, one)
    out.step(far[0])
    vec_rows = jnp.concatenate([part[:, half:] for part in right], axis=0)
    vec = dot(to_b, vec_rows)[:, :12].reshape(12, D)
    bias_qkv = jnp.concatenate([vec[:1], jnp.zeros((1, D), F32), vec[1:2]], axis=1)

    packed = project(x_a, x_b, left, right, bias_qkv)
    packed, vec, in_left.value, in_right.value, out.value = phase(
        packed, vec, in_left.value, in_right.value, out.value
    )
    in_step(one, two)
    for bit in far[1:]:
        out.step(bit)
    some = PAIRS // 3
    heads = attend(lengths, packed, 0, some)
    heads, out.value = phase(heads, out.value)
    out_left, out_right = out.cut(0, D // 2), out.cut(D // 2, D)
    out_left.step(two)
    out_right.step(one)
    heads = attend(lengths, packed, some, some, heads)
    heads, out_left.value, out_right.value, in_left.value, in_right.value = phase(
        heads, out_left.value, out_right.value, in_left.value, in_right.value
    )
    out_left.step(one)
    out_right.step(two)
    in_parts = [in_left.value, in_right.value]
    if aligned:
        in_parts += [swap(part, core, n) for part in in_parts]
    heads = attend(lengths, packed, 2 * some, some, heads)
    heads, out_left.value, out_right.value, in_parts = phase(
        heads, out_left.value, out_right.value, in_parts
    )
    out_parts = [out_left.value, out_right.value]
    out_parts += [swap(part, core, n) for part in out_parts]
    if aligned:
        chips_a, chips_b = [order.places(n // 2) // 2 for order in (order_a, order_b)]
        blocks_a, blocks_b = order_a.places(n), order_b.places(n)
        first = jnp.stack([mine, 1 - mine]) * (side // 128)
        corners = jnp.stack([first, first + cut // 128], axis=1).reshape(4)
        columns = jnp.array([0, D // 256], jnp.int32)
        places = jnp.concatenate([chips_a, chips_b, blocks_a, blocks_b, corners, columns])
        base = 3 * n
        in_pieces = tuple((i % 2 * n // 2, n // 2, base + i) for i in range(4))
        out_pieces = tuple((n + i % 2 * n + i // 2 * n // 2, n // 2, base + 4 + i % 2) for i in range(4))
    else:
        sides = []
        for i, order in enumerate((order_a, order_b)):
            value = jnp.concatenate(out_parts[i::2], axis=0).reshape(n, rows_f, D // 2)
            sides.append(value[jnp.argsort(order.places(n))].reshape(FF, D // 2))
        in_parts, out_parts = [attn_in], [jnp.concatenate(sides, axis=1)]
        places = jnp.zeros((2,), jnp.int32)
        in_pieces = out_pieces = ((0, 1, 1),)
    ctx, ctxt, lse = heads

    where = order_b.where() if aligned else jnp.arange(CHUNKS, dtype=jnp.int32)
    mixed, dres1, dctx, sums, *grads = feed(
        *(lengths, x, ctx, cotangent[0], vec, to_a, to_b, places, where),
        *((in_parts, in_pieces), (out_parts, out_pieces)),
    )
    if not aligned:
        grad = jnp.concatenate(grads[:2], axis=0).reshape(n, rows_f, D)
        grads[:2] = jnp.split(grad[order_b.places(n)].reshape(FF, D), 2)
    sum_out = Scatter(grads[0], swap(grads[1], core, n), n)
    sum_in = Scatter(grads[2], swap(grads[3], core, n), n)

    dqkv, biases = None, []
    for first, count, bits in ((0, 1, (one, two)), (1, 4, (two, one)), (5, 1, None)):
        dqkv, bias = attend_back(lengths, packed, dctx, ctxt, lse, first, count, dqkv)
        biases.append(bias)
        if bits is not None:
            sum_in.terms[-1], sum_out.terms[-1], dqkv = phase(
                sum_in.terms[-1], sum_out.terms[-1], dqkv
            )
            sum_in.step(bits[0])
            sum_out.step(bits[1])
    full_qkv = jnp.concatenate(
        [
            arrange(to_a, jnp.concatenate(left, axis=0)),
            arrange(to_b, jnp.concatenate([part[:, :half] for part in right], axis=0)),
        ],
        axis=1,
    )
    dqkv, full_qkv, sum_in.terms[-1], sum_out.terms[-1] = phase(
        dqkv, full_qkv, sum_in.terms[-1], sum_out.terms[-1]
    )

    def late_grads(side):
        cols = slice(side * D // 2, (side + 1) * D // 2)
        queries, keys = [dot_tn(x_a[:, cols], dqkv[i]).astype(BF16) for i in range(2)]
        values = dot_tn(x_b[:, cols], dqkv[2]).astype(BF16)
        return (
            jnp.concatenate([queries, keys], axis=1),
            jnp.concatenate([values, grads[4 + side]], axis=1),
        )

    away_a, away_b = late_grads(1)
    away_a, away_b, dqkv, away_in, away_out = phase(
        away_a, away_b, dqkv, sum_in.away(), sum_out.away()
    )
    got_a, got_b = swap(away_a, core, n), swap(away_b, core, n)
    sum_in.send(away_in, others[0])
    sum_out.send(away_out, others[0])
    kept_a, kept_b = late_grads(0)
    got_a, got_b, kept_a, kept_b = phase(got_a, got_b, kept_a, kept_b)
    late_a, late_b = Scatter(kept_a, got_a, n), Scatter(kept_b, got_b, n)
    late_a.step(one)
    late_b.step(two)
    late_a.terms[-1], late_b.terms[-1], sum_in.terms[-1], sum_out.terms[-1] = phase(
        late_a.terms[-1], late_b.terms[-1], sum_in.terms[-1], sum_out.terms[-1]
    )
    away_a, away_b, *aways = phase(
        late_a.away(), late_b.away(), *((sum_in.away(), sum_out.away()) if others[1:] else ())
    )
    late_a.send(away_a, two)
    late_b.send(away_b, one)
    for bit in others[1:2]:
        sum_in.send(aways[0], bit)
        sum_out.send(aways[1], bit)
    for bit in others[2:]:
        sum_in.step(bit)
        sum_out.step(bit)
    late_a.terms[-1], late_b.terms[-1] = phase(late_a.terms[-1], late_b.terms[-1])
    late = late_a.join(late_b)
    late.step(others[0])
    share_in, share_out = sum_in.total(), sum_out.total()
    late.terms[-1], share_in, share_out = phase(late.terms[-1], share_in, share_out)
    for bit in others[1:]:
        late.step(bit)
    share_late = late.total()
    bias_sums = jnp.concatenate(biases, axis=0)
    grad_vec = jnp.concatenate(
        [bias_sums[:, 0].reshape(1, D), bias_sums[:, 1].reshape(1, D), sums[2:]]
    ).reshape(-1, 128)
    input_grad = dres1
    for i in range(3):
        input_grad = input_grad + dot_nt(dqkv[i], full_qkv[:, i * D : (i + 1) * D])

    next_in = adapt_two(
        2,
        jnp.zeros((8, 128), F32),
        *(w_in, share_in, moment_in, square_in),
        *(w_out, share_out, moment_out, square_out),
    )
    next_attn = adapt_two(
        0,
        next_in[6],
        *(w_qkv, share_late[:, : 3 * D], moment_qkv, square_qkv),
        *(w_attn, share_late[:, 3 * D :], moment_attn, square_attn),
    )
    reduced = sum_all(jnp.concatenate([next_attn[6], grad_vec], axis=0), n)
    place = lax.axis_index("dp") * width
    share_vec = lax.dynamic_slice_in_dim(reduced[8:].reshape(-1), place, width, 0)
    updates = (next_attn[2], next_attn[5], next_in[2], next_in[5])
    *new_weights, norms = renew(reduced[:8], (w_qkv, w_attn, w_in, w_out), updates)
    vec_moment, vec_square, vec_update = adapt(vectors, share_vec, moment_vec, square_vec, 0.0)
    return (
        mixed[None],
        input_grad[None],
        *new_weights,
        vectors - 0.4 * vec_update,
        *(next_attn[0], next_attn[3], next_in[0], next_in[3], vec_moment),
        *(next_attn[1], next_attn[4], next_in[1], next_in[4], vec_square),
        norms[:, 0],
    )


def solution(mesh):
    clips, matrix, vector = P("dp", None, None), P("dp", None), P("dp")
    parameters = (matrix,) * 4 + (vector,)
    return jax.shard_map(
        partial(body, mesh.shape["dp"]),
        mesh=mesh,
        in_specs=(clips, clips, vector) + parameters * 3,
        out_specs=(clips, clips) + parameters * 3 + (P(),),
        check_vma=False,
    )
```

```python
from functools import partial

import jax
import jax.numpy as jnp
from jax import lax
from jax.experimental import pallas as pl
from jax.experimental.pallas import tpu as pltpu
from jax.sharding import PartitionSpec as P

D = 768
FF = 3072
HEADS = 12
HEAD_DIM = 64
PAIRS = HEADS // 2
WIDE = 2 * HEAD_DIM
CHUNKS = FF // D
STEP = 10
MASKED = -1e9
VMEM = 60 * 2**20
ROOM = 24 * 2**20


BF16 = jnp.bfloat16
F32 = jnp.float32


def dot(a, b):
    return jnp.dot(a, b, preferred_element_type=F32)


def dot_nt(a, b):
    return lax.dot_general(a, b, (((1,), (1,)), ((), ())), preferred_element_type=F32)


def dot_tn(a, b):
    return lax.dot_general(a, b, (((0,), (0,)), ((), ())), preferred_element_type=F32)


def cost(us):
    return pl.CostEstimate(flops=int(us * 5.0e7), bytes_accessed=0, transcendentals=0)


def arrange(value, matrix):
    return dot(value, matrix).astype(BF16)


def project_kernel(*refs):
    xa_ref, xb_ref, la_ref, lb_ref, ra_ref, rb_ref, source_ref, lane_ref, out_ref, bias_ref = refs
    width = la_ref.shape[1]

    @pl.when(pl.program_id(0) == 0)
    def _():
        tail = jnp.concatenate([ra_ref[:, width:], rb_ref[:, width:]], axis=0)
        start = source_ref[...] * 12
        entry = lax.broadcasted_iota(jnp.int32, (D, D), 1)
        lane = lax.broadcasted_iota(jnp.int32, (128, D), 0)
        bias_ref[...] = jnp.zeros_like(bias_ref)
        for i in range(2):
            offset = entry + i * D - start
            picked = dot_tn(tail, jnp.where((offset >= 0) & (offset < 12), 1.0, 0.0).astype(BF16))
            picked = jnp.where(lane == lane_ref[i : i + 1, :], picked, 0.0)
            bias_ref[:, 2 * i * D : (2 * i + 1) * D] = jnp.sum(picked, axis=0, keepdims=True)

    left = jnp.concatenate([la_ref[...], lb_ref[...]], axis=0)
    out_ref[:, :width] = (dot(xa_ref[...], left) + bias_ref[:, :width]).astype(BF16)
    right = jnp.concatenate([ra_ref[:, :width], rb_ref[:, :width]], axis=0)
    out_ref[:, width:] = (dot(xb_ref[...], right) + bias_ref[:, width:]).astype(BF16)


def project(x_a, x_b, left, right, source):
    seq = x_a.shape[0]
    rows = min(512, seq)
    lanes = (jnp.arange(2 * D, dtype=jnp.int32) % 12).reshape(2, D)
    operands = (*left, *right, source.reshape(D, 1), lanes)

    def fixed(shape):
        return pl.BlockSpec(shape, lambda i: (0, 0), pipeline_mode=pl.Buffered(1))

    return pl.pallas_call(
        project_kernel,
        grid=(seq // rows,),
        in_specs=[pl.BlockSpec((rows, D), lambda i: (i, 0))] * 2
        + [fixed(part.shape) for part in operands],
        out_specs=pl.BlockSpec((rows, 3 * D), lambda i: (i, 0)),
        out_shape=jax.ShapeDtypeStruct((seq, 3 * D), BF16),
        scratch_shapes=[pltpu.VMEM((1, 3 * D), F32)],
        compiler_params=pltpu.CompilerParams(vmem_limit_bytes=ROOM),
        cost_estimate=cost(5),
        name="project",
    )(x_a, x_b, *operands)


def attend_kernel(len_ref, q_ref, k_ref, v_ref, ctx_ref, ctxt_ref, lse_ref):
    seq = q_ref.shape[0]
    qt = (q_ref[...].astype(F32) * 0.125).T.astype(BF16)
    vt = v_ref[...].astype(F32).T.astype(BF16)
    k = k_ref[...]
    keep = lax.broadcasted_iota(jnp.int32, (seq, seq), 0) < len_ref[0]
    zero = jnp.zeros((HEAD_DIM, seq), BF16)
    ones = jnp.ones((16, seq), BF16)
    for h in range(2):
        rows = slice(h * HEAD_DIM, (h + 1) * HEAD_DIM)
        q = jnp.concatenate([qt[rows], zero] if h == 0 else [zero, qt[rows]], axis=0)
        scores = jnp.where(keep, dot(k, q), MASKED)
        peak = jnp.max(scores, axis=0, keepdims=True)
        expo = jnp.exp(scores - peak).astype(BF16)
        both = dot(jnp.concatenate([vt[rows], ones], axis=0), expo)
        total = both[HEAD_DIM : HEAD_DIM + 1]
        ctxt_ref[rows, :] = both[:HEAD_DIM] / total
        lse_ref[0, h : h + 1, :] = peak + jnp.log(total)
    ctx_ref[...] = ctxt_ref[...].T.astype(BF16)


def after(kernel, first, count):
    def call(*refs):
        kernel(*refs[:first], *refs[first + count :])

    return call


def untouched(values):
    return [pl.BlockSpec(memory_space=pl.ANY)] * len(values)


def attend(lengths, packed, first, count, before=(), waits=()):
    seq = packed.shape[0]
    extra = (*before, *waits)
    return pl.pallas_call(
        after(attend_kernel, 4, len(extra)),
        grid_spec=pltpu.PrefetchScalarGridSpec(
            num_scalar_prefetch=1,
            grid=(count,),
            in_specs=[
                pl.BlockSpec((seq, WIDE), lambda p, _, i=i: (0, i * PAIRS + first + p))
                for i in range(3)
            ]
            + untouched(extra),
            out_specs=[
                pl.BlockSpec((seq, WIDE), lambda p, _: (0, first + p)),
                pl.BlockSpec((WIDE, seq), lambda p, _: (first + p, 0)),
                pl.BlockSpec((1, 2, seq), lambda p, _: (first + p, 0, 0)),
            ],
        ),
        out_shape=[
            jax.ShapeDtypeStruct((seq, D), BF16),
            jax.ShapeDtypeStruct((D, seq), F32),
            jax.ShapeDtypeStruct((PAIRS, 2, seq), F32),
        ],
        input_output_aliases={4 + i: i for i in range(len(before))},
        compiler_params=pltpu.CompilerParams(vmem_limit_bytes=ROOM),
        cost_estimate=cost(4 * count),
        name="attend",
    )(lengths, packed, packed, packed, *extra)


def attend_back_kernel(
    block, len_ref, q_ref, k_ref, v_ref, do_ref, ctxt_ref, lse_ref, out_ref, sum_ref, dqt_ref
):
    seq = q_ref.shape[0]
    q = q_ref[...].astype(F32) * 0.125
    qt = q.T.astype(BF16)
    q = q.astype(BF16)
    do = do_ref[...]
    dof = do.astype(F32).T
    dot_ = dof.astype(BF16)
    prod = dof * ctxt_ref[...]
    kt = k_ref[...].astype(F32).T.astype(BF16)
    row = lax.broadcasted_iota(jnp.int32, (HEAD_DIM, seq), 0)

    def pieces(vec):
        high = vec.astype(BF16).astype(F32)
        mid = (vec - high).astype(BF16).astype(F32)
        low = vec - high - mid
        picked = jnp.where(row == 1, mid, jnp.where(row == 2, low, 0.0))
        return jnp.where(row == 0, high, picked).astype(BF16)

    q_aug, do_aug, fill = [], [], []
    for h in range(2):
        rows = slice(h * HEAD_DIM, (h + 1) * HEAD_DIM)
        lse = lse_ref[0, h : h + 1]
        delta = jnp.sum(prod[rows], axis=0, keepdims=True)
        q_parts = [qt[rows], pieces(-lse)]
        do_parts = [dot_[rows], pieces(-delta)]
        q_aug.append(jnp.concatenate(q_parts if h == 0 else q_parts[::-1], axis=0))
        do_aug.append(jnp.concatenate(do_parts if h == 0 else do_parts[::-1], axis=0))
        fill.append(MASKED - lse)
    lane = lax.broadcasted_iota(jnp.int32, (block, WIDE), 1)
    mine = (lane < HEAD_DIM, lane >= HEAD_DIM)
    one = (
        jnp.where(lane < HEAD_DIM + 3, 1.0, 0.0).astype(BF16),
        jnp.where(lane < 3, 1.0, 0.0).astype(BF16),
    )
    for j in range(seq // block):
        rows = slice(j * block, (j + 1) * block)
        keep = lax.broadcasted_iota(jnp.int32, (block, seq), 0) + j * block < len_ref[0]
        k, v = k_ref[rows, :], v_ref[rows, :]
        dv, dk = [], []
        for h in range(2):
            heads = slice(h * HEAD_DIM, (h + 1) * HEAD_DIM)
            k_aug, v_aug = jnp.where(mine[h], k, one[h]), jnp.where(mine[h], v, one[h])
            prob = jnp.exp(jnp.where(keep, dot(k_aug, q_aug[h]), fill[h]))
            dscore = (prob * dot(v_aug, do_aug[h])).astype(BF16)
            dv.append(dot(prob.astype(BF16), do))
            dk.append(dot(dscore, q))
            dq = dot(kt[heads, rows], dscore)
            if j == 0:
                dqt_ref[heads, :] = dq
            else:
                dqt_ref[heads, :] += dq
        out_ref[1, rows, :] = jnp.where(mine[0], dk[0], dk[1]).astype(BF16)
        out_ref[2, rows, :] = jnp.where(mine[0], dv[0], dv[1]).astype(BF16)
    out_ref[0] = (dqt_ref[...] * 0.125).T.astype(BF16)
    sum_ref[0, 0:1] = jnp.sum(out_ref[0].astype(F32), axis=0, keepdims=True)
    sum_ref[0, 1:2] = jnp.sum(out_ref[2].astype(F32), axis=0, keepdims=True)


def attend_back(lengths, packed, dctx, ctxt, lse, first, count, before=None, waits=()):
    seq = packed.shape[0]
    extra = tuple(waits) if before is None else (before, *waits)
    return pl.pallas_call(
        after(partial(attend_back_kernel, min(512, seq)), 7, len(extra)),
        grid_spec=pltpu.PrefetchScalarGridSpec(
            num_scalar_prefetch=1,
            grid=(count,),
            in_specs=[
                pl.BlockSpec((seq, WIDE), lambda p, _, i=i: (0, i * PAIRS + first + p))
                for i in range(3)
            ]
            + [
                pl.BlockSpec((seq, WIDE), lambda p, _: (0, first + p)),
                pl.BlockSpec((WIDE, seq), lambda p, _: (first + p, 0)),
                pl.BlockSpec((1, 2, seq), lambda p, _: (first + p, 0, 0)),
            ]
            + untouched(extra),
            out_specs=[
                pl.BlockSpec((3, seq, WIDE), lambda p, _: (0, 0, first + p)),
                pl.BlockSpec((1, 2, WIDE), lambda p, _: (p, 0, 0)),
            ],
            scratch_shapes=[pltpu.VMEM((WIDE, seq), F32)],
        ),
        out_shape=[
            jax.ShapeDtypeStruct((3, seq, D), BF16),
            jax.ShapeDtypeStruct((count, 2, WIDE), F32),
        ],
        input_output_aliases={} if before is None else {7: 0},
        compiler_params=pltpu.CompilerParams(vmem_limit_bytes=ROOM),
        cost_estimate=cost(6 * count),
        name="attend_back",
    )(lengths, packed, packed, packed, dctx, ctxt, lse, *extra)


def normal_parts(u):
    return 0.5 + 0.5 * lax.erf(u * 0.7071067811865476), jnp.exp(-0.5 * u * u)


def norm_forward(resid):
    center = resid - jnp.mean(resid, axis=-1, keepdims=True)
    inverse = lax.rsqrt(jnp.mean(center * center, axis=-1, keepdims=True) + 1e-05)
    return center * inverse, inverse


def norm_back(grad, gain, unit, inverse):
    du = grad * gain
    mean = jnp.mean(du, axis=-1, keepdims=True)
    return inverse * (du - mean - unit * jnp.mean(du * unit, axis=-1, keepdims=True))


def column_sum(value):
    return jnp.sum(value.astype(F32), axis=0, keepdims=True)


def waited(copies):
    for copy in copies:
        copy.wait()


def feed_kernel(in_pieces, out_pieces, steps, *refs):
    len_ref, place_ref, where_ref, x_ref, ctx_ref, cot_ref, vec_ref, to_a_ref, to_b_ref = refs[:9]
    in_parts, refs = refs[9 : 9 + len(in_pieces)], refs[9 + len(in_pieces) :]
    out_parts, refs = refs[: len(out_pieces)], refs[len(out_pieces) :]
    mixed_ref, dres1_ref, dctx_ref, sum_ref, *grads = refs[:10]
    out_grads, in_grads, attn_grads = grads[:2], grads[2:4], grads[4:6]
    w_ref, w2_ref, act_ref, dhid_ref, first_ref, ctxb_ref, dbr_ref, dres_ref = refs[10:18]
    unit_ref, inverse_ref, slope_ref, held_ref, in_sems, part_sems, out_sems = refs[18:]
    step = pl.program_id(0)
    size = x_ref.shape[0]
    blocks = where_ref.shape[0] // CHUNKS
    first_grad, second_grad = steps, steps + CHUNKS
    back, last = steps + 2 * CHUNKS, 2 * steps + 2 * CHUNKS

    def vec(i):
        return vec_ref[i : i + 1, :]

    def weight(c):
        return w_ref.at[:, c * D : (c + 1) * D]

    def part_copies(whole_ref, parts, pieces, sems):
        made, total = [], 0
        for part, (first, count, column) in zip(parts, pieces):
            rows, width = part.shape[0] // count, part.shape[1]
            columns = pl.ds(pl.multiple_of(place_ref[column] * 128, 128), width)
            for i in range(count):
                where = pl.multiple_of(place_ref[first + i] * rows, rows)
                target = whole_ref.at[pl.ds(where, rows), columns]
                source = part.at[pl.ds(i * rows, rows), :]
                made.append(pltpu.make_async_copy(source, target, sems.at[total]))
                total += 1
        return made

    early = sum(count for _, count, _ in in_pieces[: max(1, len(in_pieces) // 2)])

    def in_weights():
        return part_copies(w_ref, in_parts, in_pieces, in_sems)

    def out_weights():
        return part_copies(w2_ref, out_parts, out_pieces, part_sems)

    @pl.when(step == 0)
    def _():
        for copy in in_weights() + out_weights():
            copy.start()
        sum_ref[...] = jnp.zeros_like(sum_ref)

    @pl.when(step < steps)
    def _():
        rows = pl.ds(pl.multiple_of(step * size, size), size)

        @pl.when(step == 0)
        def _():
            waited(in_weights()[:early])

        resid = x_ref[...].astype(F32) + (dot(ctx_ref[...], weight(0)[...]) + vec(2))
        unit1, inverse1 = norm_forward(resid)
        unit_ref[rows, :] = unit1
        inverse_ref[rows, :] = jnp.broadcast_to(inverse1, (size, 128))
        first = unit1 * vec(3) + vec(4)
        first_b = first.astype(BF16)
        first_ref[rows, :] = arrange(first_b, to_a_ref[...])
        ctxb_ref[rows, :] = arrange(ctx_ref[...], to_b_ref[...])

        @pl.when(step == 0)
        def _():
            waited(in_weights()[early:] + out_weights())

        branch = None
        for c in range(CHUNKS):
            cols = slice(c * D, (c + 1) * D)
            hidden = dot(first_b, weight(1 + c)[...]) + vec(5 + c)
            phi, bell = normal_parts(hidden)
            active = (hidden * phi).astype(BF16)
            act_ref[rows, cols] = active
            slope_ref[:, cols] = phi + hidden * bell * 0.3989422804014327
            part = dot(active, w2_ref[cols, :])
            branch = part if branch is None else branch + part
        unit2, inverse2 = norm_forward(first + (branch + vec(9)))
        place = lax.broadcasted_iota(jnp.int32, (size, 1), 0) + step * size
        keep = (place < len_ref[0]).astype(F32)
        mixed_ref[...] = ((unit2 * vec(10) + vec(11)) * keep).astype(BF16)
        dz = cot_ref[...].astype(F32) * keep
        dres2 = norm_back(dz, vec(10), unit2, inverse2)
        dres_ref[rows, :] = dres2
        dbranch = dres2.astype(BF16)
        dbr_ref[rows, :] = dbranch
        sum_ref[9:10, :] += column_sum(dbranch)
        sum_ref[10:11, :] += column_sum(dz * unit2)
        sum_ref[11:12, :] += column_sum(dz)
        for c in range(CHUNKS):
            cols = slice(c * D, (c + 1) * D)
            dhidden = (dot_nt(dbranch, w2_ref[cols, :]) * slope_ref[:, cols]).astype(BF16)
            dhid_ref[rows, cols] = dhidden
            sum_ref[5 + c : 6 + c, :] += column_sum(dhidden)

    def out_copies(step, go):
        chunk = step - first_grad
        slot = lax.rem(chunk, 2)
        rows = D // blocks
        for i in range(blocks):
            place = where_ref[chunk * blocks + i]
            source = held_ref.at[slot, pl.ds(i * rows, rows), :]
            for half in range(2):
                where = pl.multiple_of((place - half * 2 * blocks) * rows, rows)

                @pl.when((place >= 2 * blocks) == (half == 1))
                def _(half=half, where=where, source=source, i=i):
                    target = out_grads[half].at[pl.ds(where, rows), :]
                    go(pltpu.make_async_copy(source, target, out_sems.at[slot, i]))

    def in_copies(step, grads, column):
        slot = lax.rem(step - first_grad, 2)
        made = []
        for half in range(2):
            source = held_ref.at[slot, pl.ds(half * D // 2, D // 2), :]
            target = grads[half].at[:, pl.ds(column, D)]
            made.append(pltpu.make_async_copy(source, target, out_sems.at[slot, half]))
        return made

    def in_column(step):
        return pl.multiple_of((step - second_grad) * D, D)

    def start(copy):
        copy.start()

    def wait(copy):
        copy.wait()

    @pl.when((step >= first_grad) & (step < second_grad))
    def _():
        @pl.when(step >= first_grad + 2)
        def _():
            out_copies(step - 2, wait)

        cols = pl.ds(pl.multiple_of((step - first_grad) * D, D), D)
        grad = dot_tn(act_ref[:, cols], dbr_ref[...]).astype(BF16)
        held_ref[lax.rem(step - first_grad, 2)] = grad
        out_copies(step, start)

    @pl.when((step >= second_grad) & (step < back))
    def _():
        @pl.when(step < second_grad + 2)
        def _():
            out_copies(step - 2, wait)

        @pl.when(step >= second_grad + 2)
        def _():
            waited(in_copies(step - 2, in_grads, in_column(step - 2)))

        cols = pl.ds(in_column(step), D)
        grad = dot_tn(first_ref[...], dhid_ref[:, cols]).astype(BF16)
        held_ref[lax.rem(step - first_grad, 2)] = grad
        for copy in in_copies(step, in_grads, in_column(step)):
            copy.start()

    @pl.when((step >= back) & (step < last))
    def _():
        rows = pl.ds(pl.multiple_of((step - back) * size, size), size)
        dfirst = dres_ref[rows, :]
        for c in range(CHUNKS):
            dfirst = dfirst + dot_nt(dhid_ref[rows, c * D : (c + 1) * D], weight(1 + c)[...])
        unit = unit_ref[rows, :]
        dres1 = norm_back(dfirst, vec(3), unit, inverse_ref[rows, 0:1])
        dres1_ref[...] = dres1
        dattend = dres1.astype(BF16)
        dbr_ref[rows, :] = dattend
        dctx_ref[...] = dot_nt(dattend, weight(0)[...]).astype(BF16)
        sum_ref[2:3, :] += column_sum(dattend)
        sum_ref[3:4, :] += column_sum(dfirst * unit)
        sum_ref[4:5, :] += column_sum(dfirst)

    @pl.when(step == last)
    def _():
        waited(in_copies(back - 2, in_grads, in_column(back - 2)))
        waited(in_copies(back - 1, in_grads, in_column(back - 1)))
        held_ref[0] = dot_tn(ctxb_ref[...], dbr_ref[...]).astype(BF16)
        copies = in_copies(first_grad, attn_grads, 0)
        for copy in copies:
            copy.start()
        waited(copies)


def feed(lengths, x, ctx, cot, vec, to_a, to_b, places, where, in_side, out_side):
    (in_parts, in_pieces), (out_parts, out_pieces) = in_side, out_side
    seq = x.shape[0]
    size = min(256, seq)
    steps = seq // size
    back = steps + 2 * CHUNKS
    anywhere = pl.BlockSpec(memory_space=pl.ANY)

    def early(width):
        return pl.BlockSpec((size, width), lambda i, *_: (jnp.minimum(i, steps - 1), 0))

    def late(width):
        return pl.BlockSpec((size, width), lambda i, *_: (jnp.clip(i - back, 0, steps - 1), 0))

    def fixed(shape):
        return pl.BlockSpec(shape, lambda i, *_: (0, 0), pipeline_mode=pl.Buffered(1))

    shape = jax.ShapeDtypeStruct
    return pl.pallas_call(
        partial(feed_kernel, in_pieces, out_pieces, steps),
        grid_spec=pltpu.PrefetchScalarGridSpec(
            num_scalar_prefetch=3,
            grid=(2 * steps + 2 * CHUNKS + 1,),
            in_specs=[early(D)] * 3
            + [fixed((12, D)), fixed((D, D)), fixed((D, D))]
            + untouched(in_parts)
            + untouched(out_parts),
            out_specs=[early(D), late(D), late(D), pl.BlockSpec((12, D), lambda i, *_: (0, 0))]
            + [anywhere] * 6,
            scratch_shapes=[
                pltpu.VMEM((D, D + FF), BF16),
                pltpu.VMEM((FF, D), BF16),
                pltpu.VMEM((seq, FF), BF16),
                pltpu.VMEM((seq, FF), BF16),
                pltpu.VMEM((seq, D), BF16),
                pltpu.VMEM((seq, D), BF16),
                pltpu.VMEM((seq, D), BF16),
                pltpu.VMEM((seq, D), F32),
                pltpu.VMEM((seq, D), F32),
                pltpu.VMEM((seq, 128), F32),
                pltpu.VMEM((size, FF), F32),
                pltpu.VMEM((2, D, D), BF16),
                pltpu.SemaphoreType.DMA((sum(count for _, count, _ in in_pieces),)),
                pltpu.SemaphoreType.DMA((sum(count for _, count, _ in out_pieces),)),
                pltpu.SemaphoreType.DMA((2, max(2, where.shape[0] // CHUNKS))),
            ],
        ),
        out_shape=[
            shape((seq, D), BF16),
            shape((seq, D), F32),
            shape((seq, D), BF16),
            shape((12, D), F32),
        ]
        + [shape((FF // 2, D), BF16)] * 2
        + [shape((D // 2, FF), BF16)] * 2
        + [shape((D // 2, D), BF16)] * 2,
        compiler_params=pltpu.CompilerParams(vmem_limit_bytes=VMEM),
        cost_estimate=cost(50),
        name="feed",
    )(lengths, places, where, x, ctx, cot, vec, to_a, to_b, *in_parts, *out_parts)


def swap(value, bits, n):
    mask = sum(1 << bit for bit in bits)
    return lax.ppermute(value, "dp", [(i, i ^ mask) for i in range(n)])


def subsets(bits):
    return [[bit for k, bit in enumerate(bits) if p >> k & 1] for p in range(1, 2 ** len(bits))]


def sum_all(value, groups, n):
    for bits in groups:
        value = sum([swap(value, some, n) for some in subsets(bits)], value)
    return value


def own_bit(bit):
    return (lax.axis_index("dp") >> bit) & 1


def phase(*values):
    return lax.optimization_barrier(values)


class Order:
    def __init__(self, bits):
        self.bits, self.n = bits, 2 ** len(bits)

    def mask(self, place):
        return sum(((place >> k) & 1) << bit for k, bit in enumerate(self.bits))

    def source(self):
        rows = D // self.n
        place = jnp.arange(D, dtype=jnp.int32)
        block = self.mask(place // rows) ^ lax.axis_index("dp")
        return block * rows + place % rows

    def matrix(self):
        place = jnp.arange(D, dtype=jnp.int32)
        return (place[:, None] == self.source()[None, :]).astype(BF16)

    def where(self):
        other = jnp.arange(self.n, dtype=jnp.int32) ^ lax.axis_index("dp")
        return sum(((other >> bit) & 1) << k for k, bit in enumerate(self.bits))

    def places(self, count):
        return self.mask(jnp.arange(count, dtype=jnp.int32)) ^ lax.axis_index("dp")


class Gather:
    def __init__(self, shard, n):
        self.value, self.n = shard, n

    def step(self, bits):
        got = [swap(self.value, some, self.n) for some in subsets(bits)]
        self.value = jnp.concatenate([self.value, *got], axis=0)

    def cut(self, start, stop):
        return Gather(self.value[:, start:stop], self.n)


class Scatter:
    def __init__(self, kept, got, n):
        self.terms, self.n = [kept, got], n

    def away(self, bits):
        size = self.terms[0].shape[0] >> len(bits)
        parts = range(1, 2 ** len(bits))
        return [self.total([t[p * size : (p + 1) * size] for t in self.terms], BF16) for p in parts]

    def send(self, away, bits):
        got = [swap(part, some, self.n) for part, some in zip(away, subsets(bits))]
        self.terms = [t[: away[0].shape[0]] for t in self.terms] + got
        self.recent = len(got)

    def step(self, bits):
        self.send(self.away(bits), bits)

    @property
    def got(self):
        return self.terms[-self.recent :]

    @got.setter
    def got(self, values):
        self.terms[-self.recent :] = values

    def total(self, parts=None, kind=F32):
        parts = self.terms if parts is None else parts
        result = parts[0].astype(F32)
        for part in parts[1:]:
            result = result + part.astype(F32)
        return result.astype(kind)

    def join(self, other):
        self.terms = [jnp.concatenate([self.total(), other.total()], axis=1)]
        return self


def adapt(weight, grad, moment, square, decay):
    new_moment = 0.9 * moment + 0.1 * grad
    new_square = 0.999 * square + 0.001 * grad * grad
    update = new_moment / (1.0 - 0.9**STEP) / (jnp.sqrt(new_square / (1.0 - 0.999**STEP)) + 1e-06)
    return (new_moment, new_square, update + decay * weight)


def lane_sums(value):
    columns = jnp.sum(value * value, axis=0, keepdims=True)
    result = columns[:, :128]
    for start in range(128, value.shape[1], 128):
        result = result + columns[:, start : start + 128]
    return result


def adapt_kernel(first, *refs):
    before_ref, sums_ref = refs[8], refs[15]
    sums = before_ref[...]
    row = lax.broadcasted_iota(jnp.int32, sums.shape, 0)
    for i in range(2):
        weight_ref, grad_ref, moment_ref, square_ref = refs[i * 4 : i * 4 + 4]
        outs = refs[9 + i * 3 : 12 + i * 3]
        weight = weight_ref[...]
        values = adapt(weight, grad_ref[...], moment_ref[...], square_ref[...], 0.01)
        for out, value in zip(outs, values):
            out[...] = value
        sums = jnp.where(row == first + i, lane_sums(weight), sums)
        sums = jnp.where(row == 4 + first + i, lane_sums(values[2]), sums)
    sums_ref[...] = sums


def adapt_two(first, before, *operands):
    shapes = [jax.ShapeDtypeStruct(operands[i * 4].shape, F32) for i in (0, 0, 0, 1, 1, 1)]
    return pl.pallas_call(
        partial(adapt_kernel, first),
        out_shape=shapes + [jax.ShapeDtypeStruct((8, 128), F32)],
        compiler_params=pltpu.CompilerParams(vmem_limit_bytes=VMEM),
        cost_estimate=cost(2),
        name="adapt",
    )(*operands, before)


def renew_kernel(sums_ref, *refs):
    norms = jnp.sqrt(jnp.sum(sums_ref[...], axis=1, keepdims=True))
    refs[12][...] = jnp.broadcast_to(norms, (8, 128))
    for i in range(4):
        rate = 0.25 * (norms[i : i + 1] / norms[4 + i : 5 + i])
        refs[8 + i][...] = refs[i][...] - rate * refs[4 + i][...]


def renew(sums, weights, updates):
    return pl.pallas_call(
        renew_kernel,
        out_shape=[jax.ShapeDtypeStruct(weight.shape, F32) for weight in weights]
        + [jax.ShapeDtypeStruct((8, 128), F32)],
        compiler_params=pltpu.CompilerParams(vmem_limit_bytes=VMEM),
        cost_estimate=cost(2),
        name="renew",
    )(sums, *weights, *updates)


def body(
    n,
    frames,
    cotangent,
    lengths,
    w_qkv,
    w_attn,
    w_in,
    w_out,
    vectors,
    moment_qkv,
    moment_attn,
    moment_in,
    moment_out,
    moment_vec,
    square_qkv,
    square_attn,
    square_in,
    square_out,
    square_vec,
):
    rows_d, rows_f, width = w_qkv.shape[0], w_out.shape[0], vectors.shape[0]
    core, one, two, *others = range(n.bit_length() - 1)
    far = others[::-1]
    groups = [far[i : i + 2] for i in range(0, len(far), 2)]
    order_a, order_b = Order(far + [two, one, core]), Order(far + [one, two, core])
    x = frames[0]

    aligned = rows_d % 8 == 0
    half = w_qkv.shape[1] // 2
    tail = jnp.pad(vectors.reshape(rows_d, 12), ((0, 0), (0, 116)))
    low_qkv = jnp.concatenate([w_qkv, tail], axis=1).astype(BF16)
    low_qkv, *masters = phase(low_qkv, w_attn, w_in, w_out)
    low_in = jnp.concatenate(masters[:2], axis=1).astype(BF16)
    qkv, out = Gather(low_qkv, n), Gather(masters[2].astype(BF16), n)
    to_a, to_b = phase(order_a.matrix(), order_b.matrix())
    x_a, x_b = arrange(x, to_a), arrange(x, to_b)
    inner = Gather(low_in, n)
    if aligned:
        side = low_in.shape[1] // 2
        mine = own_bit(core)
        kept = lax.dynamic_slice_in_dim(low_in, mine * side, side, 1)
        got = swap(lax.dynamic_slice_in_dim(low_in, (1 - mine) * side, side, 1), [core], n)
        pair = [jnp.where(mine == 0, kept, got), jnp.where(mine == 0, got, kept)]
        inner.value = jnp.concatenate(pair, axis=0)
    else:
        attn_in = lax.all_gather(low_in, "dp", axis=0, tiled=True)
    for bits in groups:
        qkv.step(bits)
        qkv.value, inner.value = phase(qkv.value, inner.value)
    left, right = qkv.cut(0, half), qkv.cut(half, 2 * half + 128)
    out_left, out_right = out.cut(0, D // 2), out.cut(D // 2, D)
    if aligned:
        left.value = jnp.concatenate([left.value, out_left.value], axis=1)
        right.value = jnp.concatenate([right.value, out_right.value], axis=1)
    else:
        out_left.step([two])
        out_right.step([one])
    left.step([two])
    right.step([one])
    for bit in far[:1] if aligned else ():
        inner.step([bit])
    left.value, right.value, inner.value, x_a, x_b = phase(
        left.value, right.value, inner.value, x_a, x_b
    )
    if aligned:
        out_left, left = left.cut(half, half + D // 2), left.cut(0, half)
        out_right, right = right.cut(half + 128, half + 128 + D // 2), right.cut(0, half + 128)
    out = Gather(jnp.concatenate([out_left.value, out_right.value], axis=1), n)
    left.step([one])
    right.step([two])
    for bit in far[1:] if aligned else ():
        inner.step([bit])
    left.value, right.value, inner.value, out.value = phase(
        left.value, right.value, inner.value, out.value
    )
    left = (left.value, swap(left.value, [core], n))
    right = (right.value, swap(right.value, [core], n))
    cut = 1024 if aligned else low_in.shape[1]
    in_left, in_right = inner.cut(0, cut), inner.cut(cut, inner.value.shape[1])

    def in_step(bits_left, bits_right):
        if aligned:
            in_left.step(bits_left)
            in_right.step(bits_right)

    left, right, in_left.value, in_right.value, out.value = phase(
        left, right, in_left.value, in_right.value, out.value
    )
    in_step([two], [one])
    out.step(far[:1])
    vec_rows = jnp.concatenate([part[:, half:] for part in right], axis=0)
    vec = dot(to_b, vec_rows)[:, :12].reshape(12, D)

    packed = project(x_a, x_b, left, right, order_b.source())
    some = PAIRS // 6
    heads = attend(lengths, packed, 0, some)
    heads, in_left.value, in_right.value, out.value = phase(
        heads, in_left.value, in_right.value, out.value
    )
    in_step([one], [two])
    for bit in far[1:]:
        out.step([bit])
    heads = attend(lengths, packed, some, 3 * some, heads)
    heads, out.value, in_left.value, in_right.value = phase(
        heads, out.value, in_left.value, in_right.value
    )
    out_left, out_right = out.cut(0, D // 2), out.cut(D // 2, D)
    out_left.step([one])
    out_right.step([two])
    in_parts = [in_left.value, in_right.value]
    if aligned:
        in_parts = [in_parts[0], swap(in_parts[0], [core], n)] + [
            in_parts[1],
            swap(in_parts[1], [core], n),
        ]
    heads = attend(lengths, packed, 4 * some, 2 * some, heads)
    heads, vec, out_left.value, out_right.value, in_parts = phase(
        heads, vec, out_left.value, out_right.value, in_parts
    )
    out_parts = [out_left.value, out_right.value]
    out_parts += [swap(part, [core], n) for part in out_parts]
    out_a, out_b = Order([two, *far, one, core]), Order([one, *far, two, core])
    if aligned:
        chips_a, chips_b = [order.places(n // 2) // 2 for order in (order_a, order_b)]
        blocks_a, blocks_b = out_a.places(n), out_b.places(n)
        first = jnp.stack([mine, 1 - mine]) * (side // 128)
        corners = jnp.concatenate([first, first + cut // 128])
        columns = jnp.array([0, D // 256], jnp.int32)
        places = jnp.concatenate([chips_a, chips_b, blocks_a, blocks_b, corners, columns])
        base = 3 * n
        in_pieces = tuple((i // 2 * (n // 2), n // 2, base + i) for i in range(4))
        out_pieces = tuple(
            (n + i % 2 * n + i // 2 * (n // 2), n // 2, base + 4 + i % 2) for i in range(4)
        )
    else:
        sides = []
        for i, order in enumerate((out_a, out_b)):
            value = jnp.concatenate(out_parts[i::2], axis=0).reshape(n, rows_f, D // 2)
            sides.append(value[jnp.argsort(order.places(n))].reshape(FF, D // 2))
        in_parts, out_parts = [attn_in], [jnp.concatenate(sides, axis=1)]
        places = jnp.zeros((2,), jnp.int32)
        in_pieces = out_pieces = ((0, 1, 1),)
    ctx, ctxt, lse = heads

    where = order_b.where() if aligned else jnp.arange(CHUNKS, dtype=jnp.int32)
    mixed, dres1, dctx, sums, *grads = feed(
        *(lengths, x, ctx, cotangent[0], vec, to_a, to_b, places, where),
        *((in_parts, in_pieces), (out_parts, out_pieces)),
    )
    if not aligned:
        grad = jnp.concatenate(grads[:2], axis=0).reshape(n, rows_f, D)
        grads[:2] = jnp.split(grad[order_b.places(n)].reshape(FF, D), 2)
    sum_out = Scatter(grads[0], swap(grads[1], [core], n), n)
    sum_in = Scatter(grads[2], swap(grads[3], [core], n), n)

    sum_in.recent = sum_out.recent = 1
    dqkv, biases = None, []
    for first, count, bits in ((0, 1, (one, two)), (1, 4, (two, one)), (5, 1, None)):
        dqkv, bias = attend_back(lengths, packed, dctx, ctxt, lse, first, count, dqkv)
        biases.append(bias)
        if bits is not None:
            sum_in.got, sum_out.got, dqkv = phase(sum_in.got, sum_out.got, dqkv)
            sum_in.step([bits[0]])
            sum_out.step([bits[1]])
    full_qkv = jnp.concatenate(
        [
            arrange(to_a, jnp.concatenate(left, axis=0)),
            arrange(to_b, jnp.concatenate([part[:, :half] for part in right], axis=0)),
        ],
        axis=1,
    )
    dqkv, full_qkv, sum_in.got, sum_out.got = phase(
        dqkv, full_qkv, sum_in.got, sum_out.got
    )

    def late_grads(side):
        cols = slice(side * D // 2, (side + 1) * D // 2)
        queries, keys = [dot_tn(x_a[:, cols], dqkv[i]).astype(BF16) for i in range(2)]
        values = dot_tn(x_b[:, cols], dqkv[2]).astype(BF16)
        return (
            jnp.concatenate([queries, keys], axis=1),
            jnp.concatenate([values, grads[4 + side]], axis=1),
        )

    away_a, away_b = late_grads(1)
    away_a, away_b, dqkv, away_in, away_out = phase(
        away_a, away_b, dqkv, sum_in.away(others[:1]), sum_out.away(others[:1])
    )
    got_a, got_b = swap(away_a, [core], n), swap(away_b, [core], n)
    sum_in.send(away_in, others[:1])
    sum_out.send(away_out, others[:1])
    kept_a, kept_b = late_grads(0)
    got_a, got_b, kept_a, kept_b = phase(got_a, got_b, kept_a, kept_b)
    late_a, late_b = Scatter(kept_a, got_a, n), Scatter(kept_b, got_b, n)
    late_a.step([one])
    late_b.step([two])
    late_a.got, late_b.got, sum_in.got, sum_out.got = phase(
        late_a.got, late_b.got, sum_in.got, sum_out.got
    )
    away_a, away_b, *aways = phase(
        late_a.away([two]),
        late_b.away([one]),
        *((sum_in.away(others[1:2]), sum_out.away(others[1:2])) if others[1:] else ()),
    )
    late_a.send(away_a, [two])
    late_b.send(away_b, [one])
    for bit in others[1:2]:
        sum_in.send(aways[0], [bit])
        sum_out.send(aways[1], [bit])
    for bit in others[2:]:
        sum_in.step([bit])
        sum_out.step([bit])
    late_a.got, late_b.got = phase(late_a.got, late_b.got)
    late = late_a.join(late_b)
    late.step(others[:1])
    share_in, share_out = sum_in.total(), sum_out.total()
    late.got, share_in, share_out = phase(late.got, share_in, share_out)
    for bit in others[1:]:
        late.step([bit])
    share_late = late.total()
    bias_sums = jnp.concatenate(biases, axis=0)
    grad_vec = jnp.concatenate(
        [bias_sums[:, 0].reshape(1, D), bias_sums[:, 1].reshape(1, D), sums[2:]]
    ).reshape(-1, 128)
    input_grad = dres1
    for i in range(3):
        input_grad = input_grad + dot_nt(dqkv[i], full_qkv[:, i * D : (i + 1) * D])

    next_in = adapt_two(
        2,
        jnp.zeros((8, 128), F32),
        *(w_in, share_in, moment_in, square_in),
        *(w_out, share_out, moment_out, square_out),
    )
    next_attn = adapt_two(
        0,
        next_in[6],
        *(w_qkv, share_late[:, : 3 * D], moment_qkv, square_qkv),
        *(w_attn, share_late[:, 3 * D :], moment_attn, square_attn),
    )
    reduced = sum_all(jnp.concatenate([next_attn[6], grad_vec], axis=0), [[bit] for bit in range(n.bit_length() - 1)], n)
    place = lax.axis_index("dp") * width
    share_vec = lax.dynamic_slice_in_dim(reduced[8:].reshape(-1), place, width, 0)
    updates = (next_attn[2], next_attn[5], next_in[2], next_in[5])
    *new_weights, norms = renew(reduced[:8], (w_qkv, w_attn, w_in, w_out), updates)
    vec_moment, vec_square, vec_update = adapt(vectors, share_vec, moment_vec, square_vec, 0.0)
    return (
        mixed[None],
        input_grad[None],
        *new_weights,
        vectors - 0.4 * vec_update,
        *(next_attn[0], next_attn[3], next_in[0], next_in[3], vec_moment),
        *(next_attn[1], next_attn[4], next_in[1], next_in[4], vec_square),
        norms[:, 0],
    )


def solution(mesh):
    clips, matrix, vector = P("dp", None, None), P("dp", None), P("dp")
    parameters = (matrix,) * 4 + (vector,)
    return jax.shard_map(
        partial(body, mesh.shape["dp"]),
        mesh=mesh,
        in_specs=(clips, clips, vector) + parameters * 3,
        out_specs=(clips, clips) + parameters * 3 + (P(),),
        check_vma=False,
    )
```

```python
from functools import partial

import jax
import jax.numpy as jnp
from jax import lax
from jax.experimental import pallas as pl
from jax.experimental.pallas import tpu as pltpu
from jax.sharding import PartitionSpec as P

D = 768
FF = 3072
HEADS = 12
HEAD_DIM = 64
PAIRS = HEADS // 2
WIDE = 2 * HEAD_DIM
CHUNKS = FF // D
STEP = 10
MASKED = -1e9
VMEM = 56 * 2**20
ROOM = 24 * 2**20


BF16 = jnp.bfloat16
F32 = jnp.float32


def dot(a, b):
    return jnp.dot(a, b, preferred_element_type=F32)


def dot_nt(a, b):
    return lax.dot_general(a, b, (((1,), (1,)), ((), ())), preferred_element_type=F32)


def dot_tn(a, b):
    return lax.dot_general(a, b, (((0,), (0,)), ((), ())), preferred_element_type=F32)


def cost(us):
    return pl.CostEstimate(flops=int(us * 5.0e7), bytes_accessed=0, transcendentals=0)


def arrange(value, matrix):
    return dot(value, matrix).astype(BF16)


def project_kernel(*refs):
    xa_ref, xb_ref, la_ref, lb_ref, ra_ref, rb_ref, source_ref, lane_ref, out_ref, bias_ref = refs
    width = la_ref.shape[1]

    @pl.when(pl.program_id(0) == 0)
    def _():
        tail = jnp.concatenate([ra_ref[:, width:], rb_ref[:, width:]], axis=0)
        start = source_ref[...] * 12
        entry = lax.broadcasted_iota(jnp.int32, (D, D), 1)
        lane = lax.broadcasted_iota(jnp.int32, (128, D), 0)
        bias_ref[...] = jnp.zeros_like(bias_ref)
        for i in range(2):
            offset = entry + i * D - start
            picked = dot_tn(tail, jnp.where((offset >= 0) & (offset < 12), 1.0, 0.0).astype(BF16))
            picked = jnp.where(lane == lane_ref[i : i + 1, :], picked, 0.0)
            bias_ref[:, 2 * i * D : (2 * i + 1) * D] = jnp.sum(picked, axis=0, keepdims=True)

    left = jnp.concatenate([la_ref[...], lb_ref[...]], axis=0)
    out_ref[:, :width] = (dot(xa_ref[...], left) + bias_ref[:, :width]).astype(BF16)
    right = jnp.concatenate([ra_ref[:, :width], rb_ref[:, :width]], axis=0)
    out_ref[:, width:] = (dot(xb_ref[...], right) + bias_ref[:, width:]).astype(BF16)


def project(x_a, x_b, left, right, source):
    seq = x_a.shape[0]
    rows = min(512, seq)
    lanes = (jnp.arange(2 * D, dtype=jnp.int32) % 12).reshape(2, D)
    operands = (*left, *right, source.reshape(D, 1), lanes)

    def fixed(shape):
        return pl.BlockSpec(shape, lambda i: (0, 0), pipeline_mode=pl.Buffered(1))

    return pl.pallas_call(
        project_kernel,
        grid=(seq // rows,),
        in_specs=[pl.BlockSpec((rows, D), lambda i: (i, 0))] * 2
        + [fixed(part.shape) for part in operands],
        out_specs=pl.BlockSpec((rows, 3 * D), lambda i: (i, 0)),
        out_shape=jax.ShapeDtypeStruct((seq, 3 * D), BF16),
        scratch_shapes=[pltpu.VMEM((1, 3 * D), F32)],
        compiler_params=pltpu.CompilerParams(vmem_limit_bytes=ROOM),
        cost_estimate=cost(5),
        name="project",
    )(x_a, x_b, *operands)


def attend_kernel(len_ref, q_ref, k_ref, v_ref, ctx_ref, ctxt_ref, lse_ref):
    seq = q_ref.shape[0]
    qt = (q_ref[...].astype(F32) * 0.125).T.astype(BF16)
    vt = v_ref[...].astype(F32).T.astype(BF16)
    k = k_ref[...]
    keep = lax.broadcasted_iota(jnp.int32, (seq, seq), 0) < len_ref[0]
    zero = jnp.zeros((HEAD_DIM, seq), BF16)
    ones = jnp.ones((16, seq), BF16)
    for h in range(2):
        rows = slice(h * HEAD_DIM, (h + 1) * HEAD_DIM)
        q = jnp.concatenate([qt[rows], zero] if h == 0 else [zero, qt[rows]], axis=0)
        scores = jnp.where(keep, dot(k, q), MASKED)
        peak = jnp.max(scores, axis=0, keepdims=True)
        expo = jnp.exp(scores - peak).astype(BF16)
        both = dot(jnp.concatenate([vt[rows], ones], axis=0), expo)
        total = both[HEAD_DIM : HEAD_DIM + 1]
        ctxt_ref[rows, :] = both[:HEAD_DIM] / total
        lse_ref[0, h : h + 1, :] = peak + jnp.log(total)
    ctx_ref[...] = ctxt_ref[...].T.astype(BF16)


def after(kernel, first, count):
    def call(*refs):
        kernel(*refs[:first], *refs[first + count :])

    return call


def untouched(values):
    return [pl.BlockSpec(memory_space=pl.ANY)] * len(values)


def attend(lengths, packed, first, count, before=(), waits=()):
    seq = packed.shape[0]
    extra = (*before, *waits)
    return pl.pallas_call(
        after(attend_kernel, 4, len(extra)),
        grid_spec=pltpu.PrefetchScalarGridSpec(
            num_scalar_prefetch=1,
            grid=(count,),
            in_specs=[
                pl.BlockSpec((seq, WIDE), lambda p, _, i=i: (0, i * PAIRS + first + p))
                for i in range(3)
            ]
            + untouched(extra),
            out_specs=[
                pl.BlockSpec((seq, WIDE), lambda p, _: (0, first + p)),
                pl.BlockSpec((WIDE, seq), lambda p, _: (first + p, 0)),
                pl.BlockSpec((1, 2, seq), lambda p, _: (first + p, 0, 0)),
            ],
        ),
        out_shape=[
            jax.ShapeDtypeStruct((seq, D), BF16),
            jax.ShapeDtypeStruct((D, seq), F32),
            jax.ShapeDtypeStruct((PAIRS, 2, seq), F32),
        ],
        input_output_aliases={4 + i: i for i in range(len(before))},
        compiler_params=pltpu.CompilerParams(vmem_limit_bytes=ROOM),
        cost_estimate=cost(4 * count),
        name="attend",
    )(lengths, packed, packed, packed, *extra)


def attend_back_kernel(
    block, len_ref, q_ref, k_ref, v_ref, do_ref, ctxt_ref, lse_ref, out_ref, sum_ref, dqt_ref
):
    seq = q_ref.shape[0]
    q = q_ref[...].astype(F32) * 0.125
    qt = q.T.astype(BF16)
    q = q.astype(BF16)
    do = do_ref[...]
    dof = do.astype(F32).T
    dot_ = dof.astype(BF16)
    prod = dof * ctxt_ref[...]
    kt = k_ref[...].astype(F32).T.astype(BF16)
    row = lax.broadcasted_iota(jnp.int32, (HEAD_DIM, seq), 0)

    def pieces(vec):
        high = vec.astype(BF16).astype(F32)
        mid = (vec - high).astype(BF16).astype(F32)
        low = vec - high - mid
        picked = jnp.where(row == 1, mid, jnp.where(row == 2, low, 0.0))
        return jnp.where(row == 0, high, picked).astype(BF16)

    q_aug, do_aug, fill = [], [], []
    for h in range(2):
        rows = slice(h * HEAD_DIM, (h + 1) * HEAD_DIM)
        lse = lse_ref[0, h : h + 1]
        delta = jnp.sum(prod[rows], axis=0, keepdims=True)
        q_parts = [qt[rows], pieces(-lse)]
        do_parts = [dot_[rows], pieces(-delta)]
        q_aug.append(jnp.concatenate(q_parts if h == 0 else q_parts[::-1], axis=0))
        do_aug.append(jnp.concatenate(do_parts if h == 0 else do_parts[::-1], axis=0))
        fill.append(MASKED - lse)
    lane = lax.broadcasted_iota(jnp.int32, (block, WIDE), 1)
    mine = (lane < HEAD_DIM, lane >= HEAD_DIM)
    one = (
        jnp.where(lane < HEAD_DIM + 3, 1.0, 0.0).astype(BF16),
        jnp.where(lane < 3, 1.0, 0.0).astype(BF16),
    )
    for j in range(seq // block):
        rows = slice(j * block, (j + 1) * block)
        keep = lax.broadcasted_iota(jnp.int32, (block, seq), 0) + j * block < len_ref[0]
        k, v = k_ref[rows, :], v_ref[rows, :]
        dv, dk = [], []
        for h in range(2):
            heads = slice(h * HEAD_DIM, (h + 1) * HEAD_DIM)
            k_aug, v_aug = jnp.where(mine[h], k, one[h]), jnp.where(mine[h], v, one[h])
            prob = jnp.exp(jnp.where(keep, dot(k_aug, q_aug[h]), fill[h]))
            dscore = (prob * dot(v_aug, do_aug[h])).astype(BF16)
            dv.append(dot(prob.astype(BF16), do))
            dk.append(dot(dscore, q))
            dq = dot(kt[heads, rows], dscore)
            if j == 0:
                dqt_ref[heads, :] = dq
            else:
                dqt_ref[heads, :] += dq
        out_ref[1, rows, :] = jnp.where(mine[0], dk[0], dk[1]).astype(BF16)
        out_ref[2, rows, :] = jnp.where(mine[0], dv[0], dv[1]).astype(BF16)
    out_ref[0] = (dqt_ref[...] * 0.125).T.astype(BF16)
    sum_ref[0, 0:1] = jnp.sum(out_ref[0].astype(F32), axis=0, keepdims=True)
    sum_ref[0, 1:2] = jnp.sum(out_ref[2].astype(F32), axis=0, keepdims=True)


def attend_back(lengths, packed, dctx, ctxt, lse, first, count, before=None, waits=()):
    seq = packed.shape[0]
    extra = tuple(waits) if before is None else (before, *waits)
    return pl.pallas_call(
        after(partial(attend_back_kernel, min(512, seq)), 7, len(extra)),
        grid_spec=pltpu.PrefetchScalarGridSpec(
            num_scalar_prefetch=1,
            grid=(count,),
            in_specs=[
                pl.BlockSpec((seq, WIDE), lambda p, _, i=i: (0, i * PAIRS + first + p))
                for i in range(3)
            ]
            + [
                pl.BlockSpec((seq, WIDE), lambda p, _: (0, first + p)),
                pl.BlockSpec((WIDE, seq), lambda p, _: (first + p, 0)),
                pl.BlockSpec((1, 2, seq), lambda p, _: (first + p, 0, 0)),
            ]
            + untouched(extra),
            out_specs=[
                pl.BlockSpec((3, seq, WIDE), lambda p, _: (0, 0, first + p)),
                pl.BlockSpec((1, 2, WIDE), lambda p, _: (p, 0, 0)),
            ],
            scratch_shapes=[pltpu.VMEM((WIDE, seq), F32)],
        ),
        out_shape=[
            jax.ShapeDtypeStruct((3, seq, D), BF16),
            jax.ShapeDtypeStruct((count, 2, WIDE), F32),
        ],
        input_output_aliases={} if before is None else {7: 0},
        compiler_params=pltpu.CompilerParams(vmem_limit_bytes=ROOM),
        cost_estimate=cost(6 * count),
        name="attend_back",
    )(lengths, packed, packed, packed, dctx, ctxt, lse, *extra)


def normal_parts(u):
    return 0.5 + 0.5 * lax.erf(u * 0.7071067811865476), jnp.exp(-0.5 * u * u)


def norm_forward(resid):
    center = resid - jnp.mean(resid, axis=-1, keepdims=True)
    inverse = lax.rsqrt(jnp.mean(center * center, axis=-1, keepdims=True) + 1e-05)
    return center * inverse, inverse


def norm_back(grad, gain, unit, inverse):
    du = grad * gain
    mean = jnp.mean(du, axis=-1, keepdims=True)
    return inverse * (du - mean - unit * jnp.mean(du * unit, axis=-1, keepdims=True))


def column_sum(value):
    return jnp.sum(value.astype(F32), axis=0, keepdims=True)


def waited(copies):
    for copy in copies:
        copy.wait()


def feed_kernel(in_pieces, out_pieces, steps, *refs):
    len_ref, place_ref, where_ref, x_ref, ctx_ref, cot_ref, vec_ref, to_a_ref, to_b_ref = refs[:9]
    in_parts, refs = refs[9 : 9 + len(in_pieces)], refs[9 + len(in_pieces) :]
    out_parts, refs = refs[: len(out_pieces)], refs[len(out_pieces) :]
    mixed_ref, dres1_ref, dctx_ref, sum_ref, *grads = refs[:10]
    out_grads, in_grads, attn_grads = grads[:2], grads[2:4], grads[4:6]
    w_ref, w2_ref, act_ref, dhid_ref, first_ref, ctxb_ref, dbr_ref, dres_ref = refs[10:18]
    unit_ref, inverse_ref, slope_ref, held_ref, in_sems, part_sems, out_sems = refs[18:]
    step = pl.program_id(0)
    size = x_ref.shape[0]
    blocks = where_ref.shape[0] // CHUNKS
    first_grad, second_grad = steps, steps + CHUNKS
    back, last = steps + 2 * CHUNKS, 2 * steps + 2 * CHUNKS

    def vec(i):
        return vec_ref[i : i + 1, :]

    def weight(c):
        return w_ref.at[:, c * D : (c + 1) * D]

    def part_copies(whole_ref, parts, pieces, sems):
        made, total = [], 0
        for part, (first, count, column) in zip(parts, pieces):
            rows, width = part.shape[0] // count, part.shape[1]
            columns = pl.ds(pl.multiple_of(place_ref[column] * 128, 128), width)
            for i in range(count):
                where = pl.multiple_of(place_ref[first + i] * rows, rows)
                target = whole_ref.at[pl.ds(where, rows), columns]
                source = part.at[pl.ds(i * rows, rows), :]
                made.append(pltpu.make_async_copy(source, target, sems.at[total]))
                total += 1
        return made

    early = sum(count for _, count, _ in in_pieces[: max(1, len(in_pieces) // 2)])

    def in_weights():
        return part_copies(w_ref, in_parts, in_pieces, in_sems)

    def out_weights():
        return part_copies(w2_ref, out_parts, out_pieces, part_sems)

    @pl.when(step == 0)
    def _():
        for copy in in_weights() + out_weights():
            copy.start()
        sum_ref[...] = jnp.zeros_like(sum_ref)

    @pl.when(step < steps)
    def _():
        rows = pl.ds(pl.multiple_of(step * size, size), size)

        @pl.when(step == 0)
        def _():
            waited(in_weights()[:early])

        resid = x_ref[...].astype(F32) + (dot(ctx_ref[...], weight(0)[...]) + vec(2))
        unit1, inverse1 = norm_forward(resid)
        unit_ref[rows, :] = unit1
        inverse_ref[rows, :] = jnp.broadcast_to(inverse1, (size, 128))
        first = unit1 * vec(3) + vec(4)
        first_b = first.astype(BF16)
        first_ref[rows, :] = arrange(first_b, to_a_ref[...])
        ctxb_ref[rows, :] = arrange(ctx_ref[...], to_b_ref[...])

        @pl.when(step == 0)
        def _():
            waited(in_weights()[early:] + out_weights())

        branch = None
        for c in range(CHUNKS):
            cols = slice(c * D, (c + 1) * D)
            hidden = dot(first_b, weight(1 + c)[...]) + vec(5 + c)
            phi, bell = normal_parts(hidden)
            active = (hidden * phi).astype(BF16)
            act_ref[rows, cols] = active
            slope_ref[:, cols] = phi + hidden * bell * 0.3989422804014327
            part = dot(active, w2_ref[cols, :])
            branch = part if branch is None else branch + part
        unit2, inverse2 = norm_forward(first + (branch + vec(9)))
        place = lax.broadcasted_iota(jnp.int32, (size, 1), 0) + step * size
        keep = (place < len_ref[0]).astype(F32)
        mixed_ref[...] = ((unit2 * vec(10) + vec(11)) * keep).astype(BF16)
        dz = cot_ref[...].astype(F32) * keep
        dres2 = norm_back(dz, vec(10), unit2, inverse2)
        dres_ref[rows, :] = dres2
        dbranch = dres2.astype(BF16)
        dbr_ref[rows, :] = dbranch
        sum_ref[9:10, :] += column_sum(dbranch)
        sum_ref[10:11, :] += column_sum(dz * unit2)
        sum_ref[11:12, :] += column_sum(dz)
        for c in range(CHUNKS):
            cols = slice(c * D, (c + 1) * D)
            dhidden = (dot_nt(dbranch, w2_ref[cols, :]) * slope_ref[:, cols]).astype(BF16)
            dhid_ref[rows, cols] = dhidden
            sum_ref[5 + c : 6 + c, :] += column_sum(dhidden)

    def out_copies(step, go):
        chunk = step - first_grad
        slot = lax.rem(chunk, 2)
        rows = D // blocks
        for i in range(blocks):
            place = where_ref[chunk * blocks + i]
            source = held_ref.at[slot, pl.ds(i * rows, rows), :]
            for half in range(2):
                where = pl.multiple_of((place - half * 2 * blocks) * rows, rows)

                @pl.when((place >= 2 * blocks) == (half == 1))
                def _(half=half, where=where, source=source, i=i):
                    target = out_grads[half].at[pl.ds(where, rows), :]
                    go(pltpu.make_async_copy(source, target, out_sems.at[slot, i]))

    def in_copies(step, grads, column):
        slot = lax.rem(step - first_grad, 2)
        made = []
        for half in range(2):
            source = held_ref.at[slot, pl.ds(half * D // 2, D // 2), :]
            target = grads[half].at[:, pl.ds(column, D)]
            made.append(pltpu.make_async_copy(source, target, out_sems.at[slot, half]))
        return made

    def in_column(step):
        return pl.multiple_of((step - second_grad) * D, D)

    def start(copy):
        copy.start()

    def wait(copy):
        copy.wait()

    @pl.when((step >= first_grad) & (step < second_grad))
    def _():
        @pl.when(step >= first_grad + 2)
        def _():
            out_copies(step - 2, wait)

        cols = pl.ds(pl.multiple_of((step - first_grad) * D, D), D)
        grad = dot_tn(act_ref[:, cols], dbr_ref[...]).astype(BF16)
        held_ref[lax.rem(step - first_grad, 2)] = grad
        out_copies(step, start)

    @pl.when((step >= second_grad) & (step < back))
    def _():
        @pl.when(step < second_grad + 2)
        def _():
            out_copies(step - 2, wait)

        @pl.when(step >= second_grad + 2)
        def _():
            waited(in_copies(step - 2, in_grads, in_column(step - 2)))

        cols = pl.ds(in_column(step), D)
        grad = dot_tn(first_ref[...], dhid_ref[:, cols]).astype(BF16)
        held_ref[lax.rem(step - first_grad, 2)] = grad
        for copy in in_copies(step, in_grads, in_column(step)):
            copy.start()

    @pl.when((step >= back) & (step < last))
    def _():
        rows = pl.ds(pl.multiple_of((step - back) * size, size), size)
        dfirst = dres_ref[rows, :]
        for c in range(CHUNKS):
            dfirst = dfirst + dot_nt(dhid_ref[rows, c * D : (c + 1) * D], weight(1 + c)[...])
        unit = unit_ref[rows, :]
        dres1 = norm_back(dfirst, vec(3), unit, inverse_ref[rows, 0:1])
        dres1_ref[...] = dres1
        dattend = dres1.astype(BF16)
        dbr_ref[rows, :] = dattend
        dctx_ref[...] = dot_nt(dattend, weight(0)[...]).astype(BF16)
        sum_ref[2:3, :] += column_sum(dattend)
        sum_ref[3:4, :] += column_sum(dfirst * unit)
        sum_ref[4:5, :] += column_sum(dfirst)

    @pl.when(step == last)
    def _():
        waited(in_copies(back - 2, in_grads, in_column(back - 2)))
        waited(in_copies(back - 1, in_grads, in_column(back - 1)))
        held_ref[0] = dot_tn(ctxb_ref[...], dbr_ref[...]).astype(BF16)
        copies = in_copies(first_grad, attn_grads, 0)
        for copy in copies:
            copy.start()
        waited(copies)


def feed(lengths, x, ctx, cot, vec, to_a, to_b, places, where, in_side, out_side):
    (in_parts, in_pieces), (out_parts, out_pieces) = in_side, out_side
    seq = x.shape[0]
    size = min(256, seq)
    steps = seq // size
    back = steps + 2 * CHUNKS
    anywhere = pl.BlockSpec(memory_space=pl.ANY)

    def early(width):
        return pl.BlockSpec((size, width), lambda i, *_: (jnp.minimum(i, steps - 1), 0))

    def late(width):
        return pl.BlockSpec((size, width), lambda i, *_: (jnp.clip(i - back, 0, steps - 1), 0))

    def fixed(shape):
        return pl.BlockSpec(shape, lambda i, *_: (0, 0), pipeline_mode=pl.Buffered(1))

    shape = jax.ShapeDtypeStruct
    return pl.pallas_call(
        partial(feed_kernel, in_pieces, out_pieces, steps),
        grid_spec=pltpu.PrefetchScalarGridSpec(
            num_scalar_prefetch=3,
            grid=(2 * steps + 2 * CHUNKS + 1,),
            in_specs=[early(D)] * 3
            + [fixed((12, D)), fixed((D, D)), fixed((D, D))]
            + untouched(in_parts)
            + untouched(out_parts),
            out_specs=[early(D), late(D), late(D), pl.BlockSpec((12, D), lambda i, *_: (0, 0))]
            + [anywhere] * 6,
            scratch_shapes=[
                pltpu.VMEM((D, D + FF), BF16),
                pltpu.VMEM((FF, D), BF16),
                pltpu.VMEM((seq, FF), BF16),
                pltpu.VMEM((seq, FF), BF16),
                pltpu.VMEM((seq, D), BF16),
                pltpu.VMEM((seq, D), BF16),
                pltpu.VMEM((seq, D), BF16),
                pltpu.VMEM((seq, D), F32),
                pltpu.VMEM((seq, D), F32),
                pltpu.VMEM((seq, 128), F32),
                pltpu.VMEM((size, FF), F32),
                pltpu.VMEM((2, D, D), BF16),
                pltpu.SemaphoreType.DMA((sum(count for _, count, _ in in_pieces),)),
                pltpu.SemaphoreType.DMA((sum(count for _, count, _ in out_pieces),)),
                pltpu.SemaphoreType.DMA((2, max(2, where.shape[0] // CHUNKS))),
            ],
        ),
        out_shape=[
            shape((seq, D), BF16),
            shape((seq, D), F32),
            shape((seq, D), BF16),
            shape((12, D), F32),
        ]
        + [shape((FF // 2, D), BF16)] * 2
        + [shape((D // 2, FF), BF16)] * 2
        + [shape((D // 2, D), BF16)] * 2,
        compiler_params=pltpu.CompilerParams(vmem_limit_bytes=VMEM),
        cost_estimate=cost(50),
        name="feed",
    )(lengths, places, where, x, ctx, cot, vec, to_a, to_b, *in_parts, *out_parts)


def swap(value, bits, n):
    mask = sum(1 << bit for bit in bits)
    return lax.ppermute(value, "dp", [(i, i ^ mask) for i in range(n)])


def subsets(bits):
    return [[bit for k, bit in enumerate(bits) if p >> k & 1] for p in range(1, 2 ** len(bits))]


def sum_all(value, groups, n):
    for bits in groups:
        value = sum([swap(value, some, n) for some in subsets(bits)], value)
    return value


def own_bit(bit):
    return (lax.axis_index("dp") >> bit) & 1


def phase(*values):
    return lax.optimization_barrier(values)


class Order:
    def __init__(self, bits):
        self.bits, self.n = bits, 2 ** len(bits)

    def mask(self, place):
        return sum(((place >> k) & 1) << bit for k, bit in enumerate(self.bits))

    def source(self):
        rows = D // self.n
        place = jnp.arange(D, dtype=jnp.int32)
        block = self.mask(place // rows) ^ lax.axis_index("dp")
        return block * rows + place % rows

    def matrix(self):
        place = jnp.arange(D, dtype=jnp.int32)
        return (place[:, None] == self.source()[None, :]).astype(BF16)

    def where(self):
        other = jnp.arange(self.n, dtype=jnp.int32) ^ lax.axis_index("dp")
        return sum(((other >> bit) & 1) << k for k, bit in enumerate(self.bits))

    def places(self, count):
        return self.mask(jnp.arange(count, dtype=jnp.int32)) ^ lax.axis_index("dp")


class Gather:
    def __init__(self, shard, n):
        self.value, self.n = shard, n

    def step(self, bits):
        got = [swap(self.value, some, self.n) for some in subsets(bits)]
        self.value = jnp.concatenate([self.value, *got], axis=0)

    def cut(self, start, stop):
        return Gather(self.value[:, start:stop], self.n)


class Scatter:
    def __init__(self, kept, got, n):
        self.terms, self.n = [kept, got], n

    def away(self, bits):
        size = self.terms[0].shape[0] >> len(bits)
        parts = range(1, 2 ** len(bits))
        return [self.total([t[p * size : (p + 1) * size] for t in self.terms], BF16) for p in parts]

    def send(self, away, bits):
        got = [swap(part, some, self.n) for part, some in zip(away, subsets(bits))]
        self.terms = [t[: away[0].shape[0]] for t in self.terms] + got
        self.recent = len(got)

    def step(self, bits):
        self.send(self.away(bits), bits)

    @property
    def got(self):
        return self.terms[-self.recent :]

    @got.setter
    def got(self, values):
        self.terms[-self.recent :] = values

    def total(self, parts=None, kind=F32):
        parts = self.terms if parts is None else parts
        result = parts[0].astype(F32)
        for part in parts[1:]:
            result = result + part.astype(F32)
        return result.astype(kind)

    def join(self, other):
        self.terms = [jnp.concatenate([self.total(), other.total()], axis=1)]
        return self


def adapt(weight, grad, moment, square, decay):
    new_moment = 0.9 * moment + 0.1 * grad
    new_square = 0.999 * square + 0.001 * grad * grad
    update = new_moment / (1.0 - 0.9**STEP) / (jnp.sqrt(new_square / (1.0 - 0.999**STEP)) + 1e-06)
    return (new_moment, new_square, update + decay * weight)


def lane_sums(value):
    columns = jnp.sum(value * value, axis=0, keepdims=True)
    result = columns[:, :128]
    for start in range(128, value.shape[1], 128):
        result = result + columns[:, start : start + 128]
    return result


def adapt_kernel(first, columns, *refs):
    before_ref, sums_ref = refs[8], refs[15]
    sums = before_ref[:8, :]
    row = lax.broadcasted_iota(jnp.int32, sums.shape, 0)
    for i in range(2):
        weight_ref, grad_ref, moment_ref, square_ref = refs[i * 4 : i * 4 + 4]
        outs = refs[9 + i * 3 : 12 + i * 3]
        weight = weight_ref[...]
        grad = grad_ref[:, columns[i] : columns[i] + weight.shape[1]]
        values = adapt(weight, grad, moment_ref[...], square_ref[...], 0.01)
        for out, value in zip(outs, values):
            out[...] = value
        sums = jnp.where(row == first + i, lane_sums(weight), sums)
        sums = jnp.where(row == 4 + first + i, lane_sums(values[2]), sums)
    sums_ref[:8, :] = sums
    if sums_ref.shape[0] > 8:
        sums_ref[8:, :] = before_ref[8:, :]


def adapt_two(first, columns, before, *operands):
    shapes = [jax.ShapeDtypeStruct(operands[i * 4].shape, F32) for i in (0, 0, 0, 1, 1, 1)]
    return pl.pallas_call(
        partial(adapt_kernel, first, columns),
        out_shape=shapes + [jax.ShapeDtypeStruct(before.shape, F32)],
        compiler_params=pltpu.CompilerParams(vmem_limit_bytes=ROOM),
        cost_estimate=cost(2),
        name="adapt",
    )(*operands, before)


def renew_kernel(sums_ref, *refs):
    norms = jnp.sqrt(jnp.sum(sums_ref[:8, :], axis=1, keepdims=True))
    refs[12][...] = jnp.broadcast_to(norms, (8, 128)).T[:1, :]
    for i in range(4):
        rate = 0.25 * (norms[i : i + 1] / norms[4 + i : 5 + i])
        refs[8 + i][...] = refs[i][...] - rate * refs[4 + i][...]


def renew(sums, weights, updates):
    return pl.pallas_call(
        renew_kernel,
        out_shape=[jax.ShapeDtypeStruct(weight.shape, F32) for weight in weights]
        + [jax.ShapeDtypeStruct((1, 8), F32)],
        compiler_params=pltpu.CompilerParams(vmem_limit_bytes=ROOM),
        cost_estimate=cost(2),
        name="renew",
    )(sums, *weights, *updates)


def body(
    n,
    frames,
    cotangent,
    lengths,
    w_qkv,
    w_attn,
    w_in,
    w_out,
    vectors,
    moment_qkv,
    moment_attn,
    moment_in,
    moment_out,
    moment_vec,
    square_qkv,
    square_attn,
    square_in,
    square_out,
    square_vec,
):
    rows_d, rows_f, width = w_qkv.shape[0], w_out.shape[0], vectors.shape[0]
    core, one, two, *others = range(n.bit_length() - 1)
    far = others[::-1]
    groups = [far[i : i + 2] for i in range(0, len(far), 2)]
    order_a, order_b = Order(far + [two, one, core]), Order(far + [one, two, core])
    x = frames[0]

    aligned = rows_d % 8 == 0
    half = w_qkv.shape[1] // 2
    tail = jnp.pad(vectors.reshape(rows_d, 12), ((0, 0), (0, 116)))
    low_qkv = jnp.concatenate([w_qkv, tail], axis=1).astype(BF16)
    low_qkv, *masters = phase(low_qkv, w_attn, w_in, w_out)
    low_in = jnp.concatenate(masters[:2], axis=1).astype(BF16)
    qkv, out = Gather(low_qkv, n), Gather(masters[2].astype(BF16), n)
    to_a, to_b = phase(order_a.matrix(), order_b.matrix())
    x_a, x_b = arrange(x, to_a), arrange(x, to_b)
    inner = Gather(low_in, n)
    if aligned:
        side = low_in.shape[1] // 2
        mine = own_bit(core)
        kept = lax.dynamic_slice_in_dim(low_in, mine * side, side, 1)
        got = swap(lax.dynamic_slice_in_dim(low_in, (1 - mine) * side, side, 1), [core], n)
        pair = [jnp.where(mine == 0, kept, got), jnp.where(mine == 0, got, kept)]
        inner.value = jnp.concatenate(pair, axis=0)
    else:
        attn_in = lax.all_gather(low_in, "dp", axis=0, tiled=True)
    for bits in groups:
        qkv.step(bits)
        qkv.value, inner.value = phase(qkv.value, inner.value)
    left, right = qkv.cut(0, half), qkv.cut(half, 2 * half + 128)
    out_left, out_right = out.cut(0, D // 2), out.cut(D // 2, D)
    if aligned:
        left.value = jnp.concatenate([left.value, out_left.value], axis=1)
        right.value = jnp.concatenate([right.value, out_right.value], axis=1)
    else:
        out_left.step([two])
        out_right.step([one])
    left.step([two])
    right.step([one])
    for bit in far[:1] if aligned else ():
        inner.step([bit])
    left.value, right.value, inner.value, x_a, x_b = phase(
        left.value, right.value, inner.value, x_a, x_b
    )
    if aligned:
        out_left, left = left.cut(half, half + D // 2), left.cut(0, half)
        out_right, right = right.cut(half + 128, half + 128 + D // 2), right.cut(0, half + 128)
    out = Gather(jnp.concatenate([out_left.value, out_right.value], axis=1), n)
    left.step([one])
    right.step([two])
    for bit in far[1:] if aligned else ():
        inner.step([bit])
    left.value, right.value, inner.value, out.value = phase(
        left.value, right.value, inner.value, out.value
    )
    left = (left.value, swap(left.value, [core], n))
    right = (right.value, swap(right.value, [core], n))
    cut = 1024 if aligned else low_in.shape[1]
    in_left, in_right = inner.cut(0, cut), inner.cut(cut, inner.value.shape[1])

    def in_step(bits_left, bits_right):
        if aligned:
            in_left.step(bits_left)
            in_right.step(bits_right)

    left, right, in_left.value, in_right.value, out.value = phase(
        left, right, in_left.value, in_right.value, out.value
    )
    in_step([two], [one])
    out.step(far[:1])
    vec_rows = jnp.concatenate([part[:, half:] for part in right], axis=0)
    vec = dot(to_b, vec_rows)[:, :12].reshape(12, D)

    packed = project(x_a, x_b, left, right, order_b.source())
    some = PAIRS // 6
    heads = attend(lengths, packed, 0, some)
    heads, in_left.value, in_right.value, out.value = phase(
        heads, in_left.value, in_right.value, out.value
    )
    in_step([one], [two])
    for bit in far[1:]:
        out.step([bit])
    heads = attend(lengths, packed, some, 3 * some, heads)
    heads, out.value, in_left.value, in_right.value = phase(
        heads, out.value, in_left.value, in_right.value
    )
    out_left, out_right = out.cut(0, D // 2), out.cut(D // 2, D)
    out_left.step([one])
    out_right.step([two])
    in_parts = [in_left.value, in_right.value]
    if aligned:
        in_parts = [in_parts[0], swap(in_parts[0], [core], n)] + [
            in_parts[1],
            swap(in_parts[1], [core], n),
        ]
    heads = attend(lengths, packed, 4 * some, 2 * some, heads)
    heads, vec, out_left.value, out_right.value, in_parts = phase(
        heads, vec, out_left.value, out_right.value, in_parts
    )
    out_parts = [out_left.value, out_right.value]
    out_parts += [swap(part, [core], n) for part in out_parts]
    out_a, out_b = Order([two, *far, one, core]), Order([one, *far, two, core])
    if aligned:
        chips_a, chips_b = [order.places(n // 2) // 2 for order in (order_a, order_b)]
        blocks_a, blocks_b = out_a.places(n), out_b.places(n)
        first = jnp.stack([mine, 1 - mine]) * (side // 128)
        corners = jnp.concatenate([first, first + cut // 128])
        columns = jnp.array([0, D // 256], jnp.int32)
        places = jnp.concatenate([chips_a, chips_b, blocks_a, blocks_b, corners, columns])
        base = 3 * n
        in_pieces = tuple((i // 2 * (n // 2), n // 2, base + i) for i in range(4))
        out_pieces = tuple(
            (n + i % 2 * n + i // 2 * (n // 2), n // 2, base + 4 + i % 2) for i in range(4)
        )
    else:
        sides = []
        for i, order in enumerate((out_a, out_b)):
            value = jnp.concatenate(out_parts[i::2], axis=0).reshape(n, rows_f, D // 2)
            sides.append(value[jnp.argsort(order.places(n))].reshape(FF, D // 2))
        in_parts, out_parts = [attn_in], [jnp.concatenate(sides, axis=1)]
        places = jnp.zeros((2,), jnp.int32)
        in_pieces = out_pieces = ((0, 1, 1),)
    ctx, ctxt, lse = heads

    where = order_b.where() if aligned else jnp.arange(CHUNKS, dtype=jnp.int32)
    mixed, dres1, dctx, sums, *grads = feed(
        *(lengths, x, ctx, cotangent[0], vec, to_a, to_b, places, where),
        *((in_parts, in_pieces), (out_parts, out_pieces)),
    )
    if not aligned:
        grad = jnp.concatenate(grads[:2], axis=0).reshape(n, rows_f, D)
        grads[:2] = jnp.split(grad[order_b.places(n)].reshape(FF, D), 2)
    sum_out = Scatter(grads[0], swap(grads[1], [core], n), n)
    sum_in = Scatter(grads[2], swap(grads[3], [core], n), n)

    sum_in.recent = sum_out.recent = 1
    dqkv, biases = None, []
    for first, count, bits in ((0, 1, (one, two)), (1, 4, (two, one)), (5, 1, None)):
        dqkv, bias = attend_back(lengths, packed, dctx, ctxt, lse, first, count, dqkv)
        biases.append(bias)
        if bits is not None:
            sum_in.got, sum_out.got, dqkv = phase(sum_in.got, sum_out.got, dqkv)
            sum_in.step([bits[0]])
            sum_out.step([bits[1]])
    full_qkv = jnp.concatenate(
        [
            arrange(to_a, jnp.concatenate(left, axis=0)),
            arrange(to_b, jnp.concatenate([part[:, :half] for part in right], axis=0)),
        ],
        axis=1,
    )
    dqkv, full_qkv, sum_in.got, sum_out.got = phase(
        dqkv, full_qkv, sum_in.got, sum_out.got
    )

    def late_grads(side):
        cols = slice(side * D // 2, (side + 1) * D // 2)
        queries, keys = [dot_tn(x_a[:, cols], dqkv[i]).astype(BF16) for i in range(2)]
        values = dot_tn(x_b[:, cols], dqkv[2]).astype(BF16)
        return (
            jnp.concatenate([queries, keys], axis=1),
            jnp.concatenate([values, grads[4 + side]], axis=1),
        )

    away_a, away_b = late_grads(1)
    away_a, away_b, dqkv, away_in, away_out = phase(
        away_a, away_b, dqkv, sum_in.away(others[:1]), sum_out.away(others[:1])
    )
    got_a, got_b = swap(away_a, [core], n), swap(away_b, [core], n)
    sum_in.send(away_in, others[:1])
    sum_out.send(away_out, others[:1])
    kept_a, kept_b = late_grads(0)
    got_a, got_b, kept_a, kept_b = phase(got_a, got_b, kept_a, kept_b)
    late_a, late_b = Scatter(kept_a, got_a, n), Scatter(kept_b, got_b, n)
    late_a.step([one])
    late_b.step([two])
    late_a.got, late_b.got, sum_in.got, sum_out.got = phase(
        late_a.got, late_b.got, sum_in.got, sum_out.got
    )
    away_a, away_b, *aways = phase(
        late_a.away([two]),
        late_b.away([one]),
        *((sum_in.away(others[1:2]), sum_out.away(others[1:2])) if others[1:] else ()),
    )
    late_a.send(away_a, [two])
    late_b.send(away_b, [one])
    for bit in others[1:2]:
        sum_in.send(aways[0], [bit])
        sum_out.send(aways[1], [bit])
    for bit in others[2:]:
        sum_in.step([bit])
        sum_out.step([bit])
    late_a.got, late_b.got = phase(late_a.got, late_b.got)
    late = late_a.join(late_b)
    late.step(others[:1])
    share_in, share_out = sum_in.total(), sum_out.total()
    late.got, share_in, share_out = phase(late.got, share_in, share_out)
    for bit in others[1:]:
        late.step([bit])
    share_late = late.total()
    bias_sums = jnp.concatenate(biases, axis=0)
    grad_vec = jnp.concatenate(
        [bias_sums[:, 0].reshape(1, D), bias_sums[:, 1].reshape(1, D), sums[2:]]
    ).reshape(-1, 128)
    input_grad = dres1
    for i in range(3):
        input_grad = input_grad + dot_nt(dqkv[i], full_qkv[:, i * D : (i + 1) * D])

    next_in = adapt_two(
        2,
        (0, 0),
        jnp.concatenate([jnp.zeros((8, 128), F32), grad_vec], axis=0),
        *(w_in, share_in, moment_in, square_in),
        *(w_out, share_out, moment_out, square_out),
    )
    next_attn = adapt_two(
        0,
        (0, 3 * D),
        next_in[6],
        *(w_qkv, share_late, moment_qkv, square_qkv),
        *(w_attn, share_late, moment_attn, square_attn),
    )
    reduced = sum_all(next_attn[6], [[bit] for bit in range(n.bit_length() - 1)], n)
    place = lax.axis_index("dp") * width
    share_vec = lax.dynamic_slice_in_dim(reduced[8:].reshape(-1), place, width, 0)
    updates = (next_attn[2], next_attn[5], next_in[2], next_in[5])
    *new_weights, norms = renew(reduced, (w_qkv, w_attn, w_in, w_out), updates)
    vec_moment, vec_square, vec_update = adapt(vectors, share_vec, moment_vec, square_vec, 0.0)
    return (
        mixed[None],
        input_grad[None],
        *new_weights,
        vectors - 0.4 * vec_update,
        *(next_attn[0], next_attn[3], next_in[0], next_in[3], vec_moment),
        *(next_attn[1], next_attn[4], next_in[1], next_in[4], vec_square),
        norms.reshape(8),
    )


def solution(mesh):
    clips, matrix, vector = P("dp", None, None), P("dp", None), P("dp")
    parameters = (matrix,) * 4 + (vector,)
    return jax.shard_map(
        partial(body, mesh.shape["dp"]),
        mesh=mesh,
        in_specs=(clips, clips, vector) + parameters * 3,
        out_specs=(clips, clips) + parameters * 3 + (P(),),
        check_vma=False,
    )
```

```python
from functools import partial

import jax
import jax.numpy as jnp
from jax import lax
from jax.experimental import pallas as pl
from jax.experimental.pallas import tpu as pltpu
from jax.sharding import PartitionSpec as P

D = 768
FF = 3072
HEADS = 12
HEAD_DIM = 64
PAIRS = HEADS // 2
WIDE = 2 * HEAD_DIM
CHUNKS = FF // D
STEP = 10
MASKED = -1e9
VMEM = 56 * 2**20
ROOM = 24 * 2**20


BF16 = jnp.bfloat16
F32 = jnp.float32


def dot(a, b):
    return jnp.dot(a, b, preferred_element_type=F32)


def dot_nt(a, b):
    return lax.dot_general(a, b, (((1,), (1,)), ((), ())), preferred_element_type=F32)


def dot_tn(a, b):
    return lax.dot_general(a, b, (((0,), (0,)), ((), ())), preferred_element_type=F32)


def cost(us):
    return pl.CostEstimate(flops=int(us * 5.0e7), bytes_accessed=0, transcendentals=0)


def arrange(value, matrix):
    return dot(value, matrix).astype(BF16)


def project_kernel(*refs):
    xa_ref, xb_ref, la_ref, lb_ref, ra_ref, rb_ref, source_ref, lane_ref, out_ref, bias_ref = refs
    width = la_ref.shape[1]

    @pl.when(pl.program_id(0) == 0)
    def _():
        tail = jnp.concatenate([ra_ref[:, width:], rb_ref[:, width:]], axis=0)
        start = source_ref[...] * 12
        entry = lax.broadcasted_iota(jnp.int32, (D, D), 1)
        lane = lax.broadcasted_iota(jnp.int32, (128, D), 0)
        bias_ref[...] = jnp.zeros_like(bias_ref)
        for i in range(2):
            offset = entry + i * D - start
            picked = dot_tn(tail, jnp.where((offset >= 0) & (offset < 12), 1.0, 0.0).astype(BF16))
            picked = jnp.where(lane == lane_ref[i : i + 1, :], picked, 0.0)
            bias_ref[:, 2 * i * D : (2 * i + 1) * D] = jnp.sum(picked, axis=0, keepdims=True)

    left = jnp.concatenate([la_ref[...], lb_ref[...]], axis=0)
    out_ref[:, :width] = (dot(xa_ref[...], left) + bias_ref[:, :width]).astype(BF16)
    right = jnp.concatenate([ra_ref[:, :width], rb_ref[:, :width]], axis=0)
    out_ref[:, width:] = (dot(xb_ref[...], right) + bias_ref[:, width:]).astype(BF16)


def project(x_a, x_b, left, right, source):
    seq = x_a.shape[0]
    rows = min(512, seq)
    lanes = (jnp.arange(2 * D, dtype=jnp.int32) % 12).reshape(2, D)
    operands = (*left, *right, source.reshape(D, 1), lanes)

    def fixed(shape):
        return pl.BlockSpec(shape, lambda i: (0, 0), pipeline_mode=pl.Buffered(1))

    return pl.pallas_call(
        project_kernel,
        grid=(seq // rows,),
        in_specs=[pl.BlockSpec((rows, D), lambda i: (i, 0))] * 2
        + [fixed(part.shape) for part in operands],
        out_specs=pl.BlockSpec((rows, 3 * D), lambda i: (i, 0)),
        out_shape=jax.ShapeDtypeStruct((seq, 3 * D), BF16),
        scratch_shapes=[pltpu.VMEM((1, 3 * D), F32)],
        compiler_params=pltpu.CompilerParams(vmem_limit_bytes=ROOM),
        cost_estimate=cost(5),
        name="project",
    )(x_a, x_b, *operands)


def attend_kernel(len_ref, q_ref, k_ref, v_ref, ctx_ref, ctxt_ref, lse_ref):
    seq = q_ref.shape[0]
    qt = (q_ref[...].astype(F32) * 0.125).T.astype(BF16)
    vt = v_ref[...].astype(F32).T.astype(BF16)
    k = k_ref[...]
    keep = lax.broadcasted_iota(jnp.int32, (seq, seq), 0) < len_ref[0]
    zero = jnp.zeros((HEAD_DIM, seq), BF16)
    ones = jnp.ones((16, seq), BF16)
    for h in range(2):
        rows = slice(h * HEAD_DIM, (h + 1) * HEAD_DIM)
        q = jnp.concatenate([qt[rows], zero] if h == 0 else [zero, qt[rows]], axis=0)
        scores = jnp.where(keep, dot(k, q), MASKED)
        peak = jnp.max(scores, axis=0, keepdims=True)
        expo = jnp.exp(scores - peak).astype(BF16)
        both = dot(jnp.concatenate([vt[rows], ones], axis=0), expo)
        total = both[HEAD_DIM : HEAD_DIM + 1]
        ctxt_ref[rows, :] = both[:HEAD_DIM] / total
        lse_ref[0, h : h + 1, :] = peak + jnp.log(total)
    ctx_ref[...] = ctxt_ref[...].T.astype(BF16)


def after(kernel, first, count):
    def call(*refs):
        kernel(*refs[:first], *refs[first + count :])

    return call


def untouched(values):
    return [pl.BlockSpec(memory_space=pl.ANY)] * len(values)


def attend(lengths, packed, first, count, before=(), waits=()):
    seq = packed.shape[0]
    extra = (*before, *waits)
    return pl.pallas_call(
        after(attend_kernel, 4, len(extra)),
        grid_spec=pltpu.PrefetchScalarGridSpec(
            num_scalar_prefetch=1,
            grid=(count,),
            in_specs=[
                pl.BlockSpec((seq, WIDE), lambda p, _, i=i: (0, i * PAIRS + first + p))
                for i in range(3)
            ]
            + untouched(extra),
            out_specs=[
                pl.BlockSpec((seq, WIDE), lambda p, _: (0, first + p)),
                pl.BlockSpec((WIDE, seq), lambda p, _: (first + p, 0)),
                pl.BlockSpec((1, 2, seq), lambda p, _: (first + p, 0, 0)),
            ],
        ),
        out_shape=[
            jax.ShapeDtypeStruct((seq, D), BF16),
            jax.ShapeDtypeStruct((D, seq), F32),
            jax.ShapeDtypeStruct((PAIRS, 2, seq), F32),
        ],
        input_output_aliases={4 + i: i for i in range(len(before))},
        compiler_params=pltpu.CompilerParams(vmem_limit_bytes=ROOM),
        cost_estimate=cost(4 * count),
        name="attend",
    )(lengths, packed, packed, packed, *extra)


def attend_back_kernel(
    block, len_ref, q_ref, k_ref, v_ref, do_ref, ctxt_ref, lse_ref, out_ref, sum_ref, dqt_ref
):
    seq = q_ref.shape[0]
    q = q_ref[...].astype(F32) * 0.125
    qt = q.T.astype(BF16)
    q = q.astype(BF16)
    do = do_ref[...]
    dof = do.astype(F32).T
    dot_ = dof.astype(BF16)
    prod = dof * ctxt_ref[...]
    kt = k_ref[...].astype(F32).T.astype(BF16)
    row = lax.broadcasted_iota(jnp.int32, (HEAD_DIM, seq), 0)

    def pieces(vec):
        high = vec.astype(BF16).astype(F32)
        mid = (vec - high).astype(BF16).astype(F32)
        low = vec - high - mid
        picked = jnp.where(row == 1, mid, jnp.where(row == 2, low, 0.0))
        return jnp.where(row == 0, high, picked).astype(BF16)

    q_aug, do_aug, fill = [], [], []
    for h in range(2):
        rows = slice(h * HEAD_DIM, (h + 1) * HEAD_DIM)
        lse = lse_ref[0, h : h + 1]
        delta = jnp.sum(prod[rows], axis=0, keepdims=True)
        q_parts = [qt[rows], pieces(-lse)]
        do_parts = [dot_[rows], pieces(-delta)]
        q_aug.append(jnp.concatenate(q_parts if h == 0 else q_parts[::-1], axis=0))
        do_aug.append(jnp.concatenate(do_parts if h == 0 else do_parts[::-1], axis=0))
        fill.append(MASKED - lse)
    lane = lax.broadcasted_iota(jnp.int32, (block, WIDE), 1)
    mine = (lane < HEAD_DIM, lane >= HEAD_DIM)
    one = (
        jnp.where(lane < HEAD_DIM + 3, 1.0, 0.0).astype(BF16),
        jnp.where(lane < 3, 1.0, 0.0).astype(BF16),
    )
    for j in range(seq // block):
        rows = slice(j * block, (j + 1) * block)
        keep = lax.broadcasted_iota(jnp.int32, (block, seq), 0) + j * block < len_ref[0]
        k, v = k_ref[rows, :], v_ref[rows, :]
        dv, dk = [], []
        for h in range(2):
            heads = slice(h * HEAD_DIM, (h + 1) * HEAD_DIM)
            k_aug, v_aug = jnp.where(mine[h], k, one[h]), jnp.where(mine[h], v, one[h])
            prob = jnp.exp(jnp.where(keep, dot(k_aug, q_aug[h]), fill[h]))
            dscore = (prob * dot(v_aug, do_aug[h])).astype(BF16)
            dv.append(dot(prob.astype(BF16), do))
            dk.append(dot(dscore, q))
            dq = dot(kt[heads, rows], dscore)
            if j == 0:
                dqt_ref[heads, :] = dq
            else:
                dqt_ref[heads, :] += dq
        out_ref[1, rows, :] = jnp.where(mine[0], dk[0], dk[1]).astype(BF16)
        out_ref[2, rows, :] = jnp.where(mine[0], dv[0], dv[1]).astype(BF16)
    out_ref[0] = (dqt_ref[...] * 0.125).T.astype(BF16)
    sum_ref[0, 0:1] = jnp.sum(out_ref[0].astype(F32), axis=0, keepdims=True)
    sum_ref[0, 1:2] = jnp.sum(out_ref[2].astype(F32), axis=0, keepdims=True)


def attend_back(lengths, packed, dctx, ctxt, lse, first, count, before=None, waits=()):
    seq = packed.shape[0]
    extra = tuple(waits) if before is None else (before, *waits)
    return pl.pallas_call(
        after(partial(attend_back_kernel, min(512, seq)), 7, len(extra)),
        grid_spec=pltpu.PrefetchScalarGridSpec(
            num_scalar_prefetch=1,
            grid=(count,),
            in_specs=[
                pl.BlockSpec((seq, WIDE), lambda p, _, i=i: (0, i * PAIRS + first + p))
                for i in range(3)
            ]
            + [
                pl.BlockSpec((seq, WIDE), lambda p, _: (0, first + p)),
                pl.BlockSpec((WIDE, seq), lambda p, _: (first + p, 0)),
                pl.BlockSpec((1, 2, seq), lambda p, _: (first + p, 0, 0)),
            ]
            + untouched(extra),
            out_specs=[
                pl.BlockSpec((3, seq, WIDE), lambda p, _: (0, 0, first + p)),
                pl.BlockSpec((1, 2, WIDE), lambda p, _: (p, 0, 0)),
            ],
            scratch_shapes=[pltpu.VMEM((WIDE, seq), F32)],
        ),
        out_shape=[
            jax.ShapeDtypeStruct((3, seq, D), BF16),
            jax.ShapeDtypeStruct((count, 2, WIDE), F32),
        ],
        input_output_aliases={} if before is None else {7: 0},
        compiler_params=pltpu.CompilerParams(vmem_limit_bytes=ROOM),
        cost_estimate=cost(6 * count),
        name="attend_back",
    )(lengths, packed, packed, packed, dctx, ctxt, lse, *extra)


def normal_parts(u):
    return 0.5 + 0.5 * lax.erf(u * 0.7071067811865476), jnp.exp(-0.5 * u * u)


def norm_forward(resid):
    center = resid - jnp.mean(resid, axis=-1, keepdims=True)
    inverse = lax.rsqrt(jnp.mean(center * center, axis=-1, keepdims=True) + 1e-05)
    return center * inverse, inverse


def norm_back(grad, gain, unit, inverse):
    du = grad * gain
    mean = jnp.mean(du, axis=-1, keepdims=True)
    return inverse * (du - mean - unit * jnp.mean(du * unit, axis=-1, keepdims=True))


def column_sum(value):
    return jnp.sum(value.astype(F32), axis=0, keepdims=True)


def waited(copies):
    for copy in copies:
        copy.wait()


def feed_kernel(in_pieces, out_pieces, steps, *refs):
    len_ref, place_ref, where_ref, x_ref, ctx_ref, cot_ref, vec_ref, to_a_ref, to_b_ref = refs[:9]
    in_parts, refs = refs[9 : 9 + len(in_pieces)], refs[9 + len(in_pieces) :]
    out_parts, refs = refs[: len(out_pieces)], refs[len(out_pieces) :]
    mixed_ref, dres1_ref, dctx_ref, sum_ref, *grads = refs[:10]
    out_grads, in_grads, attn_grads = grads[:2], grads[2:4], grads[4:6]
    w_ref, w2_ref, act_ref, dhid_ref, first_ref, ctxb_ref, dbr_ref, dres_ref = refs[10:18]
    unit_ref, inverse_ref, slope_ref, held_ref, in_sems, part_sems, out_sems = refs[18:]
    step = pl.program_id(0)
    size = x_ref.shape[0]
    blocks = where_ref.shape[0] // CHUNKS
    first_grad, second_grad = steps, steps + CHUNKS
    back, last = steps + 2 * CHUNKS, 2 * steps + 2 * CHUNKS

    def vec(i):
        return vec_ref[i : i + 1, :]

    def weight(c):
        return w_ref.at[:, c * D : (c + 1) * D]

    def part_copies(whole_ref, parts, pieces, sems):
        made, total = [], 0
        for part, (first, count, column) in zip(parts, pieces):
            rows, width = part.shape[0] // count, part.shape[1]
            columns = pl.ds(pl.multiple_of(place_ref[column] * 128, 128), width)
            for i in range(count):
                where = pl.multiple_of(place_ref[first + i] * rows, rows)
                target = whole_ref.at[pl.ds(where, rows), columns]
                source = part.at[pl.ds(i * rows, rows), :]
                made.append(pltpu.make_async_copy(source, target, sems.at[total]))
                total += 1
        return made

    early = sum(count for _, count, _ in in_pieces[: max(1, len(in_pieces) // 2)])

    def in_weights():
        return part_copies(w_ref, in_parts, in_pieces, in_sems)

    def out_weights():
        return part_copies(w2_ref, out_parts, out_pieces, part_sems)

    @pl.when(step == 0)
    def _():
        for copy in in_weights() + out_weights():
            copy.start()
        sum_ref[...] = jnp.zeros_like(sum_ref)

    @pl.when(step < steps)
    def _():
        rows = pl.ds(pl.multiple_of(step * size, size), size)

        @pl.when(step == 0)
        def _():
            waited(in_weights()[:early])

        resid = x_ref[...].astype(F32) + (dot(ctx_ref[...], weight(0)[...]) + vec(2))
        unit1, inverse1 = norm_forward(resid)
        unit_ref[rows, :] = unit1
        inverse_ref[rows, :] = jnp.broadcast_to(inverse1, (size, 128))
        first = unit1 * vec(3) + vec(4)
        first_b = first.astype(BF16)
        first_ref[rows, :] = arrange(first_b, to_a_ref[...])
        ctxb_ref[rows, :] = arrange(ctx_ref[...], to_b_ref[...])

        @pl.when(step == 0)
        def _():
            waited(in_weights()[early:] + out_weights())

        branch = None
        for c in range(CHUNKS):
            cols = slice(c * D, (c + 1) * D)
            hidden = dot(first_b, weight(1 + c)[...]) + vec(5 + c)
            phi, bell = normal_parts(hidden)
            active = (hidden * phi).astype(BF16)
            act_ref[rows, cols] = active
            slope_ref[:, cols] = phi + hidden * bell * 0.3989422804014327
            part = dot(active, w2_ref[cols, :])
            branch = part if branch is None else branch + part
        unit2, inverse2 = norm_forward(first + (branch + vec(9)))
        place = lax.broadcasted_iota(jnp.int32, (size, 1), 0) + step * size
        keep = (place < len_ref[0]).astype(F32)
        mixed_ref[...] = ((unit2 * vec(10) + vec(11)) * keep).astype(BF16)
        dz = cot_ref[...].astype(F32) * keep
        dres2 = norm_back(dz, vec(10), unit2, inverse2)
        dres_ref[rows, :] = dres2
        dbranch = dres2.astype(BF16)
        dbr_ref[rows, :] = dbranch
        sum_ref[9:10, :] += column_sum(dbranch)
        sum_ref[10:11, :] += column_sum(dz * unit2)
        sum_ref[11:12, :] += column_sum(dz)
        for c in range(CHUNKS):
            cols = slice(c * D, (c + 1) * D)
            dhidden = (dot_nt(dbranch, w2_ref[cols, :]) * slope_ref[:, cols]).astype(BF16)
            dhid_ref[rows, cols] = dhidden
            sum_ref[5 + c : 6 + c, :] += column_sum(dhidden)

    def out_copies(step, go):
        chunk = step - first_grad
        slot = lax.rem(chunk, 2)
        rows = D // blocks
        for i in range(blocks):
            place = where_ref[chunk * blocks + i]
            source = held_ref.at[slot, pl.ds(i * rows, rows), :]
            for half in range(2):
                where = pl.multiple_of((place - half * 2 * blocks) * rows, rows)

                @pl.when((place >= 2 * blocks) == (half == 1))
                def _(half=half, where=where, source=source, i=i):
                    target = out_grads[half].at[pl.ds(where, rows), :]
                    go(pltpu.make_async_copy(source, target, out_sems.at[slot, i]))

    def in_copies(step, grads, column):
        slot = lax.rem(step - first_grad, 2)
        made = []
        for half in range(2):
            source = held_ref.at[slot, pl.ds(half * D // 2, D // 2), :]
            target = grads[half].at[:, pl.ds(column, D)]
            made.append(pltpu.make_async_copy(source, target, out_sems.at[slot, half]))
        return made

    def in_column(step):
        return pl.multiple_of((step - second_grad) * D, D)

    def start(copy):
        copy.start()

    def wait(copy):
        copy.wait()

    @pl.when((step >= first_grad) & (step < second_grad))
    def _():
        @pl.when(step >= first_grad + 2)
        def _():
            out_copies(step - 2, wait)

        cols = pl.ds(pl.multiple_of((step - first_grad) * D, D), D)
        grad = dot_tn(act_ref[:, cols], dbr_ref[...]).astype(BF16)
        held_ref[lax.rem(step - first_grad, 2)] = grad
        out_copies(step, start)

    @pl.when((step >= second_grad) & (step < back))
    def _():
        @pl.when(step < second_grad + 2)
        def _():
            out_copies(step - 2, wait)

        @pl.when(step >= second_grad + 2)
        def _():
            waited(in_copies(step - 2, in_grads, in_column(step - 2)))

        cols = pl.ds(in_column(step), D)
        grad = dot_tn(first_ref[...], dhid_ref[:, cols]).astype(BF16)
        held_ref[lax.rem(step - first_grad, 2)] = grad
        for copy in in_copies(step, in_grads, in_column(step)):
            copy.start()

    @pl.when((step >= back) & (step < last))
    def _():
        rows = pl.ds(pl.multiple_of((step - back) * size, size), size)
        dfirst = dres_ref[rows, :]
        for c in range(CHUNKS):
            dfirst = dfirst + dot_nt(dhid_ref[rows, c * D : (c + 1) * D], weight(1 + c)[...])
        unit = unit_ref[rows, :]
        dres1 = norm_back(dfirst, vec(3), unit, inverse_ref[rows, 0:1])
        dres1_ref[...] = dres1
        dattend = dres1.astype(BF16)
        dbr_ref[rows, :] = dattend
        dctx_ref[...] = dot_nt(dattend, weight(0)[...]).astype(BF16)
        sum_ref[2:3, :] += column_sum(dattend)
        sum_ref[3:4, :] += column_sum(dfirst * unit)
        sum_ref[4:5, :] += column_sum(dfirst)

    @pl.when(step == last)
    def _():
        waited(in_copies(back - 2, in_grads, in_column(back - 2)))
        waited(in_copies(back - 1, in_grads, in_column(back - 1)))
        held_ref[0] = dot_tn(ctxb_ref[...], dbr_ref[...]).astype(BF16)
        copies = in_copies(first_grad, attn_grads, 0)
        for copy in copies:
            copy.start()
        waited(copies)


def feed(lengths, x, ctx, cot, vec, to_a, to_b, places, where, in_side, out_side):
    (in_parts, in_pieces), (out_parts, out_pieces) = in_side, out_side
    seq = x.shape[0]
    size = min(256, seq)
    steps = seq // size
    back = steps + 2 * CHUNKS
    anywhere = pl.BlockSpec(memory_space=pl.ANY)

    def early(width):
        return pl.BlockSpec((size, width), lambda i, *_: (jnp.minimum(i, steps - 1), 0))

    def late(width):
        return pl.BlockSpec((size, width), lambda i, *_: (jnp.clip(i - back, 0, steps - 1), 0))

    def fixed(shape):
        return pl.BlockSpec(shape, lambda i, *_: (0, 0), pipeline_mode=pl.Buffered(1))

    shape = jax.ShapeDtypeStruct
    return pl.pallas_call(
        partial(feed_kernel, in_pieces, out_pieces, steps),
        grid_spec=pltpu.PrefetchScalarGridSpec(
            num_scalar_prefetch=3,
            grid=(2 * steps + 2 * CHUNKS + 1,),
            in_specs=[early(D)] * 3
            + [fixed((12, D)), fixed((D, D)), fixed((D, D))]
            + untouched(in_parts)
            + untouched(out_parts),
            out_specs=[early(D), late(D), late(D), pl.BlockSpec((12, D), lambda i, *_: (0, 0))]
            + [anywhere] * 6,
            scratch_shapes=[
                pltpu.VMEM((D, D + FF), BF16),
                pltpu.VMEM((FF, D), BF16),
                pltpu.VMEM((seq, FF), BF16),
                pltpu.VMEM((seq, FF), BF16),
                pltpu.VMEM((seq, D), BF16),
                pltpu.VMEM((seq, D), BF16),
                pltpu.VMEM((seq, D), BF16),
                pltpu.VMEM((seq, D), F32),
                pltpu.VMEM((seq, D), F32),
                pltpu.VMEM((seq, 128), F32),
                pltpu.VMEM((size, FF), F32),
                pltpu.VMEM((2, D, D), BF16),
                pltpu.SemaphoreType.DMA((sum(count for _, count, _ in in_pieces),)),
                pltpu.SemaphoreType.DMA((sum(count for _, count, _ in out_pieces),)),
                pltpu.SemaphoreType.DMA((2, max(2, where.shape[0] // CHUNKS))),
            ],
        ),
        out_shape=[
            shape((seq, D), BF16),
            shape((seq, D), F32),
            shape((seq, D), BF16),
            shape((12, D), F32),
        ]
        + [shape((FF // 2, D), BF16)] * 2
        + [shape((D // 2, FF), BF16)] * 2
        + [shape((D // 2, D), BF16)] * 2,
        compiler_params=pltpu.CompilerParams(vmem_limit_bytes=VMEM),
        cost_estimate=cost(50),
        name="feed",
    )(lengths, places, where, x, ctx, cot, vec, to_a, to_b, *in_parts, *out_parts)


def swap(value, bits, n):
    mask = sum(1 << bit for bit in bits)
    return lax.ppermute(value, "dp", [(i, i ^ mask) for i in range(n)])


def subsets(bits):
    return [[bit for k, bit in enumerate(bits) if p >> k & 1] for p in range(1, 2 ** len(bits))]


def sum_all(value, groups, n):
    for bits in groups:
        value = sum([swap(value, some, n) for some in subsets(bits)], value)
    return value


def own_bit(bit):
    return (lax.axis_index("dp") >> bit) & 1


def phase(*values):
    return lax.optimization_barrier(values)


class Order:
    def __init__(self, bits):
        self.bits, self.n = bits, 2 ** len(bits)

    def mask(self, place):
        return sum(((place >> k) & 1) << bit for k, bit in enumerate(self.bits))

    def source(self):
        rows = D // self.n
        place = jnp.arange(D, dtype=jnp.int32)
        block = self.mask(place // rows) ^ lax.axis_index("dp")
        return block * rows + place % rows

    def matrix(self):
        place = jnp.arange(D, dtype=jnp.int32)
        return (place[:, None] == self.source()[None, :]).astype(BF16)

    def where(self):
        other = jnp.arange(self.n, dtype=jnp.int32) ^ lax.axis_index("dp")
        return sum(((other >> bit) & 1) << k for k, bit in enumerate(self.bits))

    def places(self, count):
        return self.mask(jnp.arange(count, dtype=jnp.int32)) ^ lax.axis_index("dp")


class Gather:
    def __init__(self, shard, n):
        self.value, self.n = shard, n

    def step(self, bits):
        got = [swap(self.value, some, self.n) for some in subsets(bits)]
        self.value = jnp.concatenate([self.value, *got], axis=0)

    def cut(self, start, stop):
        return Gather(self.value[:, start:stop], self.n)


class Scatter:
    def __init__(self, kept, got, n):
        self.terms, self.n = [kept, got], n

    def away(self, bits):
        size = self.terms[0].shape[0] >> len(bits)
        parts = range(1, 2 ** len(bits))
        return [self.total([t[p * size : (p + 1) * size] for t in self.terms], BF16) for p in parts]

    def send(self, away, bits):
        got = [swap(part, some, self.n) for part, some in zip(away, subsets(bits))]
        self.terms = [t[: away[0].shape[0]] for t in self.terms] + got
        self.recent = len(got)

    def step(self, bits):
        self.send(self.away(bits), bits)

    @property
    def got(self):
        return self.terms[-self.recent :]

    @got.setter
    def got(self, values):
        self.terms[-self.recent :] = values

    def total(self, parts=None, kind=F32):
        parts = self.terms if parts is None else parts
        result = parts[0].astype(F32)
        for part in parts[1:]:
            result = result + part.astype(F32)
        return result.astype(kind)

    def join(self, other):
        self.terms = [jnp.concatenate([self.total(), other.total()], axis=1)]
        return self


def adapt(weight, grad, moment, square, decay):
    new_moment = 0.9 * moment + 0.1 * grad
    new_square = 0.999 * square + 0.001 * grad * grad
    update = new_moment / (1.0 - 0.9**STEP) / (jnp.sqrt(new_square / (1.0 - 0.999**STEP)) + 1e-06)
    return (new_moment, new_square, update + decay * weight)


def lane_sums(value):
    columns = jnp.sum(value * value, axis=0, keepdims=True)
    result = columns[:, :128]
    for start in range(128, value.shape[1], 128):
        result = result + columns[:, start : start + 128]
    return result


def adapt_kernel(first, columns, *refs):
    before_ref, sums_ref = refs[8], refs[15]
    sums = before_ref[:8, :]
    row = lax.broadcasted_iota(jnp.int32, sums.shape, 0)
    for i in range(2):
        weight_ref, grad_ref, moment_ref, square_ref = refs[i * 4 : i * 4 + 4]
        outs = refs[9 + i * 3 : 12 + i * 3]
        weight = weight_ref[...]
        grad = grad_ref[:, columns[i] : columns[i] + weight.shape[1]]
        values = adapt(weight, grad, moment_ref[...], square_ref[...], 0.01)
        for out, value in zip(outs, values):
            out[...] = value
        sums = jnp.where(row == first + i, lane_sums(weight), sums)
        sums = jnp.where(row == 4 + first + i, lane_sums(values[2]), sums)
    sums_ref[:8, :] = sums
    if sums_ref.shape[0] > 8:
        sums_ref[8:, :] = before_ref[8:, :]


def adapt_two(first, columns, before, *operands):
    shapes = [jax.ShapeDtypeStruct(operands[i * 4].shape, F32) for i in (0, 0, 0, 1, 1, 1)]
    return pl.pallas_call(
        partial(adapt_kernel, first, columns),
        out_shape=shapes + [jax.ShapeDtypeStruct(before.shape, F32)],
        compiler_params=pltpu.CompilerParams(vmem_limit_bytes=ROOM),
        cost_estimate=cost(2),
        name="adapt",
    )(*operands, before)


def renew_kernel(sums_ref, *refs):
    norms = jnp.sqrt(jnp.sum(sums_ref[:8, :], axis=1, keepdims=True))
    refs[12][...] = jnp.broadcast_to(norms, (8, 128)).T[:1, :]
    for i in range(4):
        rate = 0.25 * (norms[i : i + 1] / norms[4 + i : 5 + i])
        refs[8 + i][...] = refs[i][...] - rate * refs[4 + i][...]


def renew(sums, weights, updates):
    return pl.pallas_call(
        renew_kernel,
        out_shape=[jax.ShapeDtypeStruct(weight.shape, F32) for weight in weights]
        + [jax.ShapeDtypeStruct((1, 8), F32)],
        compiler_params=pltpu.CompilerParams(vmem_limit_bytes=ROOM),
        cost_estimate=cost(2),
        name="renew",
    )(sums, *weights, *updates)


def body(
    n,
    frames,
    cotangent,
    lengths,
    w_qkv,
    w_attn,
    w_in,
    w_out,
    vectors,
    moment_qkv,
    moment_attn,
    moment_in,
    moment_out,
    moment_vec,
    square_qkv,
    square_attn,
    square_in,
    square_out,
    square_vec,
):
    rows_d, rows_f, width = w_qkv.shape[0], w_out.shape[0], vectors.shape[0]
    core, one, two, *others = range(n.bit_length() - 1)
    far = others[::-1]
    groups = [far[i : i + 2] for i in range(0, len(far), 2)]
    order_a, order_b = Order(far + [two, one, core]), Order(far + [one, two, core])
    x = frames[0]

    aligned = rows_d % 8 == 0
    half = w_qkv.shape[1] // 2
    tail = jnp.pad(vectors.reshape(rows_d, 12), ((0, 0), (0, 116)))
    low_qkv = jnp.concatenate([w_qkv, tail], axis=1).astype(BF16)
    low_qkv, *masters = phase(low_qkv, w_attn, w_in, w_out)
    low_in = jnp.concatenate(masters[:2], axis=1).astype(BF16)
    qkv, out = Gather(low_qkv, n), Gather(masters[2].astype(BF16), n)
    to_a, to_b = phase(order_a.matrix(), order_b.matrix())
    x_a, x_b = arrange(x, to_a), arrange(x, to_b)
    inner = Gather(low_in, n)
    if aligned:
        side = low_in.shape[1] // 2
        mine = own_bit(core)
        kept = lax.dynamic_slice_in_dim(low_in, mine * side, side, 1)
        got = swap(lax.dynamic_slice_in_dim(low_in, (1 - mine) * side, side, 1), [core], n)
        pair = [jnp.where(mine == 0, kept, got), jnp.where(mine == 0, got, kept)]
        inner.value = jnp.concatenate(pair, axis=0)
    else:
        attn_in = lax.all_gather(low_in, "dp", axis=0, tiled=True)
    for bits in groups:
        qkv.step(bits)
        qkv.value, inner.value = phase(qkv.value, inner.value)
    left, right = qkv.cut(0, half), qkv.cut(half, 2 * half + 128)
    out_left, out_right = out.cut(0, D // 2), out.cut(D // 2, D)
    if aligned:
        left.value = jnp.concatenate([left.value, out_left.value], axis=1)
        right.value = jnp.concatenate([right.value, out_right.value], axis=1)
    else:
        out_left.step([two])
        out_right.step([one])
    left.step([two])
    right.step([one])
    for bit in far[:1] if aligned else ():
        inner.step([bit])
    left.value, right.value, inner.value, x_a, x_b = phase(
        left.value, right.value, inner.value, x_a, x_b
    )
    if aligned:
        out_left, left = left.cut(half, half + D // 2), left.cut(0, half)
        out_right, right = right.cut(half + 128, half + 128 + D // 2), right.cut(0, half + 128)
    out = Gather(jnp.concatenate([out_left.value, out_right.value], axis=1), n)
    left.step([one])
    right.step([two])
    for bit in far[1:] if aligned else ():
        inner.step([bit])
    left.value, right.value, inner.value, out.value = phase(
        left.value, right.value, inner.value, out.value
    )
    left = (left.value, swap(left.value, [core], n))
    right = (right.value, swap(right.value, [core], n))
    cut = 1024 if aligned else low_in.shape[1]
    in_left, in_right = inner.cut(0, cut), inner.cut(cut, inner.value.shape[1])

    def in_step(bits_left, bits_right):
        if aligned:
            in_left.step(bits_left)
            in_right.step(bits_right)

    left, right, in_left.value, in_right.value, out.value = phase(
        left, right, in_left.value, in_right.value, out.value
    )
    in_step([two], [one])
    out.step(far[:1])
    vec_rows = jnp.concatenate([part[:, half:] for part in right], axis=0)
    vec = dot(to_b, vec_rows)[:, :12].reshape(12, D)

    packed = project(x_a, x_b, left, right, order_b.source())
    some = PAIRS // 6
    heads = attend(lengths, packed, 0, some)
    heads, in_left.value, in_right.value, out.value = phase(
        heads, in_left.value, in_right.value, out.value
    )
    in_step([one], [two])
    for bit in far[1:]:
        out.step([bit])
    heads = attend(lengths, packed, some, 3 * some, heads)
    heads, out.value, in_left.value, in_right.value = phase(
        heads, out.value, in_left.value, in_right.value
    )
    out_left, out_right = out.cut(0, D // 2), out.cut(D // 2, D)
    out_sides = [out_left.value, out_right.value]
    out_got = [swap(out_sides[0], [one], n), swap(out_sides[1], [two], n)]
    in_parts = [in_left.value, in_right.value]
    if aligned:
        in_parts = [in_parts[0], swap(in_parts[0], [core], n)] + [
            in_parts[1],
            swap(in_parts[1], [core], n),
        ]
    heads = attend(lengths, packed, 4 * some, 2 * some, heads)
    heads, vec, out_got, in_parts = phase(heads, vec, out_got, in_parts)
    out_across = [swap(value, [core], n) for value in out_sides]
    out_ends = [swap(value, [core], n) for value in out_got]
    out_sides = list(zip(out_sides, out_got, out_across, out_ends))
    out_a, out_b = Order([two, *far, one, core]), Order([one, *far, two, core])
    if aligned:
        chips_a, chips_b = [order.places(n // 2) // 2 for order in (order_a, order_b)]
        blocks_a, blocks_b = out_a.places(n), out_b.places(n)
        first = jnp.stack([mine, 1 - mine]) * (side // 128)
        corners = jnp.concatenate([first, first + cut // 128])
        columns = jnp.array([0, D // 256], jnp.int32)
        places = jnp.concatenate([chips_a, chips_b, blocks_a, blocks_b, corners, columns])
        base = 3 * n
        in_pieces = tuple((i // 2 * (n // 2), n // 2, base + i) for i in range(4))
        out_parts = [part for parts in out_sides for part in parts]
        quarter = n // 4
        out_pieces = tuple(
            (n + i * n + j * quarter, quarter, base + 4 + i) for i in range(2) for j in range(4)
        )
    else:
        sides = []
        for parts, order in zip(out_sides, (out_a, out_b)):
            value = jnp.concatenate(parts, axis=0).reshape(n, rows_f, D // 2)
            sides.append(value[jnp.argsort(order.places(n))].reshape(FF, D // 2))
        in_parts, out_parts = [attn_in], [jnp.concatenate(sides, axis=1)]
        places = jnp.zeros((2,), jnp.int32)
        in_pieces = out_pieces = ((0, 1, 1),)
    ctx, ctxt, lse = heads

    where = order_b.where() if aligned else jnp.arange(CHUNKS, dtype=jnp.int32)
    mixed, dres1, dctx, sums, *grads = feed(
        *(lengths, x, ctx, cotangent[0], vec, to_a, to_b, places, where),
        *((in_parts, in_pieces), (out_parts, out_pieces)),
    )
    if not aligned:
        grad = jnp.concatenate(grads[:2], axis=0).reshape(n, rows_f, D)
        grads[:2] = jnp.split(grad[order_b.places(n)].reshape(FF, D), 2)
    sum_out = Scatter(grads[0], swap(grads[1], [core], n), n)
    sum_in = Scatter(grads[2], swap(grads[3], [core], n), n)

    sum_in.recent = sum_out.recent = 1
    dqkv, biases = None, []
    for first, count, bits in ((0, 1, (one, two)), (1, 4, (two, one)), (5, 1, None)):
        dqkv, bias = attend_back(lengths, packed, dctx, ctxt, lse, first, count, dqkv)
        biases.append(bias)
        if bits is not None:
            sum_in.got, sum_out.got, dqkv = phase(sum_in.got, sum_out.got, dqkv)
            sum_in.step([bits[0]])
            sum_out.step([bits[1]])
    full_qkv = jnp.concatenate(
        [
            arrange(to_a, jnp.concatenate(left, axis=0)),
            arrange(to_b, jnp.concatenate([part[:, :half] for part in right], axis=0)),
        ],
        axis=1,
    )
    dqkv, full_qkv, sum_in.got, sum_out.got = phase(
        dqkv, full_qkv, sum_in.got, sum_out.got
    )

    def late_grads(side):
        cols = slice(side * D // 2, (side + 1) * D // 2)
        queries, keys = [dot_tn(x_a[:, cols], dqkv[i]).astype(BF16) for i in range(2)]
        values = dot_tn(x_b[:, cols], dqkv[2]).astype(BF16)
        return (
            jnp.concatenate([queries, keys], axis=1),
            jnp.concatenate([values, grads[4 + side]], axis=1),
        )

    away_a, away_b = late_grads(1)
    away_a, away_b, dqkv, away_in, away_out = phase(
        away_a, away_b, dqkv, sum_in.away(others[:1]), sum_out.away(others[:1])
    )
    got_a, got_b = swap(away_a, [core], n), swap(away_b, [core], n)
    sum_in.send(away_in, others[:1])
    sum_out.send(away_out, others[:1])
    kept_a, kept_b = late_grads(0)
    got_a, got_b, kept_a, kept_b = phase(got_a, got_b, kept_a, kept_b)
    late_a, late_b = Scatter(kept_a, got_a, n), Scatter(kept_b, got_b, n)
    late_a.step([one])
    late_b.step([two])
    late_a.got, late_b.got, sum_in.got, sum_out.got = phase(
        late_a.got, late_b.got, sum_in.got, sum_out.got
    )
    away_a, away_b, *aways = phase(
        late_a.away([two]),
        late_b.away([one]),
        *((sum_in.away(others[1:2]), sum_out.away(others[1:2])) if others[1:] else ()),
    )
    late_a.send(away_a, [two])
    late_b.send(away_b, [one])
    for bit in others[1:2]:
        sum_in.send(aways[0], [bit])
        sum_out.send(aways[1], [bit])
    for bit in others[2:]:
        sum_in.step([bit])
        sum_out.step([bit])
    late_a.got, late_b.got = phase(late_a.got, late_b.got)
    late = late_a.join(late_b)
    late.step(others[:1])
    share_in, share_out = sum_in.total(), sum_out.total()
    late.got, share_in, share_out = phase(late.got, share_in, share_out)
    for bit in others[1:]:
        late.step([bit])
    share_late = late.total()
    bias_sums = jnp.concatenate(biases, axis=0)
    grad_vec = jnp.concatenate(
        [bias_sums[:, 0].reshape(1, D), bias_sums[:, 1].reshape(1, D), sums[2:]]
    ).reshape(-1, 128)
    input_grad = dres1
    for i in range(3):
        input_grad = input_grad + dot_nt(dqkv[i], full_qkv[:, i * D : (i + 1) * D])

    next_in = adapt_two(
        2,
        (0, 0),
        jnp.concatenate([jnp.zeros((8, 128), F32), grad_vec], axis=0),
        *(w_in, share_in, moment_in, square_in),
        *(w_out, share_out, moment_out, square_out),
    )
    next_attn = adapt_two(
        0,
        (0, 3 * D),
        next_in[6],
        *(w_qkv, share_late, moment_qkv, square_qkv),
        *(w_attn, share_late, moment_attn, square_attn),
    )
    reduced = sum_all(next_attn[6], [[bit] for bit in range(n.bit_length() - 1)], n)
    place = lax.axis_index("dp") * width
    share_vec = lax.dynamic_slice_in_dim(reduced[8:].reshape(-1), place, width, 0)
    updates = (next_attn[2], next_attn[5], next_in[2], next_in[5])
    *new_weights, norms = renew(reduced, (w_qkv, w_attn, w_in, w_out), updates)
    vec_moment, vec_square, vec_update = adapt(vectors, share_vec, moment_vec, square_vec, 0.0)
    return (
        mixed[None],
        input_grad[None],
        *new_weights,
        vectors - 0.4 * vec_update,
        *(next_attn[0], next_attn[3], next_in[0], next_in[3], vec_moment),
        *(next_attn[1], next_attn[4], next_in[1], next_in[4], vec_square),
        norms.reshape(8),
    )


def solution(mesh):
    clips, matrix, vector = P("dp", None, None), P("dp", None), P("dp")
    parameters = (matrix,) * 4 + (vector,)
    return jax.shard_map(
        partial(body, mesh.shape["dp"]),
        mesh=mesh,
        in_specs=(clips, clips, vector) + parameters * 3,
        out_specs=(clips, clips) + parameters * 3 + (P(),),
        check_vma=False,
    )
```
